256 devices in a mesh: lat: 8 (over x, y_lo), lon: 16 (over y_hi, z), rep: 2 (over core).
Axes of the slice: x: 4, y: 4 (y_hi: 2, y_lo: 2; y = y_hi * 2 + y_lo), z: 8, core: 2. Of those that a mesh axis runs over, the one named last changes fastest.
Arguments:
- tokens: bfloat16 [4, 48, 192, 512], P('rep', 'lat', 'lon'), parts along dimension 0, may hold values from -6 to 6
- cotangent: bfloat16 [4, 48, 192, 512], P('rep', 'lat', 'lon'), parts along dimension 0, may hold values from -6 to 6
- region: int32 [4, 48, 192], P('rep', 'lat', 'lon'), parts along dimension 0, may hold values from 1 to 3
- unshifted_norm_gain: float32 [512], replicated, may hold values from 0.5 to 2.7
- unshifted_query_key_value: bfloat16 [512, 1536], replicated, may hold values from -0.9 to 0.9
- out_first: bfloat16 [512, 512], replicated, may hold values from -0.25 to 0.25
- shifted_norm_gain: float32 [512], replicated, may hold values from 0.5 to 2.7
- shifted_query_key_value: bfloat16 [512, 1536], replicated, may hold values from -0.9 to 0.9
- out_second: bfloat16 [512, 512], replicated, may hold values from -0.25 to 0.25
Outputs:
- result: bfloat16 [4, 48, 192, 512], P('rep', 'lat', 'lon'), parts along dimension 0
- token_gradient: bfloat16 [4, 48, 192, 512], P('rep', 'lat', 'lon'), parts along dimension 0
- clip_qkv_first: float32 [1024, 1536], P(('rep', 'lat', 'lon')), parts along dimension 0
- clip_out_first: float32 [1024, 512], P(('rep', 'lat', 'lon')), parts along dimension 0
- clip_qkv_second: float32 [1024, 1536], P(('rep', 'lat', 'lon')), parts along dimension 0
- clip_out_second: float32 [1024, 512], P(('rep', 'lat', 'lon')), parts along dimension 0
The draws below stay inside these ranges and needn't reach their ends.
There are 2 independent parts, one for each index of `rep`. The reference program is written for one: setup_inputs(seed, part) draws one part's arguments, and reference() takes and returns one part's arrays. A program takes and returns all parts, laid end to end along the dimension named above; an argument that names none is the same for every part. Nothing has to cross between parts.
All inputs are finite; a program needn't handle non-finite values.
Results may differ from the reference program's by a relative error of at most 0.038.
Values may be sent and summed in bfloat16 or wider, within the bound.
No kernel may reach another device: no remote copies, remote signals or barrier semaphores. Data moves between devices by JAX's collectives and lax.ppermute only.
A program may use at most 128 MiB of HBM per device.

```python
import math
import jax
import jax.numpy as jnp
from jax import lax

D = 512
HEADS = 8
HEAD = 64
WLEV = 2
WLAT = 6
WLON = 12
LEV = 2
NLAT = 48
NLON = 192


def gain_curve(key, spread):
    ramp = jnp.arange(D, dtype=jnp.float32) / D
    rough = jax.random.uniform(key, (D,), jnp.float32, 1.0 - spread, 1.0 + spread)
    return jnp.exp(0.55 * ramp) * rough


def projection(key, boost):
    split_keys = jax.random.split(key, 3)
    query_part = jnp.clip(jax.random.normal(split_keys[0], (D, D), jnp.float32), -4.5, 4.5)
    fresh_part = jnp.clip(jax.random.normal(split_keys[1], (D, D), jnp.float32), -4.5, 4.5)
    value_part = jnp.clip(jax.random.normal(split_keys[2], (D, D), jnp.float32), -4.5, 4.5)
    key_part = fresh_part
    base = boost / math.sqrt(D)
    whole_matrix = jnp.concatenate([base * query_part, base * key_part, value_part / math.sqrt(D)], axis=1)
    return jnp.clip(whole_matrix, -0.9, 0.9).astype(jnp.bfloat16)


def draw_unshifted_norm_gain(key, part):
    key = jax.random.fold_in(key, 11)
    return gain_curve(key, 0.3)


def draw_shifted_norm_gain(key, part):
    key = jax.random.fold_in(key, 12)
    return gain_curve(key, 0.3)


def draw_unshifted_query_key_value(key, part):
    key = jax.random.fold_in(key, 13)
    return projection(key, 1.0)


def draw_shifted_query_key_value(key, part):
    key = jax.random.fold_in(key, 14)
    return projection(key, 1.0)


def plant(entries, key, least, largest):
    longest = entries.shape.index(max(entries.shape))
    spots = []
    for shift in (0, 1):
        where = [jax.random.randint(jax.random.fold_in(key, axis), (), 0, length) for axis, length in enumerate(entries.shape)]
        where[longest] = (where[longest] + shift) % entries.shape[longest]
        spots.append(tuple(where))
    return entries.at[spots[0]].set(least).at[spots[1]].set(largest)


def level_of(key, shape, cuts, low, top_value):
    def one(position, parts):
        draws = jax.random.uniform(jax.random.fold_in(jax.random.fold_in(key, 6), position), (parts,), jnp.float32, low / len(cuts), top_value / len(cuts))
        return jnp.repeat(jnp.exp(draws), shape[position] // parts).reshape((-1,) + (1,) * (len(shape) - position - 1))

    loudness = one(*cuts[0])
    for cut in cuts[1:]:
        loudness = loudness * one(*cut)
    return loudness


def scatter_about(stream_key, extent, scale, limit, cuts=(), kind=jnp.bfloat16):
    entries = scale * jax.random.normal(stream_key, extent, jnp.float32)
    if cuts:
        entries = entries * level_of(stream_key, extent, cuts, -0.22, 0.18)
    return jnp.clip(entries, -limit, limit).astype(kind)


def setup_inputs(seed: int = 0, part: int = 0) -> dict:
    streams_of = jax.random.split(jax.random.key(seed), 10)
    part_keys = jax.random.split(jax.random.fold_in(streams_of[9], part), 10)
    tokens = scatter_about(part_keys[0], (LEV, NLAT, NLON, D), 1.0, 6.0, ((1, 8), (2, 16)))
    cotangent = scatter_about(part_keys[1], (LEV, NLAT, NLON, D), 1.0, 6.0, ((1, 8), (2, 16)))
    region = plant(jax.random.randint(part_keys[2], (LEV, NLAT, NLON), 1, 4), jax.random.fold_in(part_keys[2], 1), 1, 3).astype(jnp.int32)
    unshifted_norm_gain = draw_unshifted_norm_gain(jax.random.fold_in(streams_of[9], 71), part)
    unshifted_query_key_value = draw_unshifted_query_key_value(jax.random.fold_in(streams_of[9], 71), part)
    out_first = scatter_about(streams_of[5], (D, D), D ** -0.5, 0.25)
    shifted_norm_gain = draw_shifted_norm_gain(jax.random.fold_in(streams_of[9], 71), part)
    shifted_query_key_value = draw_shifted_query_key_value(jax.random.fold_in(streams_of[9], 71), part)
    out_second = scatter_about(streams_of[8], (D, D), D ** -0.5, 0.25)
    return dict(tokens=tokens, cotangent=cotangent, region=region, unshifted_norm_gain=unshifted_norm_gain, unshifted_query_key_value=unshifted_query_key_value, out_first=out_first, shifted_norm_gain=shifted_norm_gain, shifted_query_key_value=shifted_query_key_value, out_second=out_second)


EPSILON = 1e-05
NEGATIVE = -1e+30

def to_windows(token_field):
    levels, lat_rows, lon_cols = (token_field.shape[0], token_field.shape[1], token_field.shape[2])
    trailing = token_field.shape[3:]
    shaped = token_field.reshape((levels // WLEV, WLEV, lat_rows // WLAT, WLAT, lon_cols // WLON, WLON) + trailing)
    axes_order = (2, 0, 4, 1, 3, 5) + tuple(range(6, 6 + len(trailing)))
    shaped = shaped.transpose(axes_order)
    return shaped.reshape((lat_rows // WLAT, levels // WLEV * (lon_cols // WLON), WLEV * WLAT * WLON) + trailing)

def from_windows(blocks, levels, lat_rows, lon_cols):
    trailing = blocks.shape[3:]
    shaped = blocks.reshape((lat_rows // WLAT, levels // WLEV, lon_cols // WLON, WLEV, WLAT, WLON) + trailing)
    axes_order = (1, 3, 0, 4, 2, 5) + tuple(range(6, 6 + len(trailing)))
    return shaped.transpose(axes_order).reshape((levels, lat_rows, lon_cols) + trailing)

def apply_norm(token_field, gain_vector):
    values = token_field.astype(jnp.float32)
    average = lax.optimization_barrier(jnp.mean(values, -1, keepdims=True))
    mean_removed = values - average
    inverse_deviation = lax.rsqrt(lax.optimization_barrier(jnp.mean(mean_removed * mean_removed, -1, keepdims=True)) + EPSILON)
    standardized = mean_removed * inverse_deviation
    return ((standardized * gain_vector).astype(jnp.bfloat16), standardized, inverse_deviation)

def split_heads(window_block, which_part):
    section = window_block[..., which_part * D:(which_part + 1) * D]
    return section.reshape(section.shape[:-1] + (HEADS, HEAD)).astype(jnp.float32)

def probabilities(window_block, labels):
    query_heads = split_heads(window_block, 0)
    key_heads = split_heads(window_block, 1)
    scores = jnp.einsum('wqhd,wkhd->whqk', query_heads, key_heads) * HEAD ** (-0.5)
    allowed = (labels[:, :, None] == labels[:, None, :]) & (labels[:, None, :] > 0)
    scores = jnp.where(allowed[:, None], scores, NEGATIVE)
    row_max = lax.optimization_barrier(jnp.max(scores, -1, keepdims=True))
    exponent = jnp.exp(scores - row_max)
    return exponent / lax.optimization_barrier(jnp.sum(exponent, -1, keepdims=True))

def attend(window_block, labels):
    weights = probabilities(window_block, labels)
    rounded = lax.optimization_barrier(weights.astype(jnp.bfloat16)).astype(jnp.float32)
    value_heads = split_heads(window_block, 2)
    mixed_out = jnp.einsum('whqk,wkhd->wqhd', rounded, value_heads)
    return mixed_out.reshape(mixed_out.shape[0], mixed_out.shape[1], D).astype(jnp.bfloat16)

def attend_back(window_block, labels, grad_block):
    weights = probabilities(window_block, labels)
    rounded = lax.optimization_barrier(weights.astype(jnp.bfloat16)).astype(jnp.float32)
    query_heads = split_heads(window_block, 0)
    key_heads = split_heads(window_block, 1)
    value_heads = split_heads(window_block, 2)
    grad_heads = grad_block.reshape(grad_block.shape[:-1] + (HEADS, HEAD)).astype(jnp.float32)
    grad_probs = jnp.einsum('wqhd,wkhd->whqk', grad_heads, value_heads)
    grad_value = jnp.einsum('whqk,wqhd->wkhd', rounded, grad_heads)
    grad_scores = weights * (grad_probs - lax.optimization_barrier(jnp.sum(grad_probs * weights, -1, keepdims=True))) * HEAD ** (-0.5)
    grad_rounded = lax.optimization_barrier(grad_scores.astype(jnp.bfloat16)).astype(jnp.float32)
    grad_query = jnp.einsum('whqk,wkhd->wqhd', grad_rounded, key_heads)
    grad_key = jnp.einsum('whqk,wqhd->wkhd', grad_rounded, query_heads)
    windows, tokens_in = (grad_query.shape[0], grad_query.shape[1])
    grad_kv = jnp.concatenate([grad_key.reshape(windows, tokens_in, D), grad_value.reshape(windows, tokens_in, D)], -1)
    return (grad_query.reshape(windows, tokens_in, D), grad_kv)

def layer_forward(token_field, labels, gain_vector, w_qkv, w_out):
    levels, lat_rows, lon_cols = labels.shape
    normalized_tokens, standardized, inverse_deviation = apply_norm(token_field, gain_vector)
    projected_tokens = jnp.dot(normalized_tokens.reshape(-1, D), w_qkv, preferred_element_type=jnp.float32)
    projected_tokens = projected_tokens.astype(jnp.bfloat16).reshape(levels, lat_rows, lon_cols, 3 * D)
    mixed_out = lax.map(lambda both: attend(both[0], both[1]), (to_windows(projected_tokens), to_windows(labels)))
    attention_result = from_windows(mixed_out, levels, lat_rows, lon_cols)
    update = jnp.dot(attention_result.reshape(-1, D), w_out, preferred_element_type=jnp.float32).reshape(token_field.shape)
    block_output = (token_field.astype(jnp.float32) + update).astype(jnp.bfloat16)
    return (block_output, (normalized_tokens, standardized, inverse_deviation, projected_tokens, attention_result))

def layer_backward(input_gradient, labels, gain_vector, w_qkv, w_out, saved_residuals):
    normalized_tokens, standardized, inverse_deviation, projected_tokens, attention_result = saved_residuals
    levels, lat_rows, lon_cols = labels.shape
    grad16 = input_gradient.astype(jnp.bfloat16).reshape(-1, D)
    grad_wout = jnp.dot(attention_result.reshape(-1, D).T, grad16, preferred_element_type=jnp.float32)
    grad_att = jnp.dot(grad16, w_out.T, preferred_element_type=jnp.float32).astype(jnp.bfloat16)
    grad_att = grad_att.reshape(levels, lat_rows, lon_cols, D)
    grad_query, grad_kv = lax.map(lambda trio_in: attend_back(trio_in[0], trio_in[1], trio_in[2]), (to_windows(projected_tokens), to_windows(labels), to_windows(grad_att)))
    grad_proj = jnp.concatenate([from_windows(grad_query, levels, lat_rows, lon_cols), from_windows(grad_kv, levels, lat_rows, lon_cols)], -1)
    grad_proj = grad_proj.astype(jnp.bfloat16).reshape(-1, 3 * D)
    grad_wqkv = jnp.dot(normalized_tokens.reshape(-1, D).T, grad_proj, preferred_element_type=jnp.float32)
    normalized_gradient = jnp.dot(grad_proj, w_qkv.T, preferred_element_type=jnp.float32).reshape(input_gradient.shape)
    scaled_tokens = normalized_gradient * gain_vector
    field_gradient = inverse_deviation * (scaled_tokens - lax.optimization_barrier(jnp.mean(scaled_tokens, -1, keepdims=True)) - standardized * lax.optimization_barrier(jnp.mean(scaled_tokens * standardized, -1, keepdims=True))) + input_gradient
    return (field_gradient, grad_wqkv, grad_wout)

def shift_field(token_field):
    pad_widths = [(0, 0), (WLAT // 2, WLAT // 2), (0, 0)] + [(0, 0)] * (token_field.ndim - 3)
    padded = jnp.pad(token_field, pad_widths)
    return jnp.roll(padded, -(WLON // 2), axis=2)

def unshift_field(token_field):
    rolled = jnp.roll(token_field, WLON // 2, axis=2)
    return rolled[:, WLAT // 2:rolled.shape[1] - WLAT // 2]

def reference(tokens, cotangent, region, unshifted_norm_gain, unshifted_query_key_value, out_first, shifted_norm_gain, shifted_query_key_value, out_second):
    unshifted_output, saved_first = layer_forward(tokens, region, unshifted_norm_gain, unshifted_query_key_value, out_first)
    shifted_region = shift_field(region)
    second_out, saved_second = layer_forward(shift_field(unshifted_output), shifted_region, shifted_norm_gain, shifted_query_key_value, out_second)
    result = unshift_field(second_out)
    grad_second = shift_field(cotangent.astype(jnp.float32))
    middle_gradient, grad_qkv_b, grad_out_b = layer_backward(grad_second, shifted_region, shifted_norm_gain, shifted_query_key_value, out_second, saved_second)
    token_gradient, grad_qkv_a, grad_out_a = layer_backward(unshift_field(middle_gradient), region, unshifted_norm_gain, unshifted_query_key_value, out_first, saved_first)
    norm_total = jnp.sum(grad_qkv_a * grad_qkv_a) + jnp.sum(grad_out_a * grad_out_a) + jnp.sum(grad_qkv_b * grad_qkv_b) + jnp.sum(grad_out_b * grad_out_b)
    factor = jnp.minimum(1.0, math.sqrt(8.0) * D / jnp.sqrt(norm_total))
    return (result, token_gradient.astype(jnp.bfloat16), grad_qkv_a * factor, grad_out_a * factor, grad_qkv_b * factor, grad_out_b * factor)
```

```python
import math

import jax
import jax.numpy as jnp
from jax import lax
from jax.experimental import pallas as pl
from jax.experimental.pallas import tpu as pltpu
from jax.sharding import PartitionSpec as P

D = 512
HEADS = 8
HEAD = 64
PAIRS = HEADS // 2
WLEV = 2
WLAT = 6
WLON = 12
HLAT = WLAT // 2
HLON = WLON // 2
TOK = WLEV * WLAT * WLON
QUART = TOK // 4
LANES = 128

X, YLO, YHI, Z = 4, 2, 2, 8
Y = YHI * YLO
LAT, LON = X * YLO, YHI * Z
OWN = D // (LAT * LON)
GROUP = 4
WIDE = 4 * D // GROUP
PLANE_ROWS = D // GROUP
LAST_ROWS = PLANE_ROWS // Z
SEND = 2 * D + LANES

EPSILON = 1e-05
NEGATIVE = -1e30
F32 = jnp.float32
BF16 = jnp.bfloat16
VMEM_BYTES = 16 * 1024 * 1024


def dot_nn(a, b):
    return lax.dot_general(a, b, (((1,), (0,)), ((), ())), preferred_element_type=F32)


def dot_nt(a, b):
    return lax.dot_general(a, b, (((1,), (1,)), ((), ())), preferred_element_type=F32)


def dot_tn(a, b):
    return lax.dot_general(a, b, (((0,), (0,)), ((), ())), preferred_element_type=F32)


def norm_parts(values, gain):
    average = jnp.mean(values, -1, keepdims=True)
    centered = values - average
    rstd = lax.rsqrt(jnp.mean(centered * centered, -1, keepdims=True) + EPSILON)
    xhat = centered * rstd
    return (xhat * gain).astype(BF16), xhat, rstd


def norm_back(dnormed, gain, xhat, rstd, incoming):
    s = dnormed * gain
    return (
        rstd * (s - jnp.mean(s, -1, keepdims=True) - xhat * jnp.mean(s * xhat, -1, keepdims=True))
        + incoming
    )


def label_bias(labels):
    lane = lax.broadcasted_iota(jnp.int32, (TOK, LANES), 1).astype(F32)
    hot = jnp.where((lane == labels) & (lane > 0.5), 1.0, 0.0).astype(BF16)
    return (1.0 - dot_nt(hot, hot)) * NEGATIVE


def head_masks():
    lane = lax.broadcasted_iota(jnp.int32, (1, LANES), 1)
    low = (lane < HEAD).astype(F32)
    return low, 1.0 - low


def pair_of(proj, part, pair):
    start = part * D + pair * LANES
    return proj[:, start : start + LANES]


def softmax_rows(scores):
    shifted = jnp.exp(scores - jnp.max(scores, -1, keepdims=True))
    return shifted * (1.0 / jnp.sum(shifted, -1, keepdims=True))


def attention(proj, bias, grad=None, forward=True):
    low, high = head_masks()
    is_low = low > 0.5
    masks = (low.astype(BF16), high.astype(BF16))
    att, dq, dk, dv = [], [], [], []
    for pair in range(PAIRS):
        q = pair_of(proj, 0, pair)
        k = pair_of(proj, 1, pair)
        v = pair_of(proj, 2, pair)
        o_h, dq_h, dk_h, dv_h = [], [], [], []
        for mask in masks:
            probs = softmax_rows(dot_nt(q * (mask * BF16(HEAD**-0.5)), k) + bias)
            p16 = probs.astype(BF16)
            if forward:
                o_h.append(dot_nn(p16, v))
            if grad is not None:
                g = grad[:, pair * LANES : (pair + 1) * LANES]
                dp = dot_nt(g * mask, v)
                delta = jnp.sum(dp * probs, -1, keepdims=True)
                ds16 = (probs * (dp - delta) * HEAD**-0.5).astype(BF16)
                dq_h.append(dot_nn(ds16, k))
                dk_h.append(dot_tn(ds16, q))
                dv_h.append(dot_tn(p16, g))
        if forward:
            att.append(jnp.where(is_low, o_h[0], o_h[1]).astype(BF16))
        if grad is not None:
            dq.append(jnp.where(is_low, dq_h[0], dq_h[1]).astype(BF16))
            dk.append(jnp.where(is_low, dk_h[0], dk_h[1]).astype(BF16))
            dv.append(jnp.where(is_low, dv_h[0], dv_h[1]).astype(BF16))
    attended = jnp.concatenate(att, -1) if forward else None
    dproj = jnp.concatenate(dq + dk + dv, -1) if grad is not None else None
    return attended, dproj


def gather_rows(refs, scratch, column):
    wide = scratch.shape[1]
    for slot, ref in enumerate(refs):
        scratch[slot * QUART : (slot + 1) * QUART, :] = ref[:, column : column + wide].astype(F32)
    return scratch[...]


def scatter_rows(values, scratch, refs, column):
    scratch[...] = values
    wide = scratch.shape[1]
    for slot, ref in enumerate(refs):
        ref[:, column : column + wide] = scratch[slot * QUART : (slot + 1) * QUART, :].astype(BF16)


def regroup(source_of):
    to = lax.broadcasted_iota(jnp.int32, (1, D), 1)
    return (lax.broadcasted_iota(jnp.int32, (D, D), 0) == source_of(to)).astype(F32).astype(BF16)


def row_of(x, y, z, own):
    return (((x * YLO + y % YLO) * YHI + y // YLO) * Z + z) * OWN + own


def order_x(to):
    x = to // OWN % X
    return row_of(x, to // (OWN * X * Z), to // (OWN * X) % Z, to % OWN)


def order_y(to):
    y = to // OWN % Y
    return row_of(to // (OWN * Y * Z), y, to // (OWN * Y) % Z, to % OWN)


def pack(me, left_refs, right_ref, packs):
    for step, ref in enumerate(packs):
        peer = me ^ step
        is_att = peer == GROUP - 1

        @pl.when(is_att)
        def _():
            ref[:, :D] = left_refs[1][...]

        @pl.when(jnp.logical_not(is_att))
        def _():
            ref[:, :D] = left_refs[0][...]

        ref[:, D:] = right_ref[peer]


def store_right(dproj, g16, right_ref):
    for part in range(3):
        right_ref[part] = dproj[:, part * D : (part + 1) * D]
    right_ref[3] = g16


def first_forward(
    wrap, tok, cot, lab, gain, wqkv, wout,
    x0, x1, x2, x3, proj_ref, left_n, left_a, scratch, lab_scratch,
):
    values = tok[...].astype(F32)
    normed, _, _ = norm_parts(values, gain[...])
    proj = dot_nn(normed, wqkv[...]).astype(BF16)
    proj_ref[...] = proj
    labels = lab[...].astype(F32)
    attended, _ = attention(proj, label_bias(labels))
    refs = (x0, x1, x2, x3)
    scatter_rows(values + dot_nn(attended, wout[...]), scratch, refs, 0)
    scatter_rows(cot[...].astype(F32), scratch, refs, D)
    near = lax.broadcasted_iota(jnp.int32, (TOK, LANES), 0) < 2 * QUART
    moved = labels + jnp.where(near, wrap[0].astype(F32), 0.0)
    scatter_rows(moved, lab_scratch, refs, 2 * D)
    order = regroup(order_x)
    left_n[...] = dot_nn(normed, order).astype(BF16)
    left_a[...] = dot_nn(attended, order).astype(BF16)


def second_main(
    x0, x1, x2, x3, gain, wqkv, wout,
    b0, b1, b2, b3, normed_ref, att_ref, right_ref, scratch, lab_scratch,
):
    parts = (x0, x1, x2, x3)
    back = (b0, b1, b2, b3)
    values = gather_rows(parts, scratch, 0)
    g = gather_rows(parts, scratch, D)
    labels = gather_rows(parts, lab_scratch, 2 * D)
    g16 = g.astype(BF16)
    normed, xhat, rstd = norm_parts(values, gain[...])
    normed_ref[...] = normed
    proj = dot_nn(normed, wqkv[...]).astype(BF16)
    datt = dot_nt(g16, wout[...]).astype(BF16)
    attended, dproj = attention(proj, label_bias(labels), grad=datt)
    att_ref[...] = attended
    store_right(dproj, g16, right_ref)
    scatter_rows(values + dot_nn(attended, wout[...]), scratch, back, 0)
    dnormed = dot_nt(dproj, wqkv[...])
    scatter_rows(norm_back(dnormed, gain[...], xhat, rstd, g), scratch, back, D)


def second_pack(me, normed, attended, right, p0, p1, p2, p3, left_n, left_a):
    order = regroup(order_y)
    left_n[...] = dot_nn(normed[...], order).astype(BF16)
    left_a[...] = dot_nn(attended[...], order).astype(BF16)
    pack(me[0], (left_n, left_a), right, (p0, p1, p2, p3))


def first_backward(
    me, b0, b1, b2, b3, lab, wout, proj_ref, left_n, left_a,
    right_ref, p0, p1, p2, p3, scratch,
):
    g16 = gather_rows((b0, b1, b2, b3), scratch, D).astype(BF16)
    datt = dot_nt(g16, wout[...]).astype(BF16)
    _, dproj = attention(
        proj_ref[...], label_bias(lab[...].astype(F32)), grad=datt, forward=False
    )
    store_right(dproj, g16, right_ref)
    pack(me[0], (left_n, left_a), right_ref, (p0, p1, p2, p3))


def first_rest(b0, b1, b2, b3, tok, gain, wqkv, right, tg_ref, scratch):
    g = gather_rows((b0, b1, b2, b3), scratch, D)
    _, xhat, rstd = norm_parts(tok[...].astype(F32), gain[...])
    dnormed = dot_nt(right[0], wqkv[:, :D])
    dnormed += dot_nt(right[1], wqkv[:, D : 2 * D])
    dnormed += dot_nt(right[2], wqkv[:, 2 * D :])
    tg_ref[...] = norm_back(dnormed, gain[...], xhat, rstd, g).astype(BF16)


def weights(me, p0, p1, p2, p3, q0, q1, q2, q3, scratch):
    total = jnp.zeros((D, WIDE), F32)
    for part in (p0, p1, p2, p3):
        total += dot_tn(part[:, :D], part[:, D:])
    scratch[...] = total
    for step, ref in enumerate((q0, q1, q2, q3)):
        first = pl.multiple_of((me[0] ^ step) * PLANE_ROWS, PLANE_ROWS)
        ref[...] = scratch[pl.ds(first, PLANE_ROWS), :].astype(BF16)


def add_rows(a0, a1, a2, a3, b0, b1, b2, b3, out_ref):
    for slot, parts in enumerate(((a0, a1, a2, a3), (b0, b1, b2, b3))):
        total = sum(part[...].astype(F32) for part in parts).astype(BF16)
        for z in range(Z):
            out_ref[z, slot * LAST_ROWS : (slot + 1) * LAST_ROWS, :] = total[
                z * LAST_ROWS : (z + 1) * LAST_ROWS
            ]


PIECE = OWN * WIDE // LANES


def to_owners(parts, send_ref):
    total = jnp.sum(parts[...].astype(F32), 0)
    squares = jnp.sum(total * total, keepdims=True)
    for x in range(X):
        for y in range(Y):
            for slot, row in ((0, x * OWN), (1, LAST_ROWS + y * OWN)):
                for c in range(WIDE // LANES):
                    first = slot * PIECE + c * OWN
                    send_ref[x * Y + y, first : first + OWN, :] = total[
                        row : row + OWN, c * LANES : (c + 1) * LANES
                    ]
            send_ref[x * Y + y, 2 * PIECE :, :] = jnp.broadcast_to(squares, (8, LANES))


def spread(got, tile_ref):
    tile_ref[...] = jnp.broadcast_to(jnp.sum(got[:, 2 * PIECE :, :], 0)[None], tile_ref.shape)


def clipped(where, got, tiles, qkv_a, out_a, qkv_b, out_b):
    total = jnp.sum(tiles[...], 0)[:1, :1]
    factor = jnp.minimum(1.0, math.sqrt(8.0) * D / jnp.sqrt(total))
    x, y = where[0], where[1]
    for k in range(GROUP):
        for slot, source, refs in (
            (0, k * Y + y, (qkv_a, out_a)),
            (1, x * Y + k, (qkv_b, out_b)),
        ):
            ref, column = (refs[0], k * WIDE) if k < 3 else (refs[1], 0)
            for c in range(WIDE // LANES):
                first = slot * PIECE + c * OWN
                ref[:, column + c * LANES : column + (c + 1) * LANES] = (
                    got[source, first : first + OWN, :] * factor
                )


def shape_of(*dims, dtype=BF16):
    return jax.ShapeDtypeStruct(dims, dtype)


def call(kernel, outs, scratch, *args, scalar=False, dtype=F32):
    whole = pl.BlockSpec(memory_space=pltpu.VMEM)
    specs = [whole] * len(args)
    if scalar:
        specs[0] = pl.BlockSpec(memory_space=pltpu.SMEM)
    return pl.pallas_call(
        kernel,
        out_shape=outs,
        in_specs=specs,
        out_specs=[whole] * len(outs),
        scratch_shapes=[pltpu.VMEM(s, dtype) for s in scratch],
        compiler_params=pltpu.CompilerParams(vmem_limit_bytes=VMEM_BYTES),
        name=kernel.__name__,
    )(*args)


def quarters(field):
    trailing = field.shape[3:]
    shaped = field.reshape((WLEV, 2, HLAT, 2, HLON) + trailing)
    order = (1, 3, 0, 2, 4) + tuple(range(5, 5 + len(trailing)))
    return shaped.transpose(order).reshape((4, QUART) + trailing)


def unquarters(field):
    trailing = field.shape[2:]
    shaped = field.reshape((2, 2, WLEV, HLAT, HLON) + trailing)
    order = (2, 0, 3, 1, 4) + tuple(range(5, 5 + len(trailing)))
    return shaped.transpose(order).reshape((WLEV, WLAT, WLON) + trailing)


def moves(lat_count, lon_count):
    tables = []
    for a in range(2):
        for b in range(2):
            table = []
            for i in range(lat_count):
                for j in range(lon_count):
                    ti = (i - (1 - a)) % lat_count
                    tj = (j - (1 - b)) % lon_count
                    table.append((i * lon_count + j, ti * lon_count + tj))
            tables.append(table)
    return tables


def send(parts, tables, back=False):
    out = []
    for part, table in zip(parts, tables):
        if all(s == t for s, t in table):
            out.append(part)
            continue
        pairs = [(t, s) for s, t in table] if back else table
        out.append(lax.ppermute(part, ("lat", "lon"), pairs))
    return out


def index_of(x, y, z):
    return (x * YLO + y % YLO) * LON + y // YLO * Z + z


CHIPS = [(x, y, z) for x in range(X) for y in range(Y) for z in range(Z)]
PLANE = [[index_of(x, y, z) for x in range(X) for y in range(Y)] for z in range(Z)]
COLUMN = [[index_of(x, y, z) for z in range(Z)] for x in range(X) for y in range(Y)]


def swap(packs, axis):
    out = [packs[0]]
    for step in range(1, GROUP):
        pairs = [
            (index_of(x, y, z), index_of(x ^ step, y, z) if axis == "x" else index_of(x, y ^ step, z))
            for x, y, z in CHIPS
        ]
        out.append(lax.ppermute(packs[step], ("lat", "lon"), pairs))
    return out


def exchange(parts, groups):
    return lax.all_to_all(parts, ("lat", "lon"), 0, 0, axis_index_groups=groups)


def after(value, earlier):
    return lax.optimization_barrier((value, earlier))[0]


def on_device(
    tokens,
    cotangent,
    region,
    unshifted_norm_gain,
    unshifted_query_key_value,
    out_first,
    shifted_norm_gain,
    shifted_query_key_value,
    out_second,
):
    tables = moves(LAT, LON)
    lat, lon = lax.axis_index("lat"), lax.axis_index("lon")
    at_x = (lat // YLO).astype(jnp.int32)
    at_y = (lon // Z * YLO + lat % YLO).astype(jnp.int32)
    me_x, me_y = at_x.reshape(1), at_y.reshape(1)
    wrap = jnp.where(lat == 0, 4, 0).astype(jnp.int32).reshape(1)
    gain_a = unshifted_norm_gain.reshape(1, D)
    gain_b = shifted_norm_gain.reshape(1, D)
    tok = quarters(tokens).reshape(TOK, D)
    cot = quarters(cotangent).reshape(TOK, D)
    lab = jnp.broadcast_to(quarters(region).reshape(TOK, 1), (TOK, LANES)).astype(BF16)

    field = shape_of(TOK, D)
    fields = shape_of(GROUP, TOK, D)
    packs = [shape_of(TOK, D + WIDE)] * GROUP
    *x, proj_a, left_n, left_a = call(
        first_forward,
        [shape_of(QUART, SEND)] * 4 + [shape_of(TOK, 3 * D), field, field],
        [(TOK, D), (TOK, LANES)],
        wrap, tok, cot, lab, gain_a, unshifted_query_key_value, out_first,
        scalar=True,
    )
    x = send(x, tables)
    *back, normed_b, att_b, right_b = call(
        second_main,
        [shape_of(QUART, 2 * D)] * 4 + [field, field, fields],
        [(TOK, D), (TOK, LANES)],
        *x, gain_b, shifted_query_key_value, out_second,
    )
    back = send(back, tables, back=True)
    pack_b = call(
        second_pack,
        packs,
        [(TOK, D), (TOK, D)],
        me_y, normed_b, att_b, right_b,
        scalar=True, dtype=BF16,
    )
    pack_b = swap(after(pack_b, back[:3]), "y")
    right_a, *pack_a = call(
        first_backward,
        [fields] + packs,
        [(TOK, D)],
        me_x, *back, lab, out_first, proj_a, left_n, left_a,
        scalar=True,
    )
    pack_a = swap(pack_a, "x")
    (token_gradient,) = call(
        first_rest,
        [field],
        [(TOK, D)],
        *back, tok, gain_a, unshifted_query_key_value, right_a,
    )
    token_gradient = unquarters(token_gradient.reshape(4, QUART, D))
    result = unquarters(jnp.stack(back)[..., :D])

    rows = [shape_of(PLANE_ROWS, WIDE)] * GROUP
    sum_b = swap(call(weights, rows, [(D, WIDE)], me_x, *pack_b, scalar=True), "x")
    sum_a = swap(call(weights, rows, [(D, WIDE)], me_y, *pack_a, scalar=True), "y")
    (sums,) = call(add_rows, [shape_of(Z, 2 * LAST_ROWS, WIDE)], [], *sum_a, *sum_b)
    sums = exchange(sums, COLUMN)
    (pieces,) = call(
        to_owners, [shape_of(X * Y, 2 * PIECE + 8, LANES, dtype=F32)], [], sums
    )
    pieces = exchange(pieces, PLANE)
    (tiles,) = call(spread, [shape_of(Z, 8, LANES, dtype=F32)], [], pieces)
    tiles = exchange(tiles, COLUMN)
    out_qkv, out_out = shape_of(OWN, 3 * D, dtype=F32), shape_of(OWN, D, dtype=F32)
    clips = call(
        clipped, [out_qkv, out_out] * 2, [], jnp.stack([at_x, at_y]), pieces, tiles, scalar=True
    )
    return (result, token_gradient, *clips)


def solution(mesh):
    field = P("rep", "lat", "lon", None)
    rows = P(("rep", "lat", "lon"), None)
    in_specs = (field, field, P("rep", "lat", "lon"), P(), P(), P(), P(), P(), P())
    return jax.shard_map(
        on_device,
        mesh=mesh,
        in_specs=in_specs,
        out_specs=(field, field, rows, rows, rows, rows),
        check_vma=False,
    )
```

```python
import math

import jax
import jax.numpy as jnp
from jax import lax
from jax.experimental import pallas as pl
from jax.experimental.pallas import tpu as pltpu
from jax.sharding import PartitionSpec as P

D = 512
HEADS = 8
HEAD = 64
PAIRS = HEADS // 2
WLEV = 2
WLAT = 6
WLON = 12
HLAT = WLAT // 2
HLON = WLON // 2
TOK = WLEV * WLAT * WLON
QUART = TOK // 4
LANES = 128

X, YLO, YHI, Z = 4, 2, 2, 8
Y = YHI * YLO
LAT, LON = X * YLO, YHI * Z
OWN = D // (LAT * LON)
GROUP = 4
WIDE = 4 * D // GROUP
PLANE_ROWS = D // GROUP
LAST_ROWS = PLANE_ROWS // Z
SEND = 2 * D + LANES

EPSILON = 1e-05
NEGATIVE = -1e30
F32 = jnp.float32
BF16 = jnp.bfloat16
VMEM_BYTES = 16 * 1024 * 1024


def dot_nn(a, b):
    return lax.dot_general(a, b, (((1,), (0,)), ((), ())), preferred_element_type=F32)


def dot_nt(a, b):
    return lax.dot_general(a, b, (((1,), (1,)), ((), ())), preferred_element_type=F32)


def dot_tn(a, b):
    return lax.dot_general(a, b, (((0,), (0,)), ((), ())), preferred_element_type=F32)


def norm_parts(values, gain):
    average = jnp.mean(values, -1, keepdims=True)
    centered = values - average
    rstd = lax.rsqrt(jnp.mean(centered * centered, -1, keepdims=True) + EPSILON)
    xhat = centered * rstd
    return (xhat * gain).astype(BF16), xhat, rstd


def norm_back(dnormed, gain, xhat, rstd, incoming):
    s = dnormed * gain
    return (
        rstd * (s - jnp.mean(s, -1, keepdims=True) - xhat * jnp.mean(s * xhat, -1, keepdims=True))
        + incoming
    )


def label_bias(labels):
    lane = lax.broadcasted_iota(jnp.int32, (TOK, LANES), 1).astype(F32)
    hot = jnp.where((lane == labels) & (lane > 0.5), 1.0, 0.0).astype(BF16)
    return (1.0 - dot_nt(hot, hot)) * NEGATIVE


def pair_of(fields, part, pair):
    start = part * D + pair * LANES
    return fields[:, start : start + LANES]


def softmax_rows(scores):
    shifted = jnp.exp(scores - jnp.max(scores, -1, keepdims=True))
    return shifted * (1.0 / jnp.sum(shifted, -1, keepdims=True))


def attention(proj, bias, grad=None, attended=None):
    lane = lax.broadcasted_iota(jnp.int32, (1, LANES), 1)
    is_low = lane < HEAD
    low = is_low.astype(F32)
    masks = (low.astype(BF16), (1.0 - low).astype(BF16))
    bias = jnp.concatenate([bias, bias], 0)

    def stacked(field):
        return jnp.concatenate([field * masks[0], field * masks[1]], 0)

    def merged(both):
        return jnp.where(is_low, both[:TOK], both[TOK:])

    att, dq, dk, dv = [], [], [], []
    for pair in range(PAIRS):
        q = stacked(pair_of(proj, 0, pair) * BF16(HEAD**-0.5))
        k = pair_of(proj, 1, pair)
        v = pair_of(proj, 2, pair)
        probs = softmax_rows(dot_nt(q, k) + bias)
        p16 = probs.astype(BF16)
        if attended is None:
            o = merged(dot_nn(p16, v)).astype(BF16)
            att.append(o)
        else:
            o = pair_of(attended, 0, pair)
        if grad is not None:
            g = pair_of(grad, 0, pair)
            g_both = stacked(g)
            product = g.astype(F32) * o.astype(F32)
            delta = jnp.concatenate(
                [
                    jnp.sum(product * low, -1, keepdims=True),
                    jnp.sum(product * (1.0 - low), -1, keepdims=True),
                ],
                0,
            )
            ds16 = (probs * (dot_nt(g_both, v) - delta)).astype(BF16)
            dq.append((merged(dot_nn(ds16, k)) * HEAD**-0.5).astype(BF16))
            dk.append(dot_tn(ds16, q).astype(BF16))
            dv.append(dot_tn(p16, g_both).astype(BF16))
    if attended is None:
        attended = jnp.concatenate(att, -1)
    dproj = jnp.concatenate(dq + dk + dv, -1) if grad is not None else None
    return attended, dproj


def take_field(ref, scratch):
    half = HLON * WLEV
    for row in range(WLAT):
        values = ref[row].astype(F32).reshape(2 * half, D)
        for b in range(2):
            first = (2 * (row // HLAT) + b) * QUART + row % HLAT * half
            scratch[first : first + half, :] = values[b * half : (b + 1) * half]
    return scratch[...]


def put_field(values, scratch, ref):
    scratch[...] = values
    half = HLON * WLEV
    for row in range(WLAT):
        for b in range(2):
            first = (2 * (row // HLAT) + b) * QUART + row % HLAT * half
            ref[row, b * HLON : (b + 1) * HLON] = (
                scratch[first : first + half, :].reshape(HLON, WLEV, D).astype(BF16)
            )


def take_labels(region):
    places = WLAT * WLEV
    table = region[...].reshape(places, WLON).astype(F32)
    token = lax.broadcasted_iota(jnp.int32, (TOK, places), 0)
    slot, rest = token // QUART, token % QUART
    row = slot // 2 * HLAT + rest // (HLON * WLEV)
    column = slot % 2 * HLON + rest % (HLON * WLEV) // WLEV
    place = lax.broadcasted_iota(jnp.int32, (TOK, places), 1)
    rows = dot_nn((place == row * WLEV + rest % WLEV).astype(F32), table)
    return jnp.sum(jnp.where(place == column, rows, 0.0), -1, keepdims=True)


def gather_rows(refs, scratch, column):
    wide = scratch.shape[1]
    for slot, ref in enumerate(refs):
        scratch[slot * QUART : (slot + 1) * QUART, :] = ref[:, column : column + wide].astype(F32)
    return scratch[...]


def scatter_rows(values, scratch, refs, column):
    scratch[...] = values
    wide = scratch.shape[1]
    for slot, ref in enumerate(refs):
        ref[:, column : column + wide] = scratch[slot * QUART : (slot + 1) * QUART, :].astype(BF16)


def regroup(source_of):
    to = lax.broadcasted_iota(jnp.int32, (1, D), 1)
    return (lax.broadcasted_iota(jnp.int32, (D, D), 0) == source_of(to)).astype(F32).astype(BF16)


def row_of(x, y, z, own):
    return (((x * YLO + y % YLO) * YHI + y // YLO) * Z + z) * OWN + own


def order_x(to):
    x = to // OWN % X
    return row_of(x, to // (OWN * X * Z), to // (OWN * X) % Z, to % OWN)


def order_y(to):
    y = to // OWN % Y
    return row_of(to // (OWN * Y * Z), y, to // (OWN * Y) % Z, to % OWN)


def pack(me, left_refs, right_ref, packs):
    for step, ref in enumerate(packs):
        peer = me ^ step
        is_att = peer == GROUP - 1

        @pl.when(is_att)
        def _():
            ref[:, :D] = left_refs[1][...]

        @pl.when(jnp.logical_not(is_att))
        def _():
            ref[:, :D] = left_refs[0][...]

        ref[:, D:] = right_ref[peer]


def store_right(dproj, g16, right_ref):
    for part in range(3):
        right_ref[part] = dproj[:, part * D : (part + 1) * D]
    right_ref[3] = g16


def first_forward(
    wrap, region, tok, cot, gain_hbm, wqkv_hbm, wout_hbm,
    x0, x1, x2, x3, keep_ref, scratch, lab_scratch, gain, wqkv, wout, sems,
):
    copies = [
        pltpu.make_async_copy(source, target, sems.at[i])
        for i, (source, target) in enumerate(((gain_hbm, gain), (wqkv_hbm, wqkv), (wout_hbm, wout)))
    ]
    for copy in copies:
        copy.start()
    refs = (x0, x1, x2, x3)
    take_field(cot, scratch)
    for slot, ref in enumerate(refs):
        ref[:, D : 2 * D] = scratch[slot * QUART : (slot + 1) * QUART, :].astype(BF16)
    labels = jnp.broadcast_to(take_labels(region), (TOK, LANES))
    near = lax.broadcasted_iota(jnp.int32, (TOK, LANES), 0) < 2 * QUART
    moved = labels + jnp.where(near, wrap[0].astype(F32), 0.0)
    scatter_rows(moved, lab_scratch, refs, 2 * D)
    values = take_field(tok, scratch)
    copies[0].wait()
    normed, _, _ = norm_parts(values, gain[...])
    copies[1].wait()
    proj = dot_nn(normed, wqkv[...]).astype(BF16)
    keep_ref[:, : 3 * D] = proj
    keep_ref[:, 4 * D :] = labels.astype(BF16)
    attended, _ = attention(proj, label_bias(labels))
    keep_ref[:, 3 * D : 4 * D] = attended
    copies[2].wait()
    scatter_rows(values + dot_nn(attended, wout[...]), scratch, refs, 0)


def second_main(
    x0, x1, x2, x3, gain, wqkv, wout,
    b0, b1, b2, b3, normed_ref, att_ref, right_ref, scratch, lab_scratch,
):
    parts = (x0, x1, x2, x3)
    back = (b0, b1, b2, b3)
    values = gather_rows(parts, scratch, 0)
    g = gather_rows(parts, scratch, D)
    labels = gather_rows(parts, lab_scratch, 2 * D)
    g16 = g.astype(BF16)
    normed, xhat, rstd = norm_parts(values, gain[...])
    normed_ref[...] = normed
    proj = dot_nn(normed, wqkv[...]).astype(BF16)
    datt = dot_nt(g16, wout[...]).astype(BF16)
    attended, dproj = attention(proj, label_bias(labels), grad=datt)
    att_ref[...] = attended
    store_right(dproj, g16, right_ref)
    scatter_rows(values + dot_nn(attended, wout[...]), scratch, back, 0)
    dnormed = dot_nt(dproj, wqkv[...])
    scatter_rows(norm_back(dnormed, gain[...], xhat, rstd, g), scratch, back, D)


def second_pack(
    me, normed, attended, right, tok, gain, keep,
    p0, p1, p2, p3, first_n, first_a, left_n, left_a, scratch,
):
    order = regroup(order_y)
    left_n[...] = dot_nn(normed[...], order).astype(BF16)
    left_a[...] = dot_nn(attended[...], order).astype(BF16)
    pack(me[0], (left_n, left_a), right, (p0, p1, p2, p3))
    order = regroup(order_x)
    normed, _, _ = norm_parts(take_field(tok, scratch), gain[...])
    first_n[...] = dot_nn(normed, order).astype(BF16)
    first_a[...] = dot_nn(keep[:, 3 * D : 4 * D], order).astype(BF16)


def first_backward(
    me, b0, b1, b2, b3, wout, keep, left_n, left_a, right_ref, p0, p1, p2, p3, scratch
):
    g16 = gather_rows((b0, b1, b2, b3), scratch, D).astype(BF16)
    datt = dot_nt(g16, wout[...]).astype(BF16)
    bias = label_bias(keep[:, 4 * D :].astype(F32))
    _, dproj = attention(keep[...], bias, grad=datt, attended=keep[:, 3 * D : 4 * D])
    store_right(dproj, g16, right_ref)
    pack(me[0], (left_n, left_a), right_ref, (p0, p1, p2, p3))


def first_rest(b0, b1, b2, b3, tok, gain, wqkv, right, tg_ref, result_ref, scratch):
    back = (b0, b1, b2, b3)
    put_field(gather_rows(back, scratch, 0), scratch, result_ref)
    _, xhat, rstd = norm_parts(take_field(tok, scratch), gain[...])
    g = gather_rows(back, scratch, D)
    dnormed = dot_nt(right[0], wqkv[:, :D])
    dnormed += dot_nt(right[1], wqkv[:, D : 2 * D])
    dnormed += dot_nt(right[2], wqkv[:, 2 * D :])
    put_field(norm_back(dnormed, gain[...], xhat, rstd, g), scratch, tg_ref)


def weights(me, p0, p1, p2, p3, q0, q1, q2, q3, scratch):
    total = jnp.zeros((D, WIDE), F32)
    for part in (p0, p1, p2, p3):
        total += dot_tn(part[:, :D], part[:, D:])
    scratch[...] = total
    for step, ref in enumerate((q0, q1, q2, q3)):
        first = pl.multiple_of((me[0] ^ step) * PLANE_ROWS, PLANE_ROWS)
        ref[...] = scratch[pl.ds(first, PLANE_ROWS), :].astype(BF16)


def add_rows(a0, a1, a2, a3, b0, b1, b2, b3, out_ref):
    for slot, parts in enumerate(((a0, a1, a2, a3), (b0, b1, b2, b3))):
        total = sum(part[...].astype(F32) for part in parts).astype(BF16)
        for z in range(Z):
            out_ref[z, slot * LAST_ROWS : (slot + 1) * LAST_ROWS, :] = total[
                z * LAST_ROWS : (z + 1) * LAST_ROWS
            ]


PIECE = OWN * WIDE // LANES


def to_owners(parts, send_ref, scratch):
    total = jnp.sum(parts[...].astype(F32), 0)
    rest = jnp.sum(total * total, keepdims=True)
    terms = []
    for _ in range(3):
        term = rest.astype(BF16).astype(F32)
        terms.append(term)
        rest = rest - term
    terms = jnp.concatenate([jnp.broadcast_to(term, (1, LANES)) for term in terms], 0)
    for x in range(X):
        for y in range(Y):
            for slot, row in ((0, x * OWN), (1, LAST_ROWS + y * OWN)):
                for c in range(WIDE // LANES):
                    first = slot * PIECE + c * OWN
                    scratch[x * Y + y, first : first + OWN, :] = total[
                        row : row + OWN, c * LANES : (c + 1) * LANES
                    ]
            scratch[x * Y + y, 2 * PIECE :, :] = jnp.zeros((16, LANES), F32)
            scratch[x * Y + y, 2 * PIECE : 2 * PIECE + 3, :] = terms
    send_ref[...] = scratch[...].astype(BF16)


def spread(got, tile_ref):
    terms = jnp.sum(got[:, 2 * PIECE :, :].astype(F32), 0)
    squares = jnp.sum(terms, 0, keepdims=True)
    tile_ref[...] = jnp.broadcast_to(squares[None], tile_ref.shape)


def clipped(where, got, tiles, qkv_a, out_a, qkv_b, out_b, scratch):
    scratch[...] = got[:, : 2 * PIECE, :].astype(F32)
    total = jnp.sum(tiles[...], 0)[:1, :1]
    factor = jnp.minimum(1.0, math.sqrt(8.0) * D / jnp.sqrt(total))
    x, y = where[0], where[1]
    for k in range(GROUP):
        for slot, source, refs in (
            (0, k * Y + y, (qkv_a, out_a)),
            (1, x * Y + k, (qkv_b, out_b)),
        ):
            ref, column = (refs[0], k * WIDE) if k < 3 else (refs[1], 0)
            for c in range(WIDE // LANES):
                first = slot * PIECE + c * OWN
                ref[:, column + c * LANES : column + (c + 1) * LANES] = (
                    scratch[source, first : first + OWN, :] * factor
                )


def shape_of(*dims, dtype=BF16):
    return jax.ShapeDtypeStruct(dims, dtype)


def call(kernel, outs, scratch, *args, scalar=False, far=0):
    whole = pl.BlockSpec(memory_space=pltpu.VMEM)
    specs = [whole] * (len(args) - far) + [pl.BlockSpec(memory_space=pl.ANY)] * far
    if scalar:
        specs[0] = pl.BlockSpec(memory_space=pltpu.SMEM)
    scratch = [pltpu.VMEM(s, F32) if isinstance(s, tuple) else s for s in scratch]
    return pl.pallas_call(
        kernel,
        out_shape=outs,
        in_specs=specs,
        out_specs=[whole] * len(outs),
        scratch_shapes=scratch,
        compiler_params=pltpu.CompilerParams(vmem_limit_bytes=VMEM_BYTES),
        name=kernel.__name__,
    )(*args)


def moves(lat_count, lon_count):
    tables = []
    for a in range(2):
        for b in range(2):
            table = []
            for i in range(lat_count):
                for j in range(lon_count):
                    ti = (i - (1 - a)) % lat_count
                    tj = (j - (1 - b)) % lon_count
                    table.append((i * lon_count + j, ti * lon_count + tj))
            tables.append(table)
    return tables


def send(parts, tables, back=False):
    out = []
    for part, table in zip(parts, tables):
        if all(s == t for s, t in table):
            out.append(part)
            continue
        pairs = [(t, s) for s, t in table] if back else table
        out.append(lax.ppermute(part, ("lat", "lon"), pairs))
    return out


def index_of(x, y, z):
    return (x * YLO + y % YLO) * LON + y // YLO * Z + z


CHIPS = [(x, y, z) for x in range(X) for y in range(Y) for z in range(Z)]
PLANE = [[index_of(x, y, z) for x in range(X) for y in range(Y)] for z in range(Z)]
COLUMN = [[index_of(x, y, z) for z in range(Z)] for x in range(X) for y in range(Y)]


def swap(packs, axis):
    out = [packs[0]]
    for step in range(1, GROUP):
        pairs = [
            (index_of(x, y, z), index_of(x ^ step, y, z) if axis == "x" else index_of(x, y ^ step, z))
            for x, y, z in CHIPS
        ]
        out.append(lax.ppermute(packs[step], ("lat", "lon"), pairs))
    return out


def exchange(parts, groups):
    return lax.all_to_all(parts, ("lat", "lon"), 0, 0, axis_index_groups=groups)


def after(value, earlier):
    return lax.optimization_barrier((value, earlier))[0]


def on_device(
    tokens,
    cotangent,
    region,
    unshifted_norm_gain,
    unshifted_query_key_value,
    out_first,
    shifted_norm_gain,
    shifted_query_key_value,
    out_second,
):
    tables = moves(LAT, LON)
    lat, lon = lax.axis_index("lat"), lax.axis_index("lon")
    at_x = (lat // YLO).astype(jnp.int32)
    at_y = (lon // Z * YLO + lat % YLO).astype(jnp.int32)
    me_x, me_y = at_x.reshape(1), at_y.reshape(1)
    wrap = jnp.where(lat == 0, 4, 0).astype(jnp.int32).reshape(1)
    gain_a = unshifted_norm_gain.reshape(1, D)
    gain_b = shifted_norm_gain.reshape(1, D)
    tok = tokens.transpose(1, 2, 0, 3)
    cot = cotangent.transpose(1, 2, 0, 3)
    lab = region.transpose(1, 0, 2)

    field = shape_of(TOK, D)
    fields = shape_of(GROUP, TOK, D)
    packs = [shape_of(TOK, D + WIDE)] * GROUP
    *x, keep = call(
        first_forward,
        [shape_of(QUART, SEND)] * 4 + [shape_of(TOK, 4 * D + LANES)],
        [
            (TOK, D),
            (TOK, LANES),
            (1, D),
            pltpu.VMEM((D, 3 * D), BF16),
            pltpu.VMEM((D, D), BF16),
            pltpu.SemaphoreType.DMA((3,)),
        ],
        wrap, lab, tok, cot, gain_a, unshifted_query_key_value, out_first,
        scalar=True, far=3,
    )
    x = send(x, tables)
    *back, normed_b, att_b, right_b = call(
        second_main,
        [shape_of(QUART, 2 * D)] * 4 + [field, field, fields],
        [(TOK, D), (TOK, LANES)],
        *x, gain_b, shifted_query_key_value, out_second,
    )
    back = send(back, tables, back=True)
    *pack_b, left_n, left_a = call(
        second_pack,
        packs + [field, field],
        [pltpu.VMEM((TOK, D), BF16), pltpu.VMEM((TOK, D), BF16), (TOK, D)],
        me_y, normed_b, att_b, right_b, tok, gain_a, keep,
        scalar=True,
    )
    pack_b = swap(after(pack_b, back[:3]), "y")
    right_a, *pack_a = call(
        first_backward,
        [fields] + packs,
        [(TOK, D)],
        me_x, *back, out_first, keep, left_n, left_a,
        scalar=True,
    )
    pack_a = swap(pack_a, "x")
    grid = shape_of(WLAT, WLON, WLEV, D)
    token_gradient, result = call(
        first_rest,
        [grid, grid],
        [(TOK, D)],
        *back, tok, gain_a, unshifted_query_key_value, right_a,
    )
    token_gradient = token_gradient.transpose(2, 0, 1, 3)
    result = result.transpose(2, 0, 1, 3)

    rows = [shape_of(PLANE_ROWS, WIDE)] * GROUP
    sum_b = swap(call(weights, rows, [(D, WIDE)], me_x, *pack_b, scalar=True), "x")
    sum_a = swap(call(weights, rows, [(D, WIDE)], me_y, *pack_a, scalar=True), "y")
    (sums,) = call(add_rows, [shape_of(Z, 2 * LAST_ROWS, WIDE)], [], *sum_a, *sum_b)
    sums = exchange(sums, COLUMN)
    piece = (X * Y, 2 * PIECE + 16, LANES)
    (pieces,) = call(to_owners, [shape_of(*piece)], [piece], sums)
    pieces = exchange(pieces, PLANE)
    (tiles,) = call(spread, [shape_of(Z, 8, LANES, dtype=F32)], [], pieces)
    tiles = exchange(tiles, COLUMN)
    out_qkv, out_out = shape_of(OWN, 3 * D, dtype=F32), shape_of(OWN, D, dtype=F32)
    clips = call(
        clipped,
        [out_qkv, out_out] * 2,
        [(X * Y, 2 * PIECE, LANES)],
        jnp.concatenate([me_x, me_y]), pieces, tiles,
        scalar=True,
    )
    return (result, token_gradient, *clips)


def solution(mesh):
    field = P("rep", "lat", "lon", None)
    rows = P(("rep", "lat", "lon"), None)
    in_specs = (field, field, P("rep", "lat", "lon"), P(), P(), P(), P(), P(), P())
    return jax.shard_map(
        on_device,
        mesh=mesh,
        in_specs=in_specs,
        out_specs=(field, field, rows, rows, rows, rows),
        check_vma=False,
    )
```

```python
import math

import jax
import jax.numpy as jnp
from jax import lax
from jax.experimental import pallas as pl
from jax.experimental.pallas import tpu as pltpu
from jax.sharding import PartitionSpec as P

D = 512
HEADS = 8
HEAD = 64
PAIRS = HEADS // 2
WLEV = 2
WLAT = 6
WLON = 12
HLAT = WLAT // 2
HLON = WLON // 2
TOK = WLEV * WLAT * WLON
QUART = TOK // 4
LANES = 128

X, YLO, YHI, Z = 4, 2, 2, 8
Y = YHI * YLO
LAT, LON = X * YLO, YHI * Z
OWN = D // (LAT * LON)
GROUP = 4
WIDE = 4 * D // GROUP
PLANE_ROWS = D // GROUP
LAST_ROWS = PLANE_ROWS // Z
SEND = 2 * D + LANES

EPSILON = 1e-05
NEGATIVE = -1e30
F32 = jnp.float32
BF16 = jnp.bfloat16
VMEM_BYTES = 16 * 1024 * 1024
WHOLE_VMEM_BYTES = 62 * 1024 * 1024


def dot_nn(a, b):
    return lax.dot_general(a, b, (((1,), (0,)), ((), ())), preferred_element_type=F32)


def dot_nt(a, b):
    return lax.dot_general(a, b, (((1,), (1,)), ((), ())), preferred_element_type=F32)


def dot_tn(a, b):
    return lax.dot_general(a, b, (((0,), (0,)), ((), ())), preferred_element_type=F32)


def norm_parts(values, gain):
    average = jnp.mean(values, -1, keepdims=True)
    centered = values - average
    rstd = lax.rsqrt(jnp.mean(centered * centered, -1, keepdims=True) + EPSILON)
    xhat = centered * rstd
    return (xhat * gain).astype(BF16), xhat, rstd


def norm_back(dnormed, gain, xhat, rstd, incoming):
    s = dnormed * gain
    return (
        rstd * (s - jnp.mean(s, -1, keepdims=True) - xhat * jnp.mean(s * xhat, -1, keepdims=True))
        + incoming
    )


def label_bias(labels):
    lane = lax.broadcasted_iota(jnp.int32, (TOK, LANES), 1).astype(F32)
    hot = jnp.where((lane == labels) & (lane > 0.5), 1.0, 0.0).astype(BF16)
    return (1.0 - dot_nt(hot, hot)) * NEGATIVE


def pair_of(fields, part, pair):
    start = part * D + pair * LANES
    return fields[:, start : start + LANES]


def softmax_rows(scores):
    shifted = jnp.exp(scores - jnp.max(scores, -1, keepdims=True))
    return shifted * (1.0 / jnp.sum(shifted, -1, keepdims=True))


def attention(proj, bias, grad=None, attended=None):
    lane = lax.broadcasted_iota(jnp.int32, (1, LANES), 1)
    is_low = lane < HEAD
    low = is_low.astype(F32)
    masks = (low.astype(BF16), (1.0 - low).astype(BF16))
    bias = jnp.concatenate([bias, bias], 0)

    def stacked(field):
        return jnp.concatenate([field * masks[0], field * masks[1]], 0)

    def merged(both):
        return jnp.where(is_low, both[:TOK], both[TOK:])

    att, dq, dk, dv = [], [], [], []
    for pair in range(PAIRS):
        q = stacked(pair_of(proj, 0, pair) * BF16(HEAD**-0.5))
        k = pair_of(proj, 1, pair)
        v = pair_of(proj, 2, pair)
        probs = softmax_rows(dot_nt(q, k) + bias)
        p16 = probs.astype(BF16)
        if attended is None:
            o = merged(dot_nn(p16, v)).astype(BF16)
            att.append(o)
        else:
            o = pair_of(attended, 0, pair)
        if grad is not None:
            g = pair_of(grad, 0, pair)
            g_both = stacked(g)
            product = g.astype(F32) * o.astype(F32)
            delta = jnp.concatenate(
                [
                    jnp.sum(product * low, -1, keepdims=True),
                    jnp.sum(product * (1.0 - low), -1, keepdims=True),
                ],
                0,
            )
            ds16 = (probs * (dot_nt(g_both, v) - delta)).astype(BF16)
            dq.append((merged(dot_nn(ds16, k)) * HEAD**-0.5).astype(BF16))
            dk.append(dot_tn(ds16, q).astype(BF16))
            dv.append(dot_tn(p16, g_both).astype(BF16))
    if attended is None:
        attended = jnp.concatenate(att, -1)
    dproj = jnp.concatenate(dq + dk + dv, -1) if grad is not None else None
    return attended, dproj


def take_field(ref, scratch):
    half = HLON * WLEV
    for row in range(WLAT):
        values = ref[row].astype(F32).reshape(2 * half, D)
        for b in range(2):
            first = (2 * (row // HLAT) + b) * QUART + row % HLAT * half
            scratch[first : first + half, :] = values[b * half : (b + 1) * half]
    return scratch[...]


def put_field(values, scratch, ref):
    scratch[...] = values
    half = HLON * WLEV
    for row in range(WLAT):
        for b in range(2):
            first = (2 * (row // HLAT) + b) * QUART + row % HLAT * half
            ref[row, b * HLON : (b + 1) * HLON] = (
                scratch[first : first + half, :].reshape(HLON, WLEV, D).astype(BF16)
            )


def take_labels(region):
    places = WLAT * WLEV
    table = region[...].reshape(places, WLON).astype(F32)
    token = lax.broadcasted_iota(jnp.int32, (TOK, places), 0)
    slot, rest = token // QUART, token % QUART
    row = slot // 2 * HLAT + rest // (HLON * WLEV)
    column = slot % 2 * HLON + rest % (HLON * WLEV) // WLEV
    place = lax.broadcasted_iota(jnp.int32, (TOK, places), 1)
    rows = dot_nn((place == row * WLEV + rest % WLEV).astype(F32), table)
    return jnp.sum(jnp.where(place == column, rows, 0.0), -1, keepdims=True)


def gather_rows(refs, scratch, column):
    wide = scratch.shape[1]
    for slot, ref in enumerate(refs):
        scratch[slot * QUART : (slot + 1) * QUART, :] = ref[:, column : column + wide].astype(F32)
    return scratch[...]


def scatter_rows(values, scratch, refs, column):
    scratch[...] = values
    wide = scratch.shape[1]
    for slot, ref in enumerate(refs):
        ref[:, column : column + wide] = scratch[slot * QUART : (slot + 1) * QUART, :].astype(BF16)


def regroup(source_of):
    to = lax.broadcasted_iota(jnp.int32, (1, D), 1)
    return (lax.broadcasted_iota(jnp.int32, (D, D), 0) == source_of(to)).astype(F32).astype(BF16)


def row_of(x, y, z, own):
    return (((x * YLO + y % YLO) * YHI + y // YLO) * Z + z) * OWN + own


def order_x(to):
    x = to // OWN % X
    return row_of(x, to // (OWN * X * Z), to // (OWN * X) % Z, to % OWN)


def order_y(to):
    y = to // OWN % Y
    return row_of(to // (OWN * Y * Z), y, to // (OWN * Y) % Z, to % OWN)


def pack(me, left_refs, right_ref, packs):
    for step, ref in enumerate(packs):
        peer = me ^ step
        is_att = peer == GROUP - 1

        @pl.when(is_att)
        def _():
            ref[:, :D] = left_refs[1][...]

        @pl.when(jnp.logical_not(is_att))
        def _():
            ref[:, :D] = left_refs[0][...]

        ref[:, D:] = right_ref[peer]


def store_right(dproj, g16, right_ref):
    for part in range(3):
        right_ref[part] = dproj[:, part * D : (part + 1) * D]
    right_ref[3] = g16


def first_forward(
    wrap, region, tok, cot, gain_hbm, wqkv_hbm, wout_hbm,
    x0, x1, x2, x3, keep_ref, scratch, lab_scratch, gain, wqkv, wout, sems,
):
    copies = [
        pltpu.make_async_copy(source, target, sems.at[i])
        for i, (source, target) in enumerate(((gain_hbm, gain), (wqkv_hbm, wqkv), (wout_hbm, wout)))
    ]
    for copy in copies:
        copy.start()
    refs = (x0, x1, x2, x3)
    take_field(cot, scratch)
    for slot, ref in enumerate(refs):
        ref[:, D : 2 * D] = scratch[slot * QUART : (slot + 1) * QUART, :].astype(BF16)
    labels = jnp.broadcast_to(take_labels(region), (TOK, LANES))
    near = lax.broadcasted_iota(jnp.int32, (TOK, LANES), 0) < 2 * QUART
    moved = labels + jnp.where(near, wrap[0].astype(F32), 0.0)
    scatter_rows(moved, lab_scratch, refs, 2 * D)
    values = take_field(tok, scratch)
    copies[0].wait()
    normed, _, _ = norm_parts(values, gain[...])
    copies[1].wait()
    proj = dot_nn(normed, wqkv[...]).astype(BF16)
    keep_ref[:, : 3 * D] = proj
    keep_ref[:, 4 * D : 5 * D] = normed
    keep_ref[:, 5 * D :] = labels.astype(BF16)
    attended, _ = attention(proj, label_bias(labels))
    keep_ref[:, 3 * D : 4 * D] = attended
    copies[2].wait()
    scatter_rows(values + dot_nn(attended, wout[...]), scratch, refs, 0)


def second_main(
    x0, x1, x2, x3, gain, wqkv, wout,
    b0, b1, b2, b3, normed_ref, att_ref, right_ref, scratch, lab_scratch,
):
    parts = (x0, x1, x2, x3)
    back = (b0, b1, b2, b3)
    values = gather_rows(parts, scratch, 0)
    g = gather_rows(parts, scratch, D)
    labels = gather_rows(parts, lab_scratch, 2 * D)
    g16 = g.astype(BF16)
    normed, xhat, rstd = norm_parts(values, gain[...])
    normed_ref[...] = normed
    proj = dot_nn(normed, wqkv[...]).astype(BF16)
    datt = dot_nt(g16, wout[...]).astype(BF16)
    attended, dproj = attention(proj, label_bias(labels), grad=datt)
    att_ref[...] = attended
    store_right(dproj, g16, right_ref)
    scatter_rows(values + dot_nn(attended, wout[...]), scratch, back, 0)
    dnormed = dot_nt(dproj, wqkv[...])
    scatter_rows(norm_back(dnormed, gain[...], xhat, rstd, g), scratch, back, D)


def second_pack(me, normed, attended, right, p0, p1, p2, p3, left_n, left_a):
    order = regroup(order_y)
    left_n[...] = dot_nn(normed[...], order).astype(BF16)
    left_a[...] = dot_nn(attended[...], order).astype(BF16)
    pack(me[0], (left_n, left_a), right, (p0, p1, p2, p3))


def first_backward(
    me, b0, b1, b2, b3, wout, keep, right_ref, p0, p1, p2, p3, scratch, left_n, left_a
):
    g16 = gather_rows((b0, b1, b2, b3), scratch, D).astype(BF16)
    datt = dot_nt(g16, wout[...]).astype(BF16)
    bias = label_bias(keep[:, 5 * D :].astype(F32))
    _, dproj = attention(keep[...], bias, grad=datt, attended=keep[:, 3 * D : 4 * D])
    store_right(dproj, g16, right_ref)
    order = regroup(order_x)
    left_n[...] = dot_nn(keep[:, 4 * D : 5 * D], order).astype(BF16)
    left_a[...] = dot_nn(keep[:, 3 * D : 4 * D], order).astype(BF16)
    pack(me[0], (left_n, left_a), right_ref, (p0, p1, p2, p3))


def first_rest(b0, b1, b2, b3, tok, gain, wqkv, right, tg_ref, result_ref, scratch):
    back = (b0, b1, b2, b3)
    put_field(gather_rows(back, scratch, 0), scratch, result_ref)
    _, xhat, rstd = norm_parts(take_field(tok, scratch), gain[...])
    g = gather_rows(back, scratch, D)
    dnormed = dot_nt(right[0], wqkv[:, :D])
    dnormed += dot_nt(right[1], wqkv[:, D : 2 * D])
    dnormed += dot_nt(right[2], wqkv[:, 2 * D :])
    put_field(norm_back(dnormed, gain[...], xhat, rstd, g), scratch, tg_ref)


def weights(me, p0, p1, p2, p3, q0, q1, q2, q3, scratch):
    total = jnp.zeros((D, WIDE), F32)
    for part in (p0, p1, p2, p3):
        total += dot_tn(part[:, :D], part[:, D:])
    scratch[...] = total
    for step, ref in enumerate((q0, q1, q2, q3)):
        first = pl.multiple_of((me[0] ^ step) * PLANE_ROWS, PLANE_ROWS)
        ref[...] = scratch[pl.ds(first, PLANE_ROWS), :].astype(BF16)


def add_rows(a0, a1, a2, a3, b0, b1, b2, b3, out_ref):
    for slot, parts in enumerate(((a0, a1, a2, a3), (b0, b1, b2, b3))):
        total = sum(part[...].astype(F32) for part in parts).astype(BF16)
        for z in range(Z):
            out_ref[z, slot * LAST_ROWS : (slot + 1) * LAST_ROWS, :] = total[
                z * LAST_ROWS : (z + 1) * LAST_ROWS
            ]


PIECE = OWN * WIDE // LANES


def to_owners(parts, send_ref, scratch):
    total = jnp.sum(parts[...].astype(F32), 0)
    rest = jnp.sum(total * total, keepdims=True)
    terms = []
    for _ in range(3):
        term = rest.astype(BF16).astype(F32)
        terms.append(term)
        rest = rest - term
    terms = jnp.concatenate([jnp.broadcast_to(term, (1, LANES)) for term in terms], 0)
    for x in range(X):
        for y in range(Y):
            for slot, row in ((0, x * OWN), (1, LAST_ROWS + y * OWN)):
                for c in range(WIDE // LANES):
                    first = slot * PIECE + c * OWN
                    scratch[x * Y + y, first : first + OWN, :] = total[
                        row : row + OWN, c * LANES : (c + 1) * LANES
                    ]
            scratch[x * Y + y, 2 * PIECE :, :] = jnp.zeros((16, LANES), F32)
            scratch[x * Y + y, 2 * PIECE : 2 * PIECE + 3, :] = terms
    send_ref[...] = scratch[...].astype(BF16)


def spread(got, tile_ref):
    terms = jnp.sum(got[:, 2 * PIECE :, :].astype(F32), 0)
    squares = jnp.sum(terms, 0, keepdims=True)
    tile_ref[...] = jnp.broadcast_to(squares[None], tile_ref.shape)


def clipped(where, got, tiles, qkv_a, out_a, qkv_b, out_b, scratch):
    scratch[...] = got[:, : 2 * PIECE, :].astype(F32)
    total = jnp.sum(tiles[...], 0)[:1, :1]
    factor = jnp.minimum(1.0, math.sqrt(8.0) * D / jnp.sqrt(total))
    x, y = where[0], where[1]
    for k in range(GROUP):
        for slot, source, refs in (
            (0, k * Y + y, (qkv_a, out_a)),
            (1, x * Y + k, (qkv_b, out_b)),
        ):
            ref, column = (refs[0], k * WIDE) if k < 3 else (refs[1], 0)
            for c in range(WIDE // LANES):
                first = slot * PIECE + c * OWN
                ref[:, column + c * LANES : column + (c + 1) * LANES] = (
                    scratch[source, first : first + OWN, :] * factor
                )


def shape_of(*dims, dtype=BF16):
    return jax.ShapeDtypeStruct(dims, dtype)


def call(kernel, outs, scratch, *args, scalar=False, far=0, vmem=VMEM_BYTES):
    whole = pl.BlockSpec(memory_space=pltpu.VMEM)
    specs = [whole] * (len(args) - far) + [pl.BlockSpec(memory_space=pl.ANY)] * far
    if scalar:
        specs[0] = pl.BlockSpec(memory_space=pltpu.SMEM)
    scratch = [pltpu.VMEM(s, F32) if isinstance(s, tuple) else s for s in scratch]
    return pl.pallas_call(
        kernel,
        out_shape=outs,
        in_specs=specs,
        out_specs=[whole] * len(outs),
        scratch_shapes=scratch,
        compiler_params=pltpu.CompilerParams(vmem_limit_bytes=vmem),
        name=kernel.__name__,
    )(*args)


def moves(lat_count, lon_count):
    tables = []
    for a in range(2):
        for b in range(2):
            table = []
            for i in range(lat_count):
                for j in range(lon_count):
                    ti = (i - (1 - a)) % lat_count
                    tj = (j - (1 - b)) % lon_count
                    table.append((i * lon_count + j, ti * lon_count + tj))
            tables.append(table)
    return tables


def send(parts, tables, back=False):
    out = []
    for part, table in zip(parts, tables):
        if all(s == t for s, t in table):
            out.append(part)
            continue
        pairs = [(t, s) for s, t in table] if back else table
        out.append(lax.ppermute(part, ("lat", "lon"), pairs))
    return out


def index_of(x, y, z):
    return (x * YLO + y % YLO) * LON + y // YLO * Z + z


CHIPS = [(x, y, z) for x in range(X) for y in range(Y) for z in range(Z)]
PLANE = [[index_of(x, y, z) for x in range(X) for y in range(Y)] for z in range(Z)]
COLUMN = [[index_of(x, y, z) for z in range(Z)] for x in range(X) for y in range(Y)]


def swap(packs, axis):
    out = [packs[0]]
    for step in range(1, GROUP):
        pairs = [
            (index_of(x, y, z), index_of(x ^ step, y, z) if axis == "x" else index_of(x, y ^ step, z))
            for x, y, z in CHIPS
        ]
        out.append(lax.ppermute(packs[step], ("lat", "lon"), pairs))
    return out


def exchange(parts, groups):
    return lax.all_to_all(parts, ("lat", "lon"), 0, 0, axis_index_groups=groups)


def after(value, earlier):
    return lax.optimization_barrier((value, earlier))[0]


def on_device(
    tokens,
    cotangent,
    region,
    unshifted_norm_gain,
    unshifted_query_key_value,
    out_first,
    shifted_norm_gain,
    shifted_query_key_value,
    out_second,
):
    tables = moves(LAT, LON)
    lat, lon = lax.axis_index("lat"), lax.axis_index("lon")
    at_x = (lat // YLO).astype(jnp.int32)
    at_y = (lon // Z * YLO + lat % YLO).astype(jnp.int32)
    me_x, me_y = at_x.reshape(1), at_y.reshape(1)
    wrap = jnp.where(lat == 0, 4, 0).astype(jnp.int32).reshape(1)
    gain_a = unshifted_norm_gain.reshape(1, D)
    gain_b = shifted_norm_gain.reshape(1, D)
    tok = tokens.transpose(1, 2, 0, 3)
    cot = cotangent.transpose(1, 2, 0, 3)
    lab = region.transpose(1, 0, 2)

    field = shape_of(TOK, D)
    fields = shape_of(GROUP, TOK, D)
    packs = [shape_of(TOK, D + WIDE)] * GROUP
    *x, keep = call(
        first_forward,
        [shape_of(QUART, SEND)] * 4 + [shape_of(TOK, 5 * D + LANES)],
        [
            (TOK, D),
            (TOK, LANES),
            (1, D),
            pltpu.VMEM((D, 3 * D), BF16),
            pltpu.VMEM((D, D), BF16),
            pltpu.SemaphoreType.DMA((3,)),
        ],
        wrap, lab, tok, cot, gain_a, unshifted_query_key_value, out_first,
        scalar=True, far=3, vmem=WHOLE_VMEM_BYTES,
    )
    x = send(x, tables)
    *back, normed_b, att_b, right_b = call(
        second_main,
        [shape_of(QUART, 2 * D)] * 4 + [field, field, fields],
        [(TOK, D), (TOK, LANES)],
        *x, gain_b, shifted_query_key_value, out_second,
    )
    back = send(back, tables, back=True)
    half = pltpu.VMEM((TOK, D), BF16)
    pack_b = call(
        second_pack, packs, [half, half], me_y, normed_b, att_b, right_b, scalar=True
    )
    pack_b = swap(after(pack_b, back[:3]), "y")
    right_a, *pack_a = call(
        first_backward,
        [fields] + packs,
        [(TOK, D), half, half],
        me_x, *back, out_first, keep,
        scalar=True,
    )
    pack_a = swap(pack_a, "x")
    grid = shape_of(WLAT, WLON, WLEV, D)
    token_gradient, result = call(
        first_rest,
        [grid, grid],
        [(TOK, D)],
        *back, tok, gain_a, unshifted_query_key_value, right_a,
    )
    token_gradient = token_gradient.transpose(2, 0, 1, 3)
    result = result.transpose(2, 0, 1, 3)

    rows = [shape_of(PLANE_ROWS, WIDE)] * GROUP
    sum_b = swap(call(weights, rows, [(D, WIDE)], me_x, *pack_b, scalar=True), "x")
    sum_a = swap(call(weights, rows, [(D, WIDE)], me_y, *pack_a, scalar=True), "y")
    (sums,) = call(add_rows, [shape_of(Z, 2 * LAST_ROWS, WIDE)], [], *sum_a, *sum_b)
    sums = exchange(sums, COLUMN)
    piece = (X * Y, 2 * PIECE + 16, LANES)
    (pieces,) = call(to_owners, [shape_of(*piece)], [piece], sums)
    pieces = exchange(pieces, PLANE)
    (tiles,) = call(spread, [shape_of(Z, 8, LANES, dtype=F32)], [], pieces)
    tiles = exchange(tiles, COLUMN)
    out_qkv, out_out = shape_of(OWN, 3 * D, dtype=F32), shape_of(OWN, D, dtype=F32)
    clips = call(
        clipped,
        [out_qkv, out_out] * 2,
        [(X * Y, 2 * PIECE, LANES)],
        jnp.concatenate([me_x, me_y]), pieces, tiles,
        scalar=True,
    )
    return (result, token_gradient, *clips)


def solution(mesh):
    field = P("rep", "lat", "lon", None)
    rows = P(("rep", "lat", "lon"), None)
    in_specs = (field, field, P("rep", "lat", "lon"), P(), P(), P(), P(), P(), P())
    return jax.shard_map(
        on_device,
        mesh=mesh,
        in_specs=in_specs,
        out_specs=(field, field, rows, rows, rows, rows),
        check_vma=False,
    )
```

```python
import math

import jax
import jax.numpy as jnp
from jax import lax
from jax.experimental import pallas as pl
from jax.experimental.pallas import tpu as pltpu
from jax.sharding import PartitionSpec as P

D = 512
HEADS = 8
HEAD = 64
PAIRS = HEADS // 2
WLEV = 2
WLAT = 6
WLON = 12
HLAT = WLAT // 2
HLON = WLON // 2
TOK = WLEV * WLAT * WLON
QUART = TOK // 4
LANES = 128

X, YLO, YHI, Z = 4, 2, 2, 8
Y = YHI * YLO
LAT, LON = X * YLO, YHI * Z
OWN = D // (LAT * LON)
GROUP = 4
LAST = 8
WIDE = 4 * D // GROUP
PLANE_ROWS = D // GROUP
LAST_ROWS = PLANE_ROWS // LAST
SEND = 2 * D + LANES

EPSILON = 1e-05
NEGATIVE = -1e30
F32 = jnp.float32
BF16 = jnp.bfloat16
VMEM_BYTES = 16 * 1024 * 1024


def dot_nn(a, b):
    return lax.dot_general(a, b, (((1,), (0,)), ((), ())), preferred_element_type=F32)


def dot_nt(a, b):
    return lax.dot_general(a, b, (((1,), (1,)), ((), ())), preferred_element_type=F32)


def dot_tn(a, b):
    return lax.dot_general(a, b, (((0,), (0,)), ((), ())), preferred_element_type=F32)


def norm_parts(values, gain):
    average = jnp.mean(values, -1, keepdims=True)
    centered = values - average
    rstd = lax.rsqrt(jnp.mean(centered * centered, -1, keepdims=True) + EPSILON)
    xhat = centered * rstd
    return (xhat * gain).astype(BF16), xhat, rstd


def norm_back(dnormed, gain, xhat, rstd, incoming):
    s = dnormed * gain
    return (
        rstd * (s - jnp.mean(s, -1, keepdims=True) - xhat * jnp.mean(s * xhat, -1, keepdims=True))
        + incoming
    )


def label_bias(labels):
    lane = lax.broadcasted_iota(jnp.int32, (TOK, LANES), 1).astype(F32)
    hot = jnp.where((lane == labels) & (lane > 0.5), 1.0, 0.0).astype(BF16)
    return (1.0 - dot_nt(hot, hot)) * NEGATIVE


def pair_of(fields, part, pair):
    start = part * D + pair * LANES
    return fields[:, start : start + LANES]


def softmax_rows(scores):
    shifted = jnp.exp(scores - jnp.max(scores, -1, keepdims=True))
    return shifted * (1.0 / jnp.sum(shifted, -1, keepdims=True))


def attention(proj, bias, grad=None, attended=None):
    lane = lax.broadcasted_iota(jnp.int32, (1, LANES), 1)
    is_low = lane < HEAD
    low = is_low.astype(F32)
    masks = (low.astype(BF16), (1.0 - low).astype(BF16))
    bias = jnp.concatenate([bias, bias], 0)

    def stacked(field):
        return jnp.concatenate([field * masks[0], field * masks[1]], 0)

    def merged(both):
        return jnp.where(is_low, both[:TOK], both[TOK:])

    att, dq, dk, dv = [], [], [], []
    for pair in range(PAIRS):
        q = stacked(pair_of(proj, 0, pair) * BF16(HEAD**-0.5))
        k = pair_of(proj, 1, pair)
        v = pair_of(proj, 2, pair)
        probs = softmax_rows(dot_nt(q, k) + bias)
        p16 = probs.astype(BF16)
        if attended is None:
            o = merged(dot_nn(p16, v)).astype(BF16)
            att.append(o)
        else:
            o = pair_of(attended, 0, pair)
        if grad is not None:
            g = pair_of(grad, 0, pair)
            g_both = stacked(g)
            product = g.astype(F32) * o.astype(F32)
            delta = jnp.concatenate(
                [
                    jnp.sum(product * low, -1, keepdims=True),
                    jnp.sum(product * (1.0 - low), -1, keepdims=True),
                ],
                0,
            )
            ds16 = (probs * (dot_nt(g_both, v) - delta)).astype(BF16)
            dq.append((merged(dot_nn(ds16, k)) * HEAD**-0.5).astype(BF16))
            dk.append(dot_tn(ds16, q).astype(BF16))
            dv.append(dot_tn(p16, g_both).astype(BF16))
    if attended is None:
        attended = jnp.concatenate(att, -1)
    dproj = jnp.concatenate(dq + dk + dv, -1) if grad is not None else None
    return attended, dproj


def take_field(ref, scratch):
    half = HLON * WLEV
    for row in range(WLAT):
        values = ref[row].astype(F32).reshape(2 * half, D)
        for b in range(2):
            first = (2 * (row // HLAT) + b) * QUART + row % HLAT * half
            scratch[first : first + half, :] = values[b * half : (b + 1) * half]
    return scratch[...]


def put_field(values, scratch, ref):
    scratch[...] = values
    half = HLON * WLEV
    for row in range(WLAT):
        for b in range(2):
            first = (2 * (row // HLAT) + b) * QUART + row % HLAT * half
            ref[row, b * HLON : (b + 1) * HLON] = (
                scratch[first : first + half, :].reshape(HLON, WLEV, D).astype(BF16)
            )


def take_labels(region):
    places = WLAT * WLEV
    table = region[...].reshape(places, WLON).astype(F32)
    token = lax.broadcasted_iota(jnp.int32, (TOK, places), 0)
    slot, rest = token // QUART, token % QUART
    row = slot // 2 * HLAT + rest // (HLON * WLEV)
    column = slot % 2 * HLON + rest % (HLON * WLEV) // WLEV
    place = lax.broadcasted_iota(jnp.int32, (TOK, places), 1)
    rows = dot_nn((place == row * WLEV + rest % WLEV).astype(F32), table)
    return jnp.sum(jnp.where(place == column, rows, 0.0), -1, keepdims=True)


def gather_rows(refs, scratch, column):
    wide = scratch.shape[1]
    for slot, ref in enumerate(refs):
        scratch[slot * QUART : (slot + 1) * QUART, :] = ref[:, column : column + wide].astype(F32)
    return scratch[...]


def scatter_rows(values, scratch, refs, column):
    scratch[...] = values
    wide = scratch.shape[1]
    for slot, ref in enumerate(refs):
        ref[:, column : column + wide] = scratch[slot * QUART : (slot + 1) * QUART, :].astype(BF16)


def regroup(source_of):
    to = lax.broadcasted_iota(jnp.int32, (1, D), 1)
    return (lax.broadcasted_iota(jnp.int32, (D, D), 0) == source_of(to)).astype(F32).astype(BF16)


def chip_of(lat, lon):
    return lat // YLO, lon // Z * YLO + lat % YLO, lon % Z


def members_first(x, y, z):
    return x % 2 + z % 2 * 2, y, x // 2 + z // 2 * 2


def members_second(x, y, z):
    s = (x + 3) % 4
    return s % 2 + y % 2 * 2, y // 2 + z % 2 * 2, s // 2 + z // 2 * 2


def chip_first(m1, m2, m3):
    return m1 % 2 + m3 % 2 * 2, m2, m1 // 2 + m3 // 2 * 2


def chip_second(m1, m2, m3):
    return (m1 % 2 + m3 % 2 * 2 + 1) % 4, m1 // 2 + m2 % 2 * 2, m2 // 2 + m3 // 2 * 2


def row_order(chip):
    def source_of(to):
        m1, m3, m2 = to // OWN % GROUP, to // (OWN * GROUP) % LAST, to // (OWN * GROUP * LAST)
        x, y, z = chip(m1, m2, m3)
        return (((x * YLO + y % YLO) * YHI + y // YLO) * Z + z) * OWN + to % OWN

    return source_of


def here(me):
    return chip_of(me[0], me[1])


def pack(me, left_refs, right_ref, packs):
    for step, ref in enumerate(packs):
        peer = me ^ step
        is_att = peer == GROUP - 1

        @pl.when(is_att)
        def _():
            ref[:, :D] = left_refs[1][...]

        @pl.when(jnp.logical_not(is_att))
        def _():
            ref[:, :D] = left_refs[0][...]

        ref[:, D:] = right_ref[peer]


def store_right(dproj, g16, right_ref):
    for part in range(3):
        right_ref[part] = dproj[:, part * D : (part + 1) * D]
    right_ref[3] = g16


def first_forward(
    me, region, tok, cot, gain_hbm, wqkv_hbm, wout_hbm,
    x0, x1, x2, x3, keep_ref, scratch, lab_scratch, gain, wqkv, wout, sems,
):
    copies = [
        pltpu.make_async_copy(source, target, sems.at[i])
        for i, (source, target) in enumerate(((gain_hbm, gain), (wqkv_hbm, wqkv), (wout_hbm, wout)))
    ]
    for copy in copies:
        copy.start()
    refs = (x0, x1, x2, x3)
    take_field(cot, scratch)
    for slot, ref in enumerate(refs):
        ref[:, D : 2 * D] = scratch[slot * QUART : (slot + 1) * QUART, :].astype(BF16)
    labels = jnp.broadcast_to(take_labels(region), (TOK, LANES))
    near = lax.broadcasted_iota(jnp.int32, (TOK, LANES), 0) < 2 * QUART
    moved = labels + jnp.where(near & (me[0] == 0), 4.0, 0.0)
    scatter_rows(moved, lab_scratch, refs, 2 * D)
    values = take_field(tok, scratch)
    copies[0].wait()
    normed, _, _ = norm_parts(values, gain[...])
    copies[1].wait()
    proj = dot_nn(normed, wqkv[...]).astype(BF16)
    keep_ref[:, : 3 * D] = proj
    keep_ref[:, 4 * D : 5 * D] = normed
    keep_ref[:, 5 * D :] = labels.astype(BF16)
    attended, _ = attention(proj, label_bias(labels))
    keep_ref[:, 3 * D : 4 * D] = attended
    copies[2].wait()
    scatter_rows(values + dot_nn(attended, wout[...]), scratch, refs, 0)


def second_main(
    x0, x1, x2, x3, gain, wqkv, wout,
    b0, b1, b2, b3, normed_ref, att_ref, right_ref, scratch, lab_scratch,
):
    parts = (x0, x1, x2, x3)
    back = (b0, b1, b2, b3)
    values = gather_rows(parts, scratch, 0)
    g = gather_rows(parts, scratch, D)
    labels = gather_rows(parts, lab_scratch, 2 * D)
    g16 = g.astype(BF16)
    normed, xhat, rstd = norm_parts(values, gain[...])
    normed_ref[...] = normed
    proj = dot_nn(normed, wqkv[...]).astype(BF16)
    datt = dot_nt(g16, wout[...]).astype(BF16)
    attended, dproj = attention(proj, label_bias(labels), grad=datt)
    att_ref[...] = attended
    store_right(dproj, g16, right_ref)
    scatter_rows(values + dot_nn(attended, wout[...]), scratch, back, 0)
    dnormed = dot_nt(dproj, wqkv[...])
    scatter_rows(norm_back(dnormed, gain[...], xhat, rstd, g), scratch, back, D)


def second_pack(me, normed, attended, right, p0, p1, p2, p3, left_n, left_a):
    order = regroup(row_order(chip_second))
    left_n[...] = dot_nn(normed[...], order).astype(BF16)
    left_a[...] = dot_nn(attended[...], order).astype(BF16)
    pack(members_second(*here(me))[0], (left_n, left_a), right, (p0, p1, p2, p3))


def first_backward(
    me, b0, b1, b2, b3, wout, keep, right_ref, p0, p1, p2, p3, scratch, left_n, left_a
):
    g16 = gather_rows((b0, b1, b2, b3), scratch, D).astype(BF16)
    datt = dot_nt(g16, wout[...]).astype(BF16)
    bias = label_bias(keep[:, 5 * D :].astype(F32))
    _, dproj = attention(keep[...], bias, grad=datt, attended=keep[:, 3 * D : 4 * D])
    store_right(dproj, g16, right_ref)
    order = regroup(row_order(chip_first))
    left_n[...] = dot_nn(keep[:, 4 * D : 5 * D], order).astype(BF16)
    left_a[...] = dot_nn(keep[:, 3 * D : 4 * D], order).astype(BF16)
    pack(members_first(*here(me))[0], (left_n, left_a), right_ref, (p0, p1, p2, p3))


def first_rest(b0, b1, b2, b3, tok, gain, wqkv, right, tg_ref, result_ref, scratch):
    back = (b0, b1, b2, b3)
    put_field(gather_rows(back, scratch, 0), scratch, result_ref)
    _, xhat, rstd = norm_parts(take_field(tok, scratch), gain[...])
    g = gather_rows(back, scratch, D)
    dnormed = dot_nt(right[0], wqkv[:, :D])
    dnormed += dot_nt(right[1], wqkv[:, D : 2 * D])
    dnormed += dot_nt(right[2], wqkv[:, 2 * D :])
    put_field(norm_back(dnormed, gain[...], xhat, rstd, g), scratch, tg_ref)


def weights(member, p0, p1, p2, p3, q0, q1, q2, q3, scratch):
    scratch[...] = sum(dot_tn(part[:, :D], part[:, D:]) for part in (p0, p1, p2, p3))
    for step, ref in enumerate((q0, q1, q2, q3)):
        first = pl.multiple_of((member ^ step) * PLANE_ROWS, PLANE_ROWS)
        ref[...] = scratch[pl.ds(first, PLANE_ROWS), :].astype(BF16)


def first_weights(me, *refs):
    weights(members_first(*here(me))[1], *refs)


def second_weights(me, *refs):
    weights(members_second(*here(me))[1], *refs)


def add_rows(me, a0, a1, a2, a3, b0, b1, b2, b3, out_ref, scratch):
    x, y, z = here(me)
    flip = members_first(x, y, z)[2] ^ members_second(x, y, z)[2]
    total = sum(part[...].astype(F32) for part in (a0, a1, a2, a3)).astype(BF16)
    scratch[...] = sum(part[...].astype(F32) for part in (b0, b1, b2, b3))
    for last in range(LAST):
        out_ref[last, :LAST_ROWS, :] = total[last * LAST_ROWS : (last + 1) * LAST_ROWS]
        first = pl.multiple_of((last ^ flip) * LAST_ROWS, LAST_ROWS)
        out_ref[last, LAST_ROWS:, :] = scratch[pl.ds(first, LAST_ROWS), :].astype(BF16)


PIECE = OWN * WIDE // LANES
NEAR = [(x, y, z) for z in range(2) for y in range(YLO) for x in range(X)]


def near_index(x, y, z):
    return x + y % YLO * X + z % 2 * X * YLO


def to_owners(parts, send_ref, scratch):
    total = jnp.sum(parts[...].astype(F32), 0)
    rest = jnp.sum(total * total, keepdims=True)
    terms = []
    for _ in range(3):
        term = rest.astype(BF16).astype(F32)
        terms.append(term)
        rest = rest - term
    terms = jnp.concatenate([jnp.broadcast_to(term, (1, LANES)) for term in terms], 0)
    for peer, chip in enumerate(NEAR):
        rows = (members_first(*chip)[0] * OWN, LAST_ROWS + members_second(*chip)[0] * OWN)
        for slot, row in enumerate(rows):
            for c in range(WIDE // LANES):
                first = slot * PIECE + c * OWN
                scratch[peer, first : first + OWN, :] = total[
                    row : row + OWN, c * LANES : (c + 1) * LANES
                ]
        scratch[peer, 2 * PIECE :, :] = jnp.zeros((16, LANES), F32)
        scratch[peer, 2 * PIECE : 2 * PIECE + 3, :] = terms
    send_ref[...] = scratch[...].astype(BF16)


def spread(got, tile_ref):
    terms = jnp.sum(got[:, 2 * PIECE :, :].astype(F32), 0)
    squares = jnp.sum(terms, 0, keepdims=True)
    tile_ref[...] = jnp.broadcast_to(squares[None], tile_ref.shape)


def clipped(me, got, tiles, qkv_a, out_a, qkv_b, out_b, scratch):
    scratch[...] = got[:, : 2 * PIECE, :].astype(F32)
    total = jnp.sum(tiles[...], 0)[:1, :1]
    factor = jnp.minimum(1.0, math.sqrt(8.0) * D / jnp.sqrt(total))
    chip = here(me)
    _, *first_rest_of = members_first(*chip)
    _, *second_rest_of = members_second(*chip)
    for k in range(GROUP):
        for slot, source, refs in (
            (0, near_index(*chip_first(k, *first_rest_of)), (qkv_a, out_a)),
            (1, near_index(*chip_second(k, *second_rest_of)), (qkv_b, out_b)),
        ):
            ref, column = (refs[0], k * WIDE) if k < 3 else (refs[1], 0)
            for c in range(WIDE // LANES):
                first = slot * PIECE + c * OWN
                ref[:, column + c * LANES : column + (c + 1) * LANES] = (
                    scratch[source, first : first + OWN, :] * factor
                )


def shape_of(*dims, dtype=BF16):
    return jax.ShapeDtypeStruct(dims, dtype)


def call(kernel, outs, scratch, *args, scalar=False, far=0):
    whole = pl.BlockSpec(memory_space=pltpu.VMEM)
    specs = [whole] * (len(args) - far) + [pl.BlockSpec(memory_space=pl.ANY)] * far
    if scalar:
        specs[0] = pl.BlockSpec(memory_space=pltpu.SMEM)
    scratch = [pltpu.VMEM(s, F32) if isinstance(s, tuple) else s for s in scratch]
    return pl.pallas_call(
        kernel,
        out_shape=outs,
        in_specs=specs,
        out_specs=[whole] * len(outs),
        scratch_shapes=scratch,
        compiler_params=pltpu.CompilerParams(vmem_limit_bytes=VMEM_BYTES),
        name=kernel.__name__,
    )(*args)


def in_hbm(*arrays):
    return [pltpu.with_memory_space_constraint(array, pltpu.HBM) for array in arrays]


def moves(lat_count, lon_count):
    tables = []
    for a in range(2):
        for b in range(2):
            table = []
            for i in range(lat_count):
                for j in range(lon_count):
                    ti = (i - (1 - a)) % lat_count
                    tj = (j - (1 - b)) % lon_count
                    table.append((i * lon_count + j, ti * lon_count + tj))
            tables.append(table)
    return tables


def send(parts, tables, back=False):
    out = []
    for part, table in zip(parts, tables):
        if all(s == t for s, t in table):
            out.append(part)
            continue
        pairs = [(t, s) for s, t in table] if back else table
        out.append(lax.ppermute(part, ("lat", "lon"), pairs))
    return out


def index_of(x, y, z):
    return (x * YLO + y % YLO) * LON + y // YLO * Z + z


CHIPS = [(x, y, z) for x in range(X) for y in range(Y) for z in range(Z)]


def groups_of(key, order):
    table = {}
    for chip in sorted(CHIPS, key=order):
        table.setdefault(key(*chip), []).append(index_of(*chip))
    return [table[k] for k in sorted(table)]


LAST_GROUPS = groups_of(
    lambda x, y, z: members_first(x, y, z)[:2], lambda chip: members_first(*chip)[2]
)
NEAR_GROUPS = groups_of(lambda x, y, z: (y // 2, z // 2), lambda chip: near_index(*chip))
FAR_GROUPS = groups_of(lambda x, y, z: near_index(x, y, z), lambda chip: chip)


def swap(parts, members, chip, level):
    out = [parts[0]]
    for step in range(1, GROUP):
        pairs = []
        for here_chip in CHIPS:
            numbers = list(members(*here_chip))
            numbers[level] ^= step
            pairs.append((index_of(*here_chip), index_of(*chip(*numbers))))
        out.append(lax.ppermute(parts[step], ("lat", "lon"), pairs))
    return out


def swap_first(parts, level):
    return swap(parts, members_first, chip_first, level)


def swap_second(parts, level):
    return swap(parts, members_second, chip_second, level)


def exchange(parts, groups):
    return lax.all_to_all(parts, ("lat", "lon"), 0, 0, axis_index_groups=groups)


def after(value, earlier):
    return lax.optimization_barrier((value, earlier))[0]


def on_device(
    tokens,
    cotangent,
    region,
    unshifted_norm_gain,
    unshifted_query_key_value,
    out_first,
    shifted_norm_gain,
    shifted_query_key_value,
    out_second,
):
    tables = moves(LAT, LON)
    lat, lon = lax.axis_index("lat"), lax.axis_index("lon")
    me = jnp.stack([lat, lon]).astype(jnp.int32)
    gain_a = unshifted_norm_gain.reshape(1, D)
    gain_b = shifted_norm_gain.reshape(1, D)
    tok = tokens.transpose(1, 2, 0, 3)
    cot = cotangent.transpose(1, 2, 0, 3)
    lab = region.transpose(1, 0, 2)

    field = shape_of(TOK, D)
    fields = shape_of(GROUP, TOK, D)
    packs = [shape_of(TOK, D + WIDE)] * GROUP
    *x, keep = call(
        first_forward,
        [shape_of(QUART, SEND)] * 4 + [shape_of(TOK, 5 * D + LANES)],
        [
            (TOK, D),
            (TOK, LANES),
            (1, D),
            pltpu.VMEM((D, 3 * D), BF16),
            pltpu.VMEM((D, D), BF16),
            pltpu.SemaphoreType.DMA((3,)),
        ],
        me, *in_hbm(lab, tok, cot, gain_a, unshifted_query_key_value, out_first),
        scalar=True, far=3,
    )
    x = send(x, tables)
    *back, normed_b, att_b, right_b = call(
        second_main,
        [shape_of(QUART, 2 * D)] * 4 + [field, field, fields],
        [(TOK, D), (TOK, LANES)],
        *x, gain_b, shifted_query_key_value, out_second,
    )
    back = send(back, tables, back=True)
    half = pltpu.VMEM((TOK, D), BF16)
    pack_b = call(
        second_pack, packs, [half, half], me, normed_b, att_b, right_b, scalar=True
    )
    pack_b = swap_second(after(pack_b, back[:3]), 0)
    right_a, *pack_a = call(
        first_backward,
        [fields] + packs,
        [(TOK, D), half, half],
        me, *back, out_first, keep,
        scalar=True,
    )
    pack_a = swap_first(pack_a, 0)
    grid = shape_of(WLAT, WLON, WLEV, D)
    token_gradient, result = call(
        first_rest,
        [grid, grid],
        [(TOK, D)],
        *back, tok, gain_a, unshifted_query_key_value, right_a,
    )
    token_gradient = token_gradient.transpose(2, 0, 1, 3)
    result = result.transpose(2, 0, 1, 3)

    rows = [shape_of(PLANE_ROWS, WIDE)] * GROUP
    sum_b = swap_second(call(second_weights, rows, [(D, WIDE)], me, *pack_b, scalar=True), 1)
    sum_a = swap_first(call(first_weights, rows, [(D, WIDE)], me, *pack_a, scalar=True), 1)
    (sums,) = call(
        add_rows,
        [shape_of(LAST, 2 * LAST_ROWS, WIDE)],
        [(PLANE_ROWS, WIDE)],
        me, *sum_a, *sum_b,
        scalar=True,
    )
    sums = exchange(sums, LAST_GROUPS)
    piece = (len(NEAR), 2 * PIECE + 16, LANES)
    (pieces,) = call(to_owners, [shape_of(*piece)], [piece], sums)
    pieces = exchange(pieces, NEAR_GROUPS)
    (tiles,) = call(spread, [shape_of(LAST, 8, LANES, dtype=F32)], [], pieces)
    tiles = exchange(tiles, FAR_GROUPS)
    out_qkv, out_out = shape_of(OWN, 3 * D, dtype=F32), shape_of(OWN, D, dtype=F32)
    clips = call(
        clipped,
        [out_qkv, out_out] * 2,
        [(len(NEAR), 2 * PIECE, LANES)],
        me, pieces, tiles,
        scalar=True,
    )
    return (result, token_gradient, *clips)


def solution(mesh):
    field = P("rep", "lat", "lon", None)
    rows = P(("rep", "lat", "lon"), None)
    in_specs = (field, field, P("rep", "lat", "lon"), P(), P(), P(), P(), P(), P())
    return jax.shard_map(
        on_device,
        mesh=mesh,
        in_specs=in_specs,
        out_specs=(field, field, rows, rows, rows, rows),
        check_vma=False,
    )
```

```python
import math

import jax
import jax.numpy as jnp
from jax import lax
from jax.experimental import pallas as pl
from jax.experimental.pallas import tpu as pltpu
from jax.sharding import PartitionSpec as P

D = 512
HEADS = 8
HEAD = 64
PAIRS = HEADS // 2
WLEV = 2
WLAT = 6
WLON = 12
HLAT = WLAT // 2
HLON = WLON // 2
TOK = WLEV * WLAT * WLON
QUART = TOK // 4
LANES = 128

X, YLO, YHI, Z = 4, 2, 2, 8
Y = YHI * YLO
LAT, LON = X * YLO, YHI * Z
OWN = D // (LAT * LON)
GROUP = 4
LAST = 8
WIDE = 4 * D // GROUP
PLANE_ROWS = D // GROUP
LAST_ROWS = PLANE_ROWS // LAST
SEND = 2 * D + LANES

EPSILON = 1e-05
NEGATIVE = -1e30
F32 = jnp.float32
BF16 = jnp.bfloat16
VMEM_BYTES = 16 * 1024 * 1024


def dot_nn(a, b):
    return lax.dot_general(a, b, (((1,), (0,)), ((), ())), preferred_element_type=F32)


def dot_nt(a, b):
    return lax.dot_general(a, b, (((1,), (1,)), ((), ())), preferred_element_type=F32)


def dot_tn(a, b):
    return lax.dot_general(a, b, (((0,), (0,)), ((), ())), preferred_element_type=F32)


def norm_parts(values, gain):
    average = jnp.mean(values, -1, keepdims=True)
    centered = values - average
    rstd = lax.rsqrt(jnp.mean(centered * centered, -1, keepdims=True) + EPSILON)
    xhat = centered * rstd
    return (xhat * gain).astype(BF16), xhat, rstd


def norm_back(dnormed, gain, xhat, rstd, incoming):
    s = dnormed * gain
    return (
        rstd * (s - jnp.mean(s, -1, keepdims=True) - xhat * jnp.mean(s * xhat, -1, keepdims=True))
        + incoming
    )


def label_bias(labels):
    lane = lax.broadcasted_iota(jnp.int32, (TOK, LANES), 1).astype(F32)
    hot = jnp.where((lane == labels) & (lane > 0.5), 1.0, 0.0).astype(BF16)
    return (1.0 - dot_nt(hot, hot)) * NEGATIVE


def pair_of(fields, part, pair):
    start = part * D + pair * LANES
    return fields[:, start : start + LANES]


def softmax_rows(scores):
    shifted = jnp.exp(scores - jnp.max(scores, -1, keepdims=True))
    return shifted * (1.0 / jnp.sum(shifted, -1, keepdims=True))


def attention(proj, bias, grad=None, attended=None):
    lane = lax.broadcasted_iota(jnp.int32, (1, LANES), 1)
    is_low = lane < HEAD
    low = is_low.astype(F32)
    masks = (low.astype(BF16), (1.0 - low).astype(BF16))
    bias = jnp.concatenate([bias, bias], 0)

    def stacked(field):
        return jnp.concatenate([field * masks[0], field * masks[1]], 0)

    def merged(both):
        return jnp.where(is_low, both[:TOK], both[TOK:])

    att, dq, dk, dv = [], [], [], []
    for pair in range(PAIRS):
        q = stacked(pair_of(proj, 0, pair) * BF16(HEAD**-0.5))
        k = pair_of(proj, 1, pair)
        v = pair_of(proj, 2, pair)
        probs = softmax_rows(dot_nt(q, k) + bias)
        p16 = probs.astype(BF16)
        if attended is None:
            o = merged(dot_nn(p16, v)).astype(BF16)
            att.append(o)
        else:
            o = pair_of(attended, 0, pair)
        if grad is not None:
            g = pair_of(grad, 0, pair)
            g_both = stacked(g)
            product = g.astype(F32) * o.astype(F32)
            delta = jnp.concatenate(
                [
                    jnp.sum(product * low, -1, keepdims=True),
                    jnp.sum(product * (1.0 - low), -1, keepdims=True),
                ],
                0,
            )
            ds16 = (probs * (dot_nt(g_both, v) - delta)).astype(BF16)
            dq.append((merged(dot_nn(ds16, k)) * HEAD**-0.5).astype(BF16))
            dk.append(dot_tn(ds16, q).astype(BF16))
            dv.append(dot_tn(p16, g_both).astype(BF16))
    if attended is None:
        attended = jnp.concatenate(att, -1)
    dproj = jnp.concatenate(dq + dk + dv, -1) if grad is not None else None
    return attended, dproj


def take_field(ref, scratch):
    half = HLON * WLEV
    for row in range(WLAT):
        values = ref[row].astype(F32).reshape(2 * half, D)
        for b in range(2):
            first = (2 * (row // HLAT) + b) * QUART + row % HLAT * half
            scratch[first : first + half, :] = values[b * half : (b + 1) * half]
    return scratch[...]


def put_field(values, scratch, ref):
    scratch[...] = values
    half = HLON * WLEV
    for row in range(WLAT):
        for b in range(2):
            first = (2 * (row // HLAT) + b) * QUART + row % HLAT * half
            ref[row, b * HLON : (b + 1) * HLON] = (
                scratch[first : first + half, :].reshape(HLON, WLEV, D).astype(BF16)
            )


def take_labels(region):
    places = WLAT * WLEV
    table = region[...].reshape(places, WLON).astype(F32)
    token = lax.broadcasted_iota(jnp.int32, (TOK, places), 0)
    slot, rest = token // QUART, token % QUART
    row = slot // 2 * HLAT + rest // (HLON * WLEV)
    column = slot % 2 * HLON + rest % (HLON * WLEV) // WLEV
    place = lax.broadcasted_iota(jnp.int32, (TOK, places), 1)
    rows = dot_nn((place == row * WLEV + rest % WLEV).astype(F32), table)
    return jnp.sum(jnp.where(place == column, rows, 0.0), -1, keepdims=True)


def gather_rows(refs, scratch, column):
    wide = scratch.shape[1]
    for slot, ref in enumerate(refs):
        scratch[slot * QUART : (slot + 1) * QUART, :] = ref[:, column : column + wide].astype(F32)
    return scratch[...]


def scatter_rows(values, scratch, refs, column):
    scratch[...] = values
    wide = scratch.shape[1]
    for slot, ref in enumerate(refs):
        ref[:, column : column + wide] = scratch[slot * QUART : (slot + 1) * QUART, :].astype(BF16)


def regroup(source_of):
    to = lax.broadcasted_iota(jnp.int32, (1, D), 1)
    return (lax.broadcasted_iota(jnp.int32, (D, D), 0) == source_of(to)).astype(F32).astype(BF16)


def chip_of(lat, lon):
    return lat // YLO, lon // Z * YLO + lat % YLO, lon % Z


def members_first(x, y, z):
    return x % 2 + z % 2 * 2, y, x // 2 + z // 2 * 2


def members_second(x, y, z):
    s, w = (x + X - 1) % X, (z + Z - 1) % Z
    return s % 2 + y % 2 * 2, y // 2 + w % 2 * 2, s // 2 + w // 2 * 2


def chip_first(m1, m2, m3):
    return m1 % 2 + m3 % 2 * 2, m2, m1 // 2 + m3 // 2 * 2


def chip_second(m1, m2, m3):
    s, w = m1 % 2 + m3 % 2 * 2, m2 // 2 + m3 // 2 * 2
    return (s + 1) % X, m1 // 2 + m2 % 2 * 2, (w + 1) % Z


def row_order(chip):
    def source_of(to):
        m1, m3, m2 = to // OWN % GROUP, to // (OWN * GROUP) % LAST, to // (OWN * GROUP * LAST)
        x, y, z = chip(m1, m2, m3)
        return (((x * YLO + y % YLO) * YHI + y // YLO) * Z + z) * OWN + to % OWN

    return source_of


def here(me):
    return chip_of(me[0], me[1])


def pack(me, left_refs, right_ref, packs):
    for step, ref in enumerate(packs):
        peer = me ^ step
        is_att = peer == GROUP - 1

        @pl.when(is_att)
        def _():
            ref[:, :D] = left_refs[1][...]

        @pl.when(jnp.logical_not(is_att))
        def _():
            ref[:, :D] = left_refs[0][...]

        ref[:, D:] = right_ref[peer]


def store_right(dproj, g16, right_ref):
    for part in range(3):
        right_ref[part] = dproj[:, part * D : (part + 1) * D]
    right_ref[3] = g16


def first_forward(
    me, region, tok, cot, gain_hbm, wqkv_hbm, wout_hbm,
    x0, x1, x2, x3, keep_ref, scratch, lab_scratch, gain, wqkv, wout, sems,
):
    copies = [
        pltpu.make_async_copy(source, target, sems.at[i])
        for i, (source, target) in enumerate(((gain_hbm, gain), (wqkv_hbm, wqkv), (wout_hbm, wout)))
    ]
    for copy in copies:
        copy.start()
    refs = (x0, x1, x2, x3)
    take_field(cot, scratch)
    for slot, ref in enumerate(refs):
        ref[:, D : 2 * D] = scratch[slot * QUART : (slot + 1) * QUART, :].astype(BF16)
    labels = jnp.broadcast_to(take_labels(region), (TOK, LANES))
    near = lax.broadcasted_iota(jnp.int32, (TOK, LANES), 0) < 2 * QUART
    moved = labels + jnp.where(near & (me[0] == 0), 4.0, 0.0)
    scatter_rows(moved, lab_scratch, refs, 2 * D)
    values = take_field(tok, scratch)
    copies[0].wait()
    normed, _, _ = norm_parts(values, gain[...])
    copies[1].wait()
    proj = dot_nn(normed, wqkv[...]).astype(BF16)
    keep_ref[:, : 3 * D] = proj
    keep_ref[:, 4 * D : 5 * D] = normed
    keep_ref[:, 5 * D :] = labels.astype(BF16)
    attended, _ = attention(proj, label_bias(labels))
    keep_ref[:, 3 * D : 4 * D] = attended
    copies[2].wait()
    scatter_rows(values + dot_nn(attended, wout[...]), scratch, refs, 0)


def second_main(
    x0, x1, x2, x3, gain, wqkv, wout,
    b0, b1, b2, b3, normed_ref, att_ref, right_ref, scratch, lab_scratch,
):
    parts = (x0, x1, x2, x3)
    back = (b0, b1, b2, b3)
    values = gather_rows(parts, scratch, 0)
    g = gather_rows(parts, scratch, D)
    labels = gather_rows(parts, lab_scratch, 2 * D)
    g16 = g.astype(BF16)
    normed, xhat, rstd = norm_parts(values, gain[...])
    normed_ref[...] = normed
    proj = dot_nn(normed, wqkv[...]).astype(BF16)
    datt = dot_nt(g16, wout[...]).astype(BF16)
    attended, dproj = attention(proj, label_bias(labels), grad=datt)
    att_ref[...] = attended
    store_right(dproj, g16, right_ref)
    scatter_rows(values + dot_nn(attended, wout[...]), scratch, back, 0)
    dnormed = dot_nt(dproj, wqkv[...])
    scatter_rows(norm_back(dnormed, gain[...], xhat, rstd, g), scratch, back, D)


def second_pack(me, normed, attended, right, p0, p1, p2, p3, left_n, left_a):
    order = regroup(row_order(chip_second))
    left_n[...] = dot_nn(normed[...], order).astype(BF16)
    left_a[...] = dot_nn(attended[...], order).astype(BF16)
    pack(members_second(*here(me))[0], (left_n, left_a), right, (p0, p1, p2, p3))


def first_backward(
    me, b0, b1, b2, b3, wout, keep, right_ref, p0, p1, p2, p3, scratch, left_n, left_a
):
    g16 = gather_rows((b0, b1, b2, b3), scratch, D).astype(BF16)
    datt = dot_nt(g16, wout[...]).astype(BF16)
    bias = label_bias(keep[:, 5 * D :].astype(F32))
    _, dproj = attention(keep[...], bias, grad=datt, attended=keep[:, 3 * D : 4 * D])
    store_right(dproj, g16, right_ref)
    order = regroup(row_order(chip_first))
    left_n[...] = dot_nn(keep[:, 4 * D : 5 * D], order).astype(BF16)
    left_a[...] = dot_nn(keep[:, 3 * D : 4 * D], order).astype(BF16)
    pack(members_first(*here(me))[0], (left_n, left_a), right_ref, (p0, p1, p2, p3))


def first_rest(b0, b1, b2, b3, tok, gain, wqkv, right, tg_ref, result_ref, scratch):
    back = (b0, b1, b2, b3)
    put_field(gather_rows(back, scratch, 0), scratch, result_ref)
    _, xhat, rstd = norm_parts(take_field(tok, scratch), gain[...])
    g = gather_rows(back, scratch, D)
    dnormed = dot_nt(right[0], wqkv[:, :D])
    dnormed += dot_nt(right[1], wqkv[:, D : 2 * D])
    dnormed += dot_nt(right[2], wqkv[:, 2 * D :])
    put_field(norm_back(dnormed, gain[...], xhat, rstd, g), scratch, tg_ref)


def weights(member, p0, p1, p2, p3, q0, q1, q2, q3, scratch):
    scratch[...] = sum(dot_tn(part[:, :D], part[:, D:]) for part in (p0, p1, p2, p3))
    for step, ref in enumerate((q0, q1, q2, q3)):
        first = pl.multiple_of((member ^ step) * PLANE_ROWS, PLANE_ROWS)
        ref[...] = scratch[pl.ds(first, PLANE_ROWS), :].astype(BF16)


def first_weights(me, *refs):
    weights(members_first(*here(me))[1], *refs)


def second_weights(me, *refs):
    weights(members_second(*here(me))[1], *refs)


def add_rows(me, a0, a1, a2, a3, b0, b1, b2, b3, out_ref, scratch):
    m1, m2, _ = members_first(*here(me))
    total = sum(part[...].astype(F32) for part in (a0, a1, a2, a3)).astype(BF16)
    scratch[...] = sum(part[...].astype(F32) for part in (b0, b1, b2, b3))
    for last in range(LAST):
        out_ref[last, :LAST_ROWS, :] = total[last * LAST_ROWS : (last + 1) * LAST_ROWS]
        place = members_second(*chip_first(m1, m2, last))[2]
        first = pl.multiple_of(place * LAST_ROWS, LAST_ROWS)
        out_ref[last, LAST_ROWS:, :] = scratch[pl.ds(first, LAST_ROWS), :].astype(BF16)


PIECE = OWN * WIDE // LANES
NEAR = [(x, y, z) for z in range(2) for y in range(YLO) for x in range(X)]


def near_index(x, y, z):
    return x + y % YLO * X + z % 2 * X * YLO


def to_owners(parts, send_ref, scratch):
    total = jnp.sum(parts[...].astype(F32), 0)
    rest = jnp.sum(total * total, keepdims=True)
    terms = []
    for _ in range(3):
        term = rest.astype(BF16).astype(F32)
        terms.append(term)
        rest = rest - term
    terms = jnp.concatenate([jnp.broadcast_to(term, (1, LANES)) for term in terms], 0)
    for peer, chip in enumerate(NEAR):
        rows = (members_first(*chip)[0] * OWN, LAST_ROWS + members_second(*chip)[0] * OWN)
        for slot, row in enumerate(rows):
            for c in range(WIDE // LANES):
                first = slot * PIECE + c * OWN
                scratch[peer, first : first + OWN, :] = total[
                    row : row + OWN, c * LANES : (c + 1) * LANES
                ]
        scratch[peer, 2 * PIECE :, :] = jnp.zeros((16, LANES), F32)
        scratch[peer, 2 * PIECE : 2 * PIECE + 3, :] = terms
    send_ref[...] = scratch[...].astype(BF16)


def spread(got, tile_ref):
    terms = jnp.sum(got[:, 2 * PIECE :, :].astype(F32), 0)
    squares = jnp.sum(terms, 0, keepdims=True)
    tile_ref[...] = jnp.broadcast_to(squares[None], tile_ref.shape)


def collect(me, got, rows_a, rows_b, scratch):
    scratch[...] = got[:, : 2 * PIECE, :].astype(F32)
    chip = here(me)
    _, *numbers_a = members_first(*chip)
    _, *numbers_b = members_second(*chip)
    for k in range(GROUP):
        for slot, source, ref in (
            (0, near_index(*chip_first(k, *numbers_a)), rows_a),
            (1, near_index(*chip_second(k, *numbers_b)), rows_b),
        ):
            for c in range(WIDE // LANES):
                first, column = slot * PIECE + c * OWN, k * WIDE + c * LANES
                ref[:, column : column + LANES] = scratch[source, first : first + OWN, :]


def clipped(tiles, rows_a, rows_b, qkv_a, out_a, qkv_b, out_b):
    total = jnp.sum(tiles[...], 0)[:1, :1]
    factor = jnp.minimum(1.0, math.sqrt(8.0) * D / jnp.sqrt(total))
    for rows, qkv, out in ((rows_a, qkv_a, out_a), (rows_b, qkv_b, out_b)):
        qkv[...] = rows[:, : 3 * D] * factor
        out[...] = rows[:, 3 * D :] * factor


def shape_of(*dims, dtype=BF16):
    return jax.ShapeDtypeStruct(dims, dtype)


def call(kernel, outs, scratch, *args, scalar=False, far=0):
    whole = pl.BlockSpec(memory_space=pltpu.VMEM)
    specs = [whole] * (len(args) - far) + [pl.BlockSpec(memory_space=pl.ANY)] * far
    if scalar:
        specs[0] = pl.BlockSpec(memory_space=pltpu.SMEM)
    scratch = [pltpu.VMEM(s, F32) if isinstance(s, tuple) else s for s in scratch]
    return pl.pallas_call(
        kernel,
        out_shape=outs,
        in_specs=specs,
        out_specs=[whole] * len(outs),
        scratch_shapes=scratch,
        compiler_params=pltpu.CompilerParams(vmem_limit_bytes=VMEM_BYTES),
        name=kernel.__name__,
    )(*args)


def in_vmem(*arrays):
    return [pltpu.with_memory_space_constraint(array, pltpu.VMEM) for array in arrays]


def in_hbm(*arrays):
    return [pltpu.with_memory_space_constraint(array, pltpu.HBM) for array in arrays]


def moves(lat_count, lon_count):
    tables = []
    for a in range(2):
        for b in range(2):
            table = []
            for i in range(lat_count):
                for j in range(lon_count):
                    ti = (i - (1 - a)) % lat_count
                    tj = (j - (1 - b)) % lon_count
                    table.append((i * lon_count + j, ti * lon_count + tj))
            tables.append(table)
    return tables


def send(parts, tables, back=False):
    out = []
    for part, table in zip(parts, tables):
        if all(s == t for s, t in table):
            out.append(part)
            continue
        pairs = [(t, s) for s, t in table] if back else table
        out.append(lax.ppermute(part, ("lat", "lon"), pairs))
    return out


def index_of(x, y, z):
    return (x * YLO + y % YLO) * LON + y // YLO * Z + z


CHIPS = [(x, y, z) for x in range(X) for y in range(Y) for z in range(Z)]


def groups_of(key, order):
    table = {}
    for chip in sorted(CHIPS, key=order):
        table.setdefault(key(*chip), []).append(index_of(*chip))
    return [table[k] for k in sorted(table)]


LAST_GROUPS = groups_of(
    lambda x, y, z: members_first(x, y, z)[:2], lambda chip: members_first(*chip)[2]
)
NEAR_GROUPS = groups_of(lambda x, y, z: (y // 2, z // 2), lambda chip: near_index(*chip))
FAR_GROUPS = groups_of(lambda x, y, z: near_index(x, y, z), lambda chip: chip)


def swap(parts, members, chip, level):
    out = list(parts)
    for step in (3, 1, 2):
        pairs = []
        for here_chip in CHIPS:
            numbers = list(members(*here_chip))
            numbers[level] ^= step
            pairs.append((index_of(*here_chip), index_of(*chip(*numbers))))
        out[step] = lax.ppermute(parts[step], ("lat", "lon"), pairs)
    return out


def swap_first(parts, level):
    return swap(parts, members_first, chip_first, level)


def swap_second(parts, level):
    return swap(parts, members_second, chip_second, level)


def exchange(parts, groups):
    return lax.all_to_all(parts, ("lat", "lon"), 0, 0, axis_index_groups=groups)


def after(value, earlier):
    return lax.optimization_barrier((value, earlier))[0]


def on_device(
    tokens,
    cotangent,
    region,
    unshifted_norm_gain,
    unshifted_query_key_value,
    out_first,
    shifted_norm_gain,
    shifted_query_key_value,
    out_second,
):
    tables = moves(LAT, LON)
    lat, lon = lax.axis_index("lat"), lax.axis_index("lon")
    me = jnp.stack([lat, lon]).astype(jnp.int32)
    gain_a = unshifted_norm_gain.reshape(1, D)
    gain_b = shifted_norm_gain.reshape(1, D)
    tok = tokens.transpose(1, 2, 0, 3)
    cot = cotangent.transpose(1, 2, 0, 3)
    lab = region.transpose(1, 0, 2)

    field = shape_of(TOK, D)
    fields = shape_of(GROUP, TOK, D)
    packs = [shape_of(TOK, D + WIDE)] * GROUP
    *x, keep = call(
        first_forward,
        [shape_of(QUART, SEND)] * 4 + [shape_of(TOK, 5 * D + LANES)],
        [
            (TOK, D),
            (TOK, LANES),
            (1, D),
            pltpu.VMEM((D, 3 * D), BF16),
            pltpu.VMEM((D, D), BF16),
            pltpu.SemaphoreType.DMA((3,)),
        ],
        me, *in_hbm(lab, tok, cot, gain_a, unshifted_query_key_value, out_first),
        scalar=True, far=3,
    )
    x = send(x, tables)
    *back, normed_b, att_b, right_b = call(
        second_main,
        [shape_of(QUART, 2 * D)] * 4 + [field, field, fields],
        [(TOK, D), (TOK, LANES)],
        *x, gain_b, shifted_query_key_value, out_second,
    )
    back = send(back, tables, back=True)
    half = pltpu.VMEM((TOK, D), BF16)
    pack_b = call(
        second_pack, packs, [half, half], me, normed_b, att_b, right_b, scalar=True
    )
    pack_b = swap_second(after(pack_b, back[:3]), 0)
    right_a, *pack_a = call(
        first_backward,
        [fields] + packs,
        [(TOK, D), half, half],
        me, *back, out_first, keep,
        scalar=True,
    )
    pack_a = swap_first(pack_a, 0)
    grid = shape_of(WLAT, WLON, WLEV, D)
    token_gradient, result = call(
        first_rest,
        [grid, grid],
        [(TOK, D)],
        *back, tok, gain_a, unshifted_query_key_value, right_a,
    )
    token_gradient = token_gradient.transpose(2, 0, 1, 3)
    result = result.transpose(2, 0, 1, 3)

    rows = [shape_of(PLANE_ROWS, WIDE)] * GROUP
    sum_b = swap_second(call(second_weights, rows, [(D, WIDE)], me, *in_vmem(*pack_b), scalar=True), 1)
    sum_a = swap_first(call(first_weights, rows, [(D, WIDE)], me, *in_vmem(*pack_a), scalar=True), 1)
    (sums,) = call(
        add_rows,
        [shape_of(LAST, 2 * LAST_ROWS, WIDE)],
        [(PLANE_ROWS, WIDE)],
        me, *sum_a, *sum_b,
        scalar=True,
    )
    sums = exchange(sums, LAST_GROUPS)
    piece = (len(NEAR), 2 * PIECE + 16, LANES)
    (pieces,) = call(to_owners, [shape_of(*piece)], [piece], sums)
    pieces = exchange(pieces, NEAR_GROUPS)
    (tiles,) = call(spread, [shape_of(LAST, 8, LANES, dtype=F32)], [], pieces)
    pieces = after(pieces, tiles)
    tiles = exchange(tiles, FAR_GROUPS)
    own = shape_of(OWN, 4 * D, dtype=F32)
    mine = call(collect, [own, own], [(len(NEAR), 2 * PIECE, LANES)], me, pieces, scalar=True)
    out_qkv, out_out = shape_of(OWN, 3 * D, dtype=F32), shape_of(OWN, D, dtype=F32)
    clips = call(clipped, [out_qkv, out_out] * 2, [], tiles, *mine)
    return (result, token_gradient, *clips)


def solution(mesh):
    field = P("rep", "lat", "lon", None)
    rows = P(("rep", "lat", "lon"), None)
    in_specs = (field, field, P("rep", "lat", "lon"), P(), P(), P(), P(), P(), P())
    return jax.shard_map(
        on_device,
        mesh=mesh,
        in_specs=in_specs,
        out_specs=(field, field, rows, rows, rows, rows),
        check_vma=False,
    )
```

```python
import math

import jax
import jax.numpy as jnp
from jax import lax
from jax.experimental import pallas as pl
from jax.experimental.pallas import tpu as pltpu
from jax.sharding import PartitionSpec as P

D = 512
HEADS = 8
HEAD = 64
PAIRS = HEADS // 2
WLEV = 2
WLAT = 6
WLON = 12
HLAT = WLAT // 2
HLON = WLON // 2
TOK = WLEV * WLAT * WLON
QUART = TOK // 4
LANES = 128

X, YLO, YHI, Z = 4, 2, 2, 8
Y = YHI * YLO
LAT, LON = X * YLO, YHI * Z
OWN = D // (LAT * LON)
GROUP = 4
LAST = 8
WIDE = 4 * D // GROUP
PLANE_ROWS = D // GROUP
LAST_ROWS = PLANE_ROWS // LAST
SEND = 2 * D + LANES

EPSILON = 1e-05
NEGATIVE = -1e30
F32 = jnp.float32
BF16 = jnp.bfloat16
VMEM_BYTES = 16 * 1024 * 1024


def dot_nn(a, b):
    return lax.dot_general(a, b, (((1,), (0,)), ((), ())), preferred_element_type=F32)


def dot_nt(a, b):
    return lax.dot_general(a, b, (((1,), (1,)), ((), ())), preferred_element_type=F32)


def dot_tn(a, b):
    return lax.dot_general(a, b, (((0,), (0,)), ((), ())), preferred_element_type=F32)


def norm_parts(values, gain):
    average = jnp.mean(values, -1, keepdims=True)
    centered = values - average
    rstd = lax.rsqrt(jnp.mean(centered * centered, -1, keepdims=True) + EPSILON)
    xhat = centered * rstd
    return (xhat * gain).astype(BF16), xhat, rstd


def norm_back(dnormed, gain, xhat, rstd, incoming):
    s = dnormed * gain
    return (
        rstd * (s - jnp.mean(s, -1, keepdims=True) - xhat * jnp.mean(s * xhat, -1, keepdims=True))
        + incoming
    )


def label_bias(labels):
    lane = lax.broadcasted_iota(jnp.int32, (TOK, LANES), 1).astype(F32)
    hot = jnp.where((lane == labels) & (lane > 0.5), 1.0, 0.0).astype(BF16)
    return (1.0 - dot_nt(hot, hot)) * NEGATIVE


def pair_of(fields, part, pair):
    start = part * D + pair * LANES
    return fields[:, start : start + LANES]


def softmax_rows(scores):
    shifted = jnp.exp(scores - jnp.max(scores, -1, keepdims=True))
    return shifted * (1.0 / jnp.sum(shifted, -1, keepdims=True))


def attention(proj, bias, grad=None, attended=None):
    lane = lax.broadcasted_iota(jnp.int32, (1, LANES), 1)
    is_low = lane < HEAD
    low = is_low.astype(F32)
    masks = (low.astype(BF16), (1.0 - low).astype(BF16))
    bias = jnp.concatenate([bias, bias], 0)

    def stacked(field):
        return jnp.concatenate([field * masks[0], field * masks[1]], 0)

    def merged(both):
        return jnp.where(is_low, both[:TOK], both[TOK:])

    att, dq, dk, dv = [], [], [], []
    for pair in range(PAIRS):
        q = stacked(pair_of(proj, 0, pair) * BF16(HEAD**-0.5))
        k = pair_of(proj, 1, pair)
        v = pair_of(proj, 2, pair)
        probs = softmax_rows(dot_nt(q, k) + bias)
        p16 = probs.astype(BF16)
        if attended is None:
            o = merged(dot_nn(p16, v)).astype(BF16)
            att.append(o)
        else:
            o = pair_of(attended, 0, pair)
        if grad is not None:
            g = pair_of(grad, 0, pair)
            g_both = stacked(g)
            product = g.astype(F32) * o.astype(F32)
            delta = jnp.concatenate(
                [
                    jnp.sum(product * low, -1, keepdims=True),
                    jnp.sum(product * (1.0 - low), -1, keepdims=True),
                ],
                0,
            )
            ds16 = (probs * (dot_nt(g_both, v) - delta)).astype(BF16)
            dq.append((merged(dot_nn(ds16, k)) * HEAD**-0.5).astype(BF16))
            dk.append(dot_tn(ds16, q).astype(BF16))
            dv.append(dot_tn(p16, g_both).astype(BF16))
    if attended is None:
        attended = jnp.concatenate(att, -1)
    dproj = jnp.concatenate(dq + dk + dv, -1) if grad is not None else None
    return attended, dproj


def take_field(ref, scratch):
    half = HLON * WLEV
    for row in range(WLAT):
        values = ref[row].astype(F32).reshape(2 * half, D)
        for b in range(2):
            first = (2 * (row // HLAT) + b) * QUART + row % HLAT * half
            scratch[first : first + half, :] = values[b * half : (b + 1) * half]
    return scratch[...]


def put_field(values, scratch, ref):
    scratch[...] = values
    half = HLON * WLEV
    for row in range(WLAT):
        for b in range(2):
            first = (2 * (row // HLAT) + b) * QUART + row % HLAT * half
            ref[row, b * HLON : (b + 1) * HLON] = (
                scratch[first : first + half, :].reshape(HLON, WLEV, D).astype(BF16)
            )


def take_labels(region):
    places = WLAT * WLEV
    table = region[...].reshape(places, WLON).astype(F32)
    token = lax.broadcasted_iota(jnp.int32, (TOK, places), 0)
    slot, rest = token // QUART, token % QUART
    row = slot // 2 * HLAT + rest // (HLON * WLEV)
    column = slot % 2 * HLON + rest % (HLON * WLEV) // WLEV
    place = lax.broadcasted_iota(jnp.int32, (TOK, places), 1)
    rows = dot_nn((place == row * WLEV + rest % WLEV).astype(F32), table)
    return jnp.sum(jnp.where(place == column, rows, 0.0), -1, keepdims=True)


def gather_rows(refs, scratch, column):
    wide = scratch.shape[1]
    for slot, ref in enumerate(refs):
        scratch[slot * QUART : (slot + 1) * QUART, :] = ref[:, column : column + wide].astype(F32)
    return scratch[...]


def scatter_rows(values, scratch, refs, column):
    scratch[...] = values
    wide = scratch.shape[1]
    for slot, ref in enumerate(refs):
        ref[:, column : column + wide] = scratch[slot * QUART : (slot + 1) * QUART, :].astype(BF16)


def regroup(source_of):
    to = lax.broadcasted_iota(jnp.int32, (1, D), 1)
    return (lax.broadcasted_iota(jnp.int32, (D, D), 0) == source_of(to)).astype(F32).astype(BF16)


def chip_of(lat, lon):
    return lat // YLO, lon // Z * YLO + lat % YLO, lon % Z


def squares(x, z):
    return x % 2 + z % 2 * 2, x // 2 + z // 2 * 2


def members_first(x, y, z):
    m1, m3 = squares(x, z)
    return m1, y, m3


def members_second(x, y, z):
    m1, m3 = squares((x + X - 1) % X, (z + Z - 1) % Z)
    return m1, y, m3


def chip_first(m1, m2, m3):
    return m1 % 2 + m3 % 2 * 2, m2, m1 // 2 + m3 // 2 * 2


def chip_second(m1, m2, m3):
    x, y, z = chip_first(m1, m2, m3)
    return (x + 1) % X, y, (z + 1) % Z


def row_order(chip):
    def source_of(to):
        m1, m3, m2 = to // OWN % GROUP, to // (OWN * GROUP) % LAST, to // (OWN * GROUP * LAST)
        x, y, z = chip(m1, m2, m3)
        return (((x * YLO + y % YLO) * YHI + y // YLO) * Z + z) * OWN + to % OWN

    return source_of


def here(me):
    return chip_of(me[0], me[1])


def pack(me, left_refs, right_ref, packs):
    for step, ref in enumerate(packs):
        peer = me ^ step
        is_att = peer == GROUP - 1

        @pl.when(is_att)
        def _():
            ref[:, :D] = left_refs[1][...]

        @pl.when(jnp.logical_not(is_att))
        def _():
            ref[:, :D] = left_refs[0][...]

        ref[:, D:] = right_ref[peer]


def store_right(dproj, g16, right_ref):
    for part in range(3):
        right_ref[part] = dproj[:, part * D : (part + 1) * D]
    right_ref[3] = g16


def first_forward(
    me, region, tok, cot, gain_hbm, wqkv_hbm, wout_hbm,
    x0, x1, x2, x3, keep_ref, scratch, lab_scratch, gain, wqkv, wout, sems,
):
    copies = [
        pltpu.make_async_copy(source, target, sems.at[i])
        for i, (source, target) in enumerate(((gain_hbm, gain), (wqkv_hbm, wqkv), (wout_hbm, wout)))
    ]
    for copy in copies:
        copy.start()
    refs = (x0, x1, x2, x3)
    take_field(cot, scratch)
    for slot, ref in enumerate(refs):
        ref[:, D : 2 * D] = scratch[slot * QUART : (slot + 1) * QUART, :].astype(BF16)
    labels = jnp.broadcast_to(take_labels(region), (TOK, LANES))
    near = lax.broadcasted_iota(jnp.int32, (TOK, LANES), 0) < 2 * QUART
    moved = labels + jnp.where(near & (me[0] == 0), 4.0, 0.0)
    scatter_rows(moved, lab_scratch, refs, 2 * D)
    values = take_field(tok, scratch)
    copies[0].wait()
    normed, _, _ = norm_parts(values, gain[...])
    copies[1].wait()
    proj = dot_nn(normed, wqkv[...]).astype(BF16)
    keep_ref[:, : 3 * D] = proj
    keep_ref[:, 4 * D : 5 * D] = normed
    keep_ref[:, 5 * D :] = labels.astype(BF16)
    attended, _ = attention(proj, label_bias(labels))
    keep_ref[:, 3 * D : 4 * D] = attended
    copies[2].wait()
    scatter_rows(values + dot_nn(attended, wout[...]), scratch, refs, 0)


def second_main(
    x0, x1, x2, x3, gain, wqkv, wout,
    b0, b1, b2, b3, normed_ref, att_ref, right_ref, scratch, lab_scratch,
):
    parts = (x0, x1, x2, x3)
    back = (b0, b1, b2, b3)
    values = gather_rows(parts, scratch, 0)
    g = gather_rows(parts, scratch, D)
    labels = gather_rows(parts, lab_scratch, 2 * D)
    g16 = g.astype(BF16)
    normed, xhat, rstd = norm_parts(values, gain[...])
    normed_ref[...] = normed
    proj = dot_nn(normed, wqkv[...]).astype(BF16)
    datt = dot_nt(g16, wout[...]).astype(BF16)
    attended, dproj = attention(proj, label_bias(labels), grad=datt)
    att_ref[...] = attended
    store_right(dproj, g16, right_ref)
    scatter_rows(values + dot_nn(attended, wout[...]), scratch, back, 0)
    dnormed = dot_nt(dproj, wqkv[...])
    scatter_rows(norm_back(dnormed, gain[...], xhat, rstd, g), scratch, back, D)


def second_pack(me, normed, attended, right, p0, p1, p2, p3, left_n, left_a):
    order = regroup(row_order(chip_second))
    left_n[...] = dot_nn(normed[...], order).astype(BF16)
    left_a[...] = dot_nn(attended[...], order).astype(BF16)
    pack(members_second(*here(me))[0], (left_n, left_a), right, (p0, p1, p2, p3))


def first_backward(
    me, b0, b1, b2, b3, wout, keep, right_ref, p0, p1, p2, p3, scratch, left_n, left_a
):
    g16 = gather_rows((b0, b1, b2, b3), scratch, D).astype(BF16)
    datt = dot_nt(g16, wout[...]).astype(BF16)
    bias = label_bias(keep[:, 5 * D :].astype(F32))
    _, dproj = attention(keep[...], bias, grad=datt, attended=keep[:, 3 * D : 4 * D])
    store_right(dproj, g16, right_ref)
    order = regroup(row_order(chip_first))
    left_n[...] = dot_nn(keep[:, 4 * D : 5 * D], order).astype(BF16)
    left_a[...] = dot_nn(keep[:, 3 * D : 4 * D], order).astype(BF16)
    pack(members_first(*here(me))[0], (left_n, left_a), right_ref, (p0, p1, p2, p3))


def first_rest(b0, b1, b2, b3, tok, gain, wqkv, right, tg_ref, result_ref, scratch):
    back = (b0, b1, b2, b3)
    put_field(gather_rows(back, scratch, 0), scratch, result_ref)
    _, xhat, rstd = norm_parts(take_field(tok, scratch), gain[...])
    g = gather_rows(back, scratch, D)
    dnormed = dot_nt(right[0], wqkv[:, :D])
    dnormed += dot_nt(right[1], wqkv[:, D : 2 * D])
    dnormed += dot_nt(right[2], wqkv[:, 2 * D :])
    put_field(norm_back(dnormed, gain[...], xhat, rstd, g), scratch, tg_ref)


def weights(member, p0, p1, p2, p3, q0, q1, q2, q3, scratch):
    total = jnp.zeros((D, WIDE), F32)
    for part in (p0, p1, p2, p3):
        total += dot_tn(part[:, :D], part[:, D:])
    scratch[...] = total
    for step, ref in enumerate((q0, q1, q2, q3)):
        first = pl.multiple_of((member ^ step) * PLANE_ROWS, PLANE_ROWS)
        ref[...] = scratch[pl.ds(first, PLANE_ROWS), :].astype(BF16)


def first_weights(me, *refs):
    weights(members_first(*here(me))[1], *refs)


def second_weights(me, *refs):
    weights(members_second(*here(me))[1], *refs)


PIECE = OWN * WIDE // LANES
SHEET = [(x, z) for x in range(X) for z in range(Z)]


def add_rows(a0, a1, a2, a3, b0, b1, b2, b3, out_ref, scratch):
    blocks = ((members_first, (a0, a1, a2, a3)), (members_second, (b0, b1, b2, b3)))
    for slot, (members, parts) in enumerate(blocks):
        total = sum(part[...].astype(F32) for part in parts)
        for peer, (x, z) in enumerate(SHEET):
            m1, _, m3 = members(x, 0, z)
            row = (m3 * GROUP + m1) * OWN
            for c in range(WIDE // LANES):
                first = slot * PIECE + c * OWN
                scratch[peer, first : first + OWN, :] = total[
                    row : row + OWN, c * LANES : (c + 1) * LANES
                ]
    out_ref[...] = scratch[...].astype(BF16)


def own_rows(parts, rows_ref, tile_ref):
    norm = jnp.zeros((1, 1), F32)
    for slot, members in enumerate((members_first, members_second)):
        totals = [jnp.zeros((PIECE, LANES), F32)] * GROUP
        for source, (x, z) in enumerate(SHEET):
            m1 = members(x, 0, z)[0]
            piece = parts[source, slot * PIECE : (slot + 1) * PIECE, :]
            totals[m1] = totals[m1] + piece.astype(F32)
        for m1, total in enumerate(totals):
            rows_ref[m1, slot * PIECE : (slot + 1) * PIECE, :] = total
        norm += jnp.sum(sum(total * total for total in totals), keepdims=True)
    tile_ref[...] = jnp.broadcast_to(norm[None], tile_ref.shape)


def clipped(tiles, rows, qkv_a, out_a, qkv_b, out_b):
    total = jnp.sum(tiles[...], 0)[:1, :1]
    factor = jnp.minimum(1.0, math.sqrt(8.0) * D / jnp.sqrt(total))
    for slot, refs in enumerate(((qkv_a, out_a), (qkv_b, out_b))):
        for k in range(GROUP):
            ref, column = (refs[0], k * WIDE) if k < GROUP - 1 else (refs[1], 0)
            for c in range(WIDE // LANES):
                first = slot * PIECE + c * OWN
                ref[:, column + c * LANES : column + (c + 1) * LANES] = (
                    rows[k, first : first + OWN, :] * factor
                )


def shape_of(*dims, dtype=BF16):
    return jax.ShapeDtypeStruct(dims, dtype)


def call(kernel, outs, scratch, *args, scalar=False, far=0):
    whole = pl.BlockSpec(memory_space=pltpu.VMEM)
    specs = [whole] * (len(args) - far) + [pl.BlockSpec(memory_space=pl.ANY)] * far
    if scalar:
        specs[0] = pl.BlockSpec(memory_space=pltpu.SMEM)
    scratch = [pltpu.VMEM(s, F32) if isinstance(s, tuple) else s for s in scratch]
    return pl.pallas_call(
        kernel,
        out_shape=outs,
        in_specs=specs,
        out_specs=[whole] * len(outs),
        scratch_shapes=scratch,
        compiler_params=pltpu.CompilerParams(vmem_limit_bytes=VMEM_BYTES),
        name=kernel.__name__,
    )(*args)


def in_vmem(*arrays):
    return [pltpu.with_memory_space_constraint(array, pltpu.VMEM) for array in arrays]


def in_hbm(*arrays):
    return [pltpu.with_memory_space_constraint(array, pltpu.HBM) for array in arrays]


def moves(lat_count, lon_count):
    tables = []
    for a in range(2):
        for b in range(2):
            table = []
            for i in range(lat_count):
                for j in range(lon_count):
                    ti = (i - (1 - a)) % lat_count
                    tj = (j - (1 - b)) % lon_count
                    table.append((i * lon_count + j, ti * lon_count + tj))
            tables.append(table)
    return tables


def send(parts, tables, back=False):
    out = []
    for part, table in zip(parts, tables):
        if all(s == t for s, t in table):
            out.append(part)
            continue
        pairs = [(t, s) for s, t in table] if back else table
        out.append(lax.ppermute(part, ("lat", "lon"), pairs))
    return out


def index_of(x, y, z):
    return (x * YLO + y % YLO) * LON + y // YLO * Z + z


CHIPS = [(x, y, z) for x in range(X) for y in range(Y) for z in range(Z)]


SHEETS = [[index_of(x, y, z) for x, z in SHEET] for y in range(Y)]


def swap(parts, members, chip, level):
    out = list(parts)
    for step in (3, 1, 2):
        pairs = []
        for here_chip in CHIPS:
            numbers = list(members(*here_chip))
            numbers[level] ^= step
            pairs.append((index_of(*here_chip), index_of(*chip(*numbers))))
        out[step] = lax.ppermute(parts[step], ("lat", "lon"), pairs)
    return out


def swap_first(parts, level):
    return swap(parts, members_first, chip_first, level)


def swap_second(parts, level):
    return swap(parts, members_second, chip_second, level)


def exchange(parts, groups):
    return lax.all_to_all(parts, ("lat", "lon"), 0, 0, axis_index_groups=groups)


def after(value, earlier):
    return lax.optimization_barrier((value, earlier))[0]


def on_device(
    tokens,
    cotangent,
    region,
    unshifted_norm_gain,
    unshifted_query_key_value,
    out_first,
    shifted_norm_gain,
    shifted_query_key_value,
    out_second,
):
    tables = moves(LAT, LON)
    lat, lon = lax.axis_index("lat"), lax.axis_index("lon")
    me = jnp.stack([lat, lon]).astype(jnp.int32)
    gain_a = unshifted_norm_gain.reshape(1, D)
    gain_b = shifted_norm_gain.reshape(1, D)
    tok = tokens.transpose(1, 2, 0, 3)
    cot = cotangent.transpose(1, 2, 0, 3)
    lab = region.transpose(1, 0, 2)

    field = shape_of(TOK, D)
    fields = shape_of(GROUP, TOK, D)
    packs = [shape_of(TOK, D + WIDE)] * GROUP
    *x, keep = call(
        first_forward,
        [shape_of(QUART, SEND)] * 4 + [shape_of(TOK, 5 * D + LANES)],
        [
            (TOK, D),
            (TOK, LANES),
            (1, D),
            pltpu.VMEM((D, 3 * D), BF16),
            pltpu.VMEM((D, D), BF16),
            pltpu.SemaphoreType.DMA((3,)),
        ],
        me, *in_hbm(lab, tok, cot, gain_a, unshifted_query_key_value, out_first),
        scalar=True, far=3,
    )
    x = send(x, tables)
    *back, normed_b, att_b, right_b = call(
        second_main,
        [shape_of(QUART, 2 * D)] * 4 + [field, field, fields],
        [(TOK, D), (TOK, LANES)],
        *x, gain_b, shifted_query_key_value, out_second,
    )
    back = send(back, tables, back=True)
    half = pltpu.VMEM((TOK, D), BF16)
    pack_b = call(
        second_pack, packs, [half, half], me, normed_b, att_b, right_b, scalar=True
    )
    pack_b = swap_second(after(pack_b, back[:3]), 0)
    right_a, *pack_a = call(
        first_backward,
        [fields] + packs,
        [(TOK, D), half, half],
        me, *back, out_first, keep,
        scalar=True,
    )
    pack_a = swap_first(pack_a, 0)
    grid = shape_of(WLAT, WLON, WLEV, D)
    token_gradient, result = call(
        first_rest,
        [grid, grid],
        [(TOK, D)],
        *back, tok, gain_a, unshifted_query_key_value, right_a,
    )
    token_gradient = token_gradient.transpose(2, 0, 1, 3)
    result = result.transpose(2, 0, 1, 3)

    rows = [shape_of(PLANE_ROWS, WIDE)] * GROUP
    sum_b = swap_second(call(second_weights, rows, [(D, WIDE)], me, *in_vmem(*pack_b), scalar=True), 1)
    sum_a = swap_first(call(first_weights, rows, [(D, WIDE)], me, *in_vmem(*pack_a), scalar=True), 1)
    piece = (len(SHEET), 2 * PIECE, LANES)
    (sums,) = call(add_rows, [shape_of(*piece)], [piece], *sum_a, *sum_b)
    sums = exchange(sums, SHEETS)
    mine, tiles = call(
        own_rows,
        [shape_of(GROUP, 2 * PIECE, LANES, dtype=F32), shape_of(LAT * LON, 1, LANES, dtype=F32)],
        [],
        sums,
    )
    tiles = lax.all_to_all(tiles, ("lat", "lon"), 0, 0)
    out_qkv, out_out = shape_of(OWN, 3 * D, dtype=F32), shape_of(OWN, D, dtype=F32)
    clips = call(clipped, [out_qkv, out_out] * 2, [], tiles, mine)
    return (result, token_gradient, *clips)


def solution(mesh):
    field = P("rep", "lat", "lon", None)
    rows = P(("rep", "lat", "lon"), None)
    in_specs = (field, field, P("rep", "lat", "lon"), P(), P(), P(), P(), P(), P())
    return jax.shard_map(
        on_device,
        mesh=mesh,
        in_specs=in_specs,
        out_specs=(field, field, rows, rows, rows, rows),
        check_vma=False,
    )
```

```python
import math

import jax
import jax.numpy as jnp
from jax import lax
from jax.experimental import pallas as pl
from jax.experimental.pallas import tpu as pltpu
from jax.sharding import PartitionSpec as P

D = 512
HEADS = 8
HEAD = 64
PAIRS = HEADS // 2
WLEV = 2
WLAT = 6
WLON = 12
HLAT = WLAT // 2
HLON = WLON // 2
TOK = WLEV * WLAT * WLON
QUART = TOK // 4
LANES = 128

X, YLO, YHI, Z = 4, 2, 2, 8
Y = YHI * YLO
LAT, LON = X * YLO, YHI * Z
OWN = D // (LAT * LON)
GROUP = 4
LAST = 8
WIDE = 4 * D // GROUP
PLANE_ROWS = D // GROUP
LAST_ROWS = PLANE_ROWS // LAST
SEND = 2 * D + LANES

EPSILON = 1e-05
NEGATIVE = -1e30
F32 = jnp.float32
BF16 = jnp.bfloat16
VMEM_BYTES = 16 * 1024 * 1024


def dot_nn(a, b):
    return lax.dot_general(a, b, (((1,), (0,)), ((), ())), preferred_element_type=F32)


def dot_nt(a, b):
    return lax.dot_general(a, b, (((1,), (1,)), ((), ())), preferred_element_type=F32)


def dot_tn(a, b):
    return lax.dot_general(a, b, (((0,), (0,)), ((), ())), preferred_element_type=F32)


def norm_parts(values, gain):
    average = jnp.mean(values, -1, keepdims=True)
    centered = values - average
    rstd = lax.rsqrt(jnp.mean(centered * centered, -1, keepdims=True) + EPSILON)
    xhat = centered * rstd
    return (xhat * gain).astype(BF16), xhat, rstd


def norm_back(dnormed, gain, xhat, rstd, incoming):
    s = dnormed * gain
    return (
        rstd * (s - jnp.mean(s, -1, keepdims=True) - xhat * jnp.mean(s * xhat, -1, keepdims=True))
        + incoming
    )


def label_bias(labels):
    lane = lax.broadcasted_iota(jnp.int32, (TOK, LANES), 1).astype(F32)
    hot = jnp.where((lane == labels) & (lane > 0.5), 1.0, 0.0).astype(BF16)
    return (1.0 - dot_nt(hot, hot)) * NEGATIVE


def pair_of(fields, part, pair):
    start = part * D + pair * LANES
    return fields[:, start : start + LANES]


def softmax_rows(scores):
    shifted = jnp.exp(scores - jnp.max(scores, -1, keepdims=True))
    return shifted * (1.0 / jnp.sum(shifted, -1, keepdims=True))


def attention(proj, bias, grad=None, attended=None):
    lane = lax.broadcasted_iota(jnp.int32, (1, LANES), 1)
    is_low = lane < HEAD
    low = is_low.astype(F32)
    masks = (low.astype(BF16), (1.0 - low).astype(BF16))
    bias = jnp.concatenate([bias, bias], 0)

    def stacked(field):
        return jnp.concatenate([field * masks[0], field * masks[1]], 0)

    def merged(both):
        return jnp.where(is_low, both[:TOK], both[TOK:])

    att, dq, dk, dv = [], [], [], []
    for pair in range(PAIRS):
        q = stacked(pair_of(proj, 0, pair) * BF16(HEAD**-0.5))
        k = pair_of(proj, 1, pair)
        v = pair_of(proj, 2, pair)
        probs = softmax_rows(dot_nt(q, k) + bias)
        p16 = probs.astype(BF16)
        if attended is None:
            o = merged(dot_nn(p16, v)).astype(BF16)
            att.append(o)
        else:
            o = pair_of(attended, 0, pair)
        if grad is not None:
            g = pair_of(grad, 0, pair)
            g_both = stacked(g)
            product = g.astype(F32) * o.astype(F32)
            delta = jnp.concatenate(
                [
                    jnp.sum(product * low, -1, keepdims=True),
                    jnp.sum(product * (1.0 - low), -1, keepdims=True),
                ],
                0,
            )
            ds16 = (probs * (dot_nt(g_both, v) - delta)).astype(BF16)
            dq.append((merged(dot_nn(ds16, k)) * HEAD**-0.5).astype(BF16))
            dk.append(dot_tn(ds16, q).astype(BF16))
            dv.append(dot_tn(p16, g_both).astype(BF16))
    if attended is None:
        attended = jnp.concatenate(att, -1)
    dproj = jnp.concatenate(dq + dk + dv, -1) if grad is not None else None
    return attended, dproj


def take_field(ref, scratch):
    half = HLON * WLEV
    for row in range(WLAT):
        values = ref[row].astype(F32).reshape(2 * half, D)
        for b in range(2):
            first = (2 * (row // HLAT) + b) * QUART + row % HLAT * half
            scratch[first : first + half, :] = values[b * half : (b + 1) * half]
    return scratch[...]


def put_field(values, scratch, ref):
    scratch[...] = values
    half = HLON * WLEV
    for row in range(WLAT):
        for b in range(2):
            first = (2 * (row // HLAT) + b) * QUART + row % HLAT * half
            ref[row, b * HLON : (b + 1) * HLON] = (
                scratch[first : first + half, :].reshape(HLON, WLEV, D).astype(BF16)
            )


def take_labels(region):
    places = WLAT * WLEV
    table = region[...].reshape(places, WLON).astype(F32)
    token = lax.broadcasted_iota(jnp.int32, (TOK, places), 0)
    slot, rest = token // QUART, token % QUART
    row = slot // 2 * HLAT + rest // (HLON * WLEV)
    column = slot % 2 * HLON + rest % (HLON * WLEV) // WLEV
    place = lax.broadcasted_iota(jnp.int32, (TOK, places), 1)
    rows = dot_nn((place == row * WLEV + rest % WLEV).astype(F32), table)
    return jnp.sum(jnp.where(place == column, rows, 0.0), -1, keepdims=True)


def gather_rows(refs, scratch, column):
    wide = scratch.shape[1]
    for slot, ref in enumerate(refs):
        scratch[slot * QUART : (slot + 1) * QUART, :] = ref[:, column : column + wide].astype(F32)
    return scratch[...]


def scatter_rows(values, scratch, refs, column):
    scratch[...] = values
    wide = scratch.shape[1]
    for slot, ref in enumerate(refs):
        ref[:, column : column + wide] = scratch[slot * QUART : (slot + 1) * QUART, :].astype(BF16)


def regroup(source_of):
    to = lax.broadcasted_iota(jnp.int32, (1, D), 1)
    return (lax.broadcasted_iota(jnp.int32, (D, D), 0) == source_of(to)).astype(F32).astype(BF16)


def squares(x, z):
    return (x & 1) + (z & 1) * 2, (x >> 1) + (z >> 1) * 2


def members_first(x, y, z):
    m1, m3 = squares(x, z)
    return m1, y, m3


def members_second(x, y, z):
    m1, m3 = squares(x + X - 1 & X - 1, z + Z - 1 & Z - 1)
    return m1, y, m3


def chip_first(m1, m2, m3):
    return (m1 & 1) + (m3 & 1) * 2, m2, (m1 >> 1) + (m3 >> 1) * 2


def chip_second(m1, m2, m3):
    x, y, z = chip_first(m1, m2, m3)
    return x + 1 & X - 1, y, z + 1 & Z - 1


def row_order(chip):
    def source_of(to):
        m1, m3, m2 = to // OWN % GROUP, to // (OWN * GROUP) % LAST, to // (OWN * GROUP * LAST)
        x, y, z = chip(m1, m2, m3)
        return (((x * YLO + y % YLO) * YHI + y // YLO) * Z + z) * OWN + to % OWN

    return source_of


def here(me):
    place = me[0]
    return place >> 5, (place >> 3 & 1) * 2 + (place >> 4 & 1), place & 7


def pack(me, left_refs, right_ref, packs):
    for step, ref in enumerate(packs):
        peer = me ^ step
        is_att = peer == GROUP - 1

        @pl.when(is_att)
        def _():
            ref[:, :D] = left_refs[1][...]

        @pl.when(jnp.logical_not(is_att))
        def _():
            ref[:, :D] = left_refs[0][...]

        ref[:, D:] = right_ref[peer]


def store_right(dproj, g16, right_ref):
    for part in range(3):
        right_ref[part] = dproj[:, part * D : (part + 1) * D]
    right_ref[3] = g16


def first_forward(
    me, region, tok, cot, gain_hbm, wqkv_hbm, wout_hbm,
    x0, x1, x2, x3, keep_ref, scratch, lab_scratch, gain, wqkv, wout, sems,
):
    copies = [
        pltpu.make_async_copy(source, target, sems.at[i])
        for i, (source, target) in enumerate(((gain_hbm, gain), (wqkv_hbm, wqkv), (wout_hbm, wout)))
    ]
    for copy in copies:
        copy.start()
    refs = (x0, x1, x2, x3)
    take_field(cot, scratch)
    for slot, ref in enumerate(refs):
        ref[:, D : 2 * D] = scratch[slot * QUART : (slot + 1) * QUART, :].astype(BF16)
    labels = jnp.broadcast_to(take_labels(region), (TOK, LANES))
    near = lax.broadcasted_iota(jnp.int32, (TOK, LANES), 0) < 2 * QUART
    moved = labels + jnp.where(near & (me[0] < LON), 4.0, 0.0)
    scatter_rows(moved, lab_scratch, refs, 2 * D)
    values = take_field(tok, scratch)
    copies[0].wait()
    normed, _, _ = norm_parts(values, gain[...])
    copies[1].wait()
    proj = dot_nn(normed, wqkv[...]).astype(BF16)
    keep_ref[:, : 3 * D] = proj
    keep_ref[:, 4 * D : 5 * D] = normed
    keep_ref[:, 5 * D :] = labels.astype(BF16)
    attended, _ = attention(proj, label_bias(labels))
    keep_ref[:, 3 * D : 4 * D] = attended
    copies[2].wait()
    scatter_rows(values + dot_nn(attended, wout[...]), scratch, refs, 0)


def second_main(
    x0, x1, x2, x3, gain, wqkv, wout,
    b0, b1, b2, b3, normed_ref, att_ref, right_ref, scratch, lab_scratch,
):
    parts = (x0, x1, x2, x3)
    back = (b0, b1, b2, b3)
    values = gather_rows(parts, scratch, 0)
    g = gather_rows(parts, scratch, D)
    labels = gather_rows(parts, lab_scratch, 2 * D)
    g16 = g.astype(BF16)
    normed, xhat, rstd = norm_parts(values, gain[...])
    normed_ref[...] = normed
    proj = dot_nn(normed, wqkv[...]).astype(BF16)
    datt = dot_nt(g16, wout[...]).astype(BF16)
    attended, dproj = attention(proj, label_bias(labels), grad=datt)
    att_ref[...] = attended
    store_right(dproj, g16, right_ref)
    scatter_rows(values + dot_nn(attended, wout[...]), scratch, back, 0)
    dnormed = dot_nt(dproj, wqkv[...])
    scatter_rows(norm_back(dnormed, gain[...], xhat, rstd, g), scratch, back, D)


def second_pack(me, normed, attended, right, p0, p1, p2, p3, left_n, left_a):
    order = regroup(row_order(chip_second))
    left_n[...] = dot_nn(normed[...], order).astype(BF16)
    left_a[...] = dot_nn(attended[...], order).astype(BF16)
    pack(members_second(*here(me))[0], (left_n, left_a), right, (p0, p1, p2, p3))


def first_backward(
    me, b0, b1, b2, b3, wout, keep, right_ref, p0, p1, p2, p3, scratch, left_n, left_a
):
    g16 = gather_rows((b0, b1, b2, b3), scratch, D).astype(BF16)
    datt = dot_nt(g16, wout[...]).astype(BF16)
    bias = label_bias(keep[:, 5 * D :].astype(F32))
    _, dproj = attention(keep[...], bias, grad=datt, attended=keep[:, 3 * D : 4 * D])
    store_right(dproj, g16, right_ref)
    order = regroup(row_order(chip_first))
    left_n[...] = dot_nn(keep[:, 4 * D : 5 * D], order).astype(BF16)
    left_a[...] = dot_nn(keep[:, 3 * D : 4 * D], order).astype(BF16)
    pack(members_first(*here(me))[0], (left_n, left_a), right_ref, (p0, p1, p2, p3))


def first_rest(b0, b1, b2, b3, tok, gain, wqkv, right, tg_ref, result_ref, scratch):
    back = (b0, b1, b2, b3)
    put_field(gather_rows(back, scratch, 0), scratch, result_ref)
    _, xhat, rstd = norm_parts(take_field(tok, scratch), gain[...])
    g = gather_rows(back, scratch, D)
    dnormed = dot_nt(right[0], wqkv[:, :D])
    dnormed += dot_nt(right[1], wqkv[:, D : 2 * D])
    dnormed += dot_nt(right[2], wqkv[:, 2 * D :])
    put_field(norm_back(dnormed, gain[...], xhat, rstd, g), scratch, tg_ref)


def weights(member, p0, p1, p2, p3, q0, q1, q2, q3, scratch):
    total = jnp.zeros((D, WIDE), F32)
    for part in (p0, p1, p2, p3):
        total += dot_tn(part[:, :D], part[:, D:])
    scratch[...] = total
    for step, ref in enumerate((q0, q1, q2, q3)):
        first = pl.multiple_of((member ^ step) * PLANE_ROWS, PLANE_ROWS)
        ref[...] = scratch[pl.ds(first, PLANE_ROWS), :].astype(BF16)


def first_weights(me, *refs):
    weights(members_first(*here(me))[1], *refs)


def second_weights(me, *refs):
    weights(members_second(*here(me))[1], *refs)


PIECE = OWN * WIDE // LANES
SHEET = [(x, z) for x in range(X) for z in range(Z)]


def add_rows(a0, a1, a2, a3, b0, b1, b2, b3, out_ref, scratch):
    blocks = ((members_first, (a0, a1, a2, a3)), (members_second, (b0, b1, b2, b3)))
    for slot, (members, parts) in enumerate(blocks):
        total = sum(part[...].astype(F32) for part in parts)
        for peer, (x, z) in enumerate(SHEET):
            m1, _, m3 = members(x, 0, z)
            row = (m3 * GROUP + m1) * OWN
            for c in range(WIDE // LANES):
                first = slot * PIECE + c * OWN
                scratch[peer, first : first + OWN, :] = total[
                    row : row + OWN, c * LANES : (c + 1) * LANES
                ]
    out_ref[...] = scratch[...].astype(BF16)


def own_rows(parts, rows_ref, tile_ref):
    norm = jnp.zeros((1, 1), F32)
    for slot, members in enumerate((members_first, members_second)):
        totals = [jnp.zeros((PIECE, LANES), F32)] * GROUP
        for source, (x, z) in enumerate(SHEET):
            m1 = members(x, 0, z)[0]
            piece = parts[source, slot * PIECE : (slot + 1) * PIECE, :]
            totals[m1] = totals[m1] + piece.astype(F32)
        for m1, total in enumerate(totals):
            rows_ref[m1, slot * PIECE : (slot + 1) * PIECE, :] = total
        norm += jnp.sum(sum(total * total for total in totals), keepdims=True)
    tile_ref[...] = jnp.broadcast_to(norm[None], tile_ref.shape)


def clipped(tiles, rows, qkv_a, out_a, qkv_b, out_b):
    total = jnp.sum(tiles[...], 0)[:1, :1]
    factor = jnp.minimum(1.0, math.sqrt(8.0) * D / jnp.sqrt(total))
    for slot, refs in enumerate(((qkv_a, out_a), (qkv_b, out_b))):
        for k in range(GROUP):
            ref, column = (refs[0], k * WIDE) if k < GROUP - 1 else (refs[1], 0)
            for c in range(WIDE // LANES):
                first = slot * PIECE + c * OWN
                ref[:, column + c * LANES : column + (c + 1) * LANES] = (
                    rows[k, first : first + OWN, :] * factor
                )


def shape_of(*dims, dtype=BF16):
    return jax.ShapeDtypeStruct(dims, dtype)


def call(kernel, outs, scratch, *args, scalar=False, far=0):
    whole = pl.BlockSpec(memory_space=pltpu.VMEM)
    specs = [whole] * (len(args) - far) + [pl.BlockSpec(memory_space=pl.ANY)] * far
    if scalar:
        specs[0] = pl.BlockSpec(memory_space=pltpu.SMEM)
    scratch = [pltpu.VMEM(s, F32) if isinstance(s, tuple) else s for s in scratch]
    return pl.pallas_call(
        kernel,
        out_shape=outs,
        in_specs=specs,
        out_specs=[whole] * len(outs),
        scratch_shapes=scratch,
        compiler_params=pltpu.CompilerParams(vmem_limit_bytes=VMEM_BYTES),
        name=kernel.__name__,
    )(*args)


def in_vmem(*arrays):
    return [pltpu.with_memory_space_constraint(array, pltpu.VMEM) for array in arrays]


def in_hbm(*arrays):
    return [pltpu.with_memory_space_constraint(array, pltpu.HBM) for array in arrays]


def moves(lat_count, lon_count):
    tables = []
    for a in range(2):
        for b in range(2):
            table = []
            for i in range(lat_count):
                for j in range(lon_count):
                    ti = (i - (1 - a)) % lat_count
                    tj = (j - (1 - b)) % lon_count
                    table.append((i * lon_count + j, ti * lon_count + tj))
            tables.append(table)
    return tables


def send(parts, tables, back=False):
    out = []
    for part, table in zip(parts, tables):
        if all(s == t for s, t in table):
            out.append(part)
            continue
        pairs = [(t, s) for s, t in table] if back else table
        out.append(lax.ppermute(part, ("lat", "lon"), pairs))
    return out


def index_of(x, y, z):
    return (x * YLO + y % YLO) * LON + y // YLO * Z + z


CHIPS = [(x, y, z) for x in range(X) for y in range(Y) for z in range(Z)]


SHEETS = [[index_of(x, y, z) for x, z in SHEET] for y in range(Y)]


def swap(parts, members, chip, level):
    out = list(parts)
    for step in (3, 1, 2):
        pairs = []
        for here_chip in CHIPS:
            numbers = list(members(*here_chip))
            numbers[level] ^= step
            pairs.append((index_of(*here_chip), index_of(*chip(*numbers))))
        out[step] = lax.ppermute(parts[step], ("lat", "lon"), pairs)
    return out


def swap_first(parts, level):
    return swap(parts, members_first, chip_first, level)


def swap_second(parts, level):
    return swap(parts, members_second, chip_second, level)


def exchange(parts, groups):
    return lax.all_to_all(parts, ("lat", "lon"), 0, 0, axis_index_groups=groups)


def after(value, earlier):
    return lax.optimization_barrier((value, earlier))[0]


def on_device(
    tokens,
    cotangent,
    region,
    unshifted_norm_gain,
    unshifted_query_key_value,
    out_first,
    shifted_norm_gain,
    shifted_query_key_value,
    out_second,
):
    tables = moves(LAT, LON)
    lat, lon = lax.axis_index("lat"), lax.axis_index("lon")
    me = (lat * LON + lon).astype(jnp.int32).reshape(1)
    gain_a = unshifted_norm_gain.reshape(1, D)
    gain_b = shifted_norm_gain.reshape(1, D)
    tok = tokens.transpose(1, 2, 0, 3)
    cot = cotangent.transpose(1, 2, 0, 3)
    lab = region.transpose(1, 0, 2)

    field = shape_of(TOK, D)
    fields = shape_of(GROUP, TOK, D)
    packs = [shape_of(TOK, D + WIDE)] * GROUP
    *x, keep = call(
        first_forward,
        [shape_of(QUART, SEND)] * 4 + [shape_of(TOK, 5 * D + LANES)],
        [
            (TOK, D),
            (TOK, LANES),
            (1, D),
            pltpu.VMEM((D, 3 * D), BF16),
            pltpu.VMEM((D, D), BF16),
            pltpu.SemaphoreType.DMA((3,)),
        ],
        me, *in_hbm(lab, tok, cot, gain_a, unshifted_query_key_value, out_first),
        scalar=True, far=3,
    )
    x = send(x, tables)
    *back, normed_b, att_b, right_b = call(
        second_main,
        [shape_of(QUART, 2 * D)] * 4 + [field, field, fields],
        [(TOK, D), (TOK, LANES)],
        *x, gain_b, shifted_query_key_value, out_second,
    )
    back = send(back, tables, back=True)
    half = pltpu.VMEM((TOK, D), BF16)
    pack_b = call(
        second_pack, packs, [half, half], me, normed_b, att_b, right_b, scalar=True
    )
    pack_b = swap_second(after(pack_b, back[:3]), 0)
    right_a, *pack_a = call(
        first_backward,
        [fields] + packs,
        [(TOK, D), half, half],
        me, *back, out_first, keep,
        scalar=True,
    )
    pack_a = swap_first(pack_a, 0)
    grid = shape_of(WLAT, WLON, WLEV, D)
    token_gradient, result = call(
        first_rest,
        [grid, grid],
        [(TOK, D)],
        *back, tok, gain_a, unshifted_query_key_value, right_a,
    )
    token_gradient = token_gradient.transpose(2, 0, 1, 3)
    result = result.transpose(2, 0, 1, 3)

    rows = [shape_of(PLANE_ROWS, WIDE)] * GROUP
    sum_b = swap_second(call(second_weights, rows, [(D, WIDE)], me, *in_vmem(*pack_b), scalar=True), 1)
    sum_a = swap_first(call(first_weights, rows, [(D, WIDE)], me, *in_vmem(*pack_a), scalar=True), 1)
    piece = (len(SHEET), 2 * PIECE, LANES)
    (sums,) = call(add_rows, [shape_of(*piece)], [piece], *sum_a, *sum_b)
    sums = exchange(sums, SHEETS)
    mine, tiles = call(
        own_rows,
        [shape_of(GROUP, 2 * PIECE, LANES, dtype=F32), shape_of(LAT * LON, 1, LANES, dtype=F32)],
        [],
        sums,
    )
    tiles = lax.all_to_all(tiles, ("lat", "lon"), 0, 0)
    out_qkv, out_out = shape_of(OWN, 3 * D, dtype=F32), shape_of(OWN, D, dtype=F32)
    clips = call(clipped, [out_qkv, out_out] * 2, [], tiles, mine)
    return (result, token_gradient, *clips)


def solution(mesh):
    field = P("rep", "lat", "lon", None)
    rows = P(("rep", "lat", "lon"), None)
    in_specs = (field, field, P("rep", "lat", "lon"), P(), P(), P(), P(), P(), P())
    return jax.shard_map(
        on_device,
        mesh=mesh,
        in_specs=in_specs,
        out_specs=(field, field, rows, rows, rows, rows),
        check_vma=False,
    )
```

```python
import math

import jax
import jax.numpy as jnp
from jax import lax
from jax.experimental import pallas as pl
from jax.experimental.pallas import tpu as pltpu
from jax.sharding import PartitionSpec as P

D = 512
HEADS = 8
HEAD = 64
PAIRS = HEADS // 2
WLEV = 2
WLAT = 6
WLON = 12
HLAT = WLAT // 2
HLON = WLON // 2
TOK = WLEV * WLAT * WLON
QUART = TOK // 4
LANES = 128

X, YLO, YHI, Z = 4, 2, 2, 8
Y = YHI * YLO
LAT, LON = X * YLO, YHI * Z
OWN = D // (LAT * LON)
GROUP = 4
LAST = 8
WIDE = 4 * D // GROUP
PLANE_ROWS = D // GROUP
LAST_ROWS = PLANE_ROWS // LAST
SEND = 2 * D + LANES

EPSILON = 1e-05
NEGATIVE = -1e30
F32 = jnp.float32
BF16 = jnp.bfloat16
VMEM_BYTES = 16 * 1024 * 1024


def dot_nn(a, b):
    return lax.dot_general(a, b, (((1,), (0,)), ((), ())), preferred_element_type=F32)


def dot_nt(a, b):
    return lax.dot_general(a, b, (((1,), (1,)), ((), ())), preferred_element_type=F32)


def dot_tn(a, b):
    return lax.dot_general(a, b, (((0,), (0,)), ((), ())), preferred_element_type=F32)


def norm_parts(values, gain):
    average = jnp.mean(values, -1, keepdims=True)
    centered = values - average
    rstd = lax.rsqrt(jnp.mean(centered * centered, -1, keepdims=True) + EPSILON)
    xhat = centered * rstd
    return (xhat * gain).astype(BF16), xhat, rstd


def norm_back(dnormed, gain, xhat, rstd, incoming):
    s = dnormed * gain
    return (
        rstd * (s - jnp.mean(s, -1, keepdims=True) - xhat * jnp.mean(s * xhat, -1, keepdims=True))
        + incoming
    )


def label_bias(labels):
    lane = lax.broadcasted_iota(jnp.int32, (TOK, LANES), 1).astype(F32)
    hot = jnp.where((lane == labels) & (lane > 0.5), 1.0, 0.0).astype(BF16)
    return (1.0 - dot_nt(hot, hot)) * NEGATIVE


def pair_of(fields, part, pair):
    start = part * D + pair * LANES
    return fields[:, start : start + LANES]


def softmax_rows(scores):
    shifted = jnp.exp(scores - jnp.max(scores, -1, keepdims=True))
    return shifted * (1.0 / jnp.sum(shifted, -1, keepdims=True))


def attention(proj, bias, grad=None, attended=None):
    lane = lax.broadcasted_iota(jnp.int32, (1, LANES), 1)
    is_low = lane < HEAD
    low = is_low.astype(F32)
    masks = (low.astype(BF16), (1.0 - low).astype(BF16))
    bias = jnp.concatenate([bias, bias], 0)

    def stacked(field):
        return jnp.concatenate([field * masks[0], field * masks[1]], 0)

    def merged(both):
        return jnp.where(is_low, both[:TOK], both[TOK:])

    att, dq, dk, dv = [], [], [], []
    for pair in range(PAIRS):
        q = stacked(pair_of(proj, 0, pair) * BF16(HEAD**-0.5))
        k = pair_of(proj, 1, pair)
        v = pair_of(proj, 2, pair)
        probs = softmax_rows(dot_nt(q, k) + bias)
        p16 = probs.astype(BF16)
        if attended is None:
            o = merged(dot_nn(p16, v)).astype(BF16)
            att.append(o)
        else:
            o = pair_of(attended, 0, pair)
        if grad is not None:
            g = pair_of(grad, 0, pair)
            g_both = stacked(g)
            product = g.astype(F32) * o.astype(F32)
            delta = jnp.concatenate(
                [
                    jnp.sum(product * low, -1, keepdims=True),
                    jnp.sum(product * (1.0 - low), -1, keepdims=True),
                ],
                0,
            )
            ds16 = (probs * (dot_nt(g_both, v) - delta)).astype(BF16)
            dq.append((merged(dot_nn(ds16, k)) * HEAD**-0.5).astype(BF16))
            dk.append(dot_tn(ds16, q).astype(BF16))
            dv.append(dot_tn(p16, g_both).astype(BF16))
    if attended is None:
        attended = jnp.concatenate(att, -1)
    dproj = jnp.concatenate(dq + dk + dv, -1) if grad is not None else None
    return attended, dproj


def take_field(ref, scratch):
    half = HLON * WLEV
    for row in range(WLAT):
        values = ref[row].astype(F32).reshape(2 * half, D)
        for b in range(2):
            first = (2 * (row // HLAT) + b) * QUART + row % HLAT * half
            scratch[first : first + half, :] = values[b * half : (b + 1) * half]
    return scratch[...]


def put_field(values, scratch, ref):
    scratch[...] = values
    half = HLON * WLEV
    for row in range(WLAT):
        for b in range(2):
            first = (2 * (row // HLAT) + b) * QUART + row % HLAT * half
            ref[row, b * HLON : (b + 1) * HLON] = (
                scratch[first : first + half, :].reshape(HLON, WLEV, D).astype(BF16)
            )


def take_labels(region):
    places = WLAT * WLEV
    table = region[...].reshape(places, WLON).astype(F32)
    token = lax.broadcasted_iota(jnp.int32, (TOK, places), 0)
    slot, rest = token // QUART, token % QUART
    row = slot // 2 * HLAT + rest // (HLON * WLEV)
    column = slot % 2 * HLON + rest % (HLON * WLEV) // WLEV
    place = lax.broadcasted_iota(jnp.int32, (TOK, places), 1)
    rows = dot_nn((place == row * WLEV + rest % WLEV).astype(F32), table)
    return jnp.sum(jnp.where(place == column, rows, 0.0), -1, keepdims=True)


def gather_rows(refs, scratch, column):
    wide = scratch.shape[1]
    for slot, ref in enumerate(refs):
        scratch[slot * QUART : (slot + 1) * QUART, :] = ref[:, column : column + wide].astype(F32)
    return scratch[...]


def scatter_rows(values, scratch, refs, column):
    scratch[...] = values
    wide = scratch.shape[1]
    for slot, ref in enumerate(refs):
        ref[:, column : column + wide] = scratch[slot * QUART : (slot + 1) * QUART, :].astype(BF16)


def regroup(source_of):
    to = lax.broadcasted_iota(jnp.int32, (1, D), 1)
    return (lax.broadcasted_iota(jnp.int32, (D, D), 0) == source_of(to)).astype(F32).astype(BF16)


def squares(x, z):
    return (x & 1) + (z & 1) * 2, (x >> 1) + (z >> 1) * 2


def members_first(x, y, z):
    m1, m3 = squares(x, z)
    return m1, y, m3


def members_second(x, y, z):
    m1, m3 = squares(x + X - 1 & X - 1, z + Z - 1 & Z - 1)
    return m1, y, m3


def chip_first(m1, m2, m3):
    return (m1 & 1) + (m3 & 1) * 2, m2, (m1 >> 1) + (m3 >> 1) * 2


def chip_second(m1, m2, m3):
    x, y, z = chip_first(m1, m2, m3)
    return x + 1 & X - 1, y, z + 1 & Z - 1


def row_order(chip):
    def source_of(to):
        m1, m3, m2 = to // OWN % GROUP, to // (OWN * GROUP) % LAST, to // (OWN * GROUP * LAST)
        x, y, z = chip(m1, m2, m3)
        return (((x * YLO + y % YLO) * YHI + y // YLO) * Z + z) * OWN + to % OWN

    return source_of


def here(me):
    place = me[0]
    return place >> 5, (place >> 3 & 1) * 2 + (place >> 4 & 1), place & 7


def pack(me, left_refs, right_ref, packs):
    for step, ref in enumerate(packs):
        peer = me ^ step
        is_att = peer == GROUP - 1

        @pl.when(is_att)
        def _():
            ref[:, :D] = left_refs[1][...]

        @pl.when(jnp.logical_not(is_att))
        def _():
            ref[:, :D] = left_refs[0][...]

        ref[:, D:] = right_ref[peer]


def store_right(dproj, g16, right_ref):
    for part in range(3):
        right_ref[part] = dproj[:, part * D : (part + 1) * D]
    right_ref[3] = g16


def first_forward(
    me, tok_hbm, gain_hbm, region_hbm, cot_hbm, wqkv_hbm, wout_hbm,
    x0, x1, x2, x3, keep_ref, scratch, lab_scratch, tok, gain, region, cot, wqkv, wout, sems,
):
    far = (tok_hbm, gain_hbm, region_hbm, cot_hbm, wqkv_hbm, wout_hbm)
    copies = [
        pltpu.make_async_copy(source, target, sems.at[i])
        for i, (source, target) in enumerate(zip(far, (tok, gain, region, cot, wqkv, wout)))
    ]
    for copy in copies:
        copy.start()
    refs = (x0, x1, x2, x3)
    copies[0].wait()
    values = take_field(tok, scratch)
    copies[1].wait()
    normed, _, _ = norm_parts(values, gain[...])
    copies[2].wait()
    labels = jnp.broadcast_to(take_labels(region), (TOK, LANES))
    near = lax.broadcasted_iota(jnp.int32, (TOK, LANES), 0) < 2 * QUART
    moved = labels + jnp.where(near & (me[0] < LON), 4.0, 0.0)
    scatter_rows(moved, lab_scratch, refs, 2 * D)
    copies[3].wait()
    take_field(cot, scratch)
    for slot, ref in enumerate(refs):
        ref[:, D : 2 * D] = scratch[slot * QUART : (slot + 1) * QUART, :].astype(BF16)
    copies[4].wait()
    proj = dot_nn(normed, wqkv[...]).astype(BF16)
    keep_ref[:, : 3 * D] = proj
    keep_ref[:, 4 * D : 5 * D] = normed
    keep_ref[:, 5 * D :] = labels.astype(BF16)
    attended, _ = attention(proj, label_bias(labels))
    keep_ref[:, 3 * D : 4 * D] = attended
    copies[5].wait()
    scatter_rows(values + dot_nn(attended, wout[...]), scratch, refs, 0)


def second_main(
    x0, x1, x2, x3, gain, wqkv, wout,
    b0, b1, b2, b3, normed_ref, att_ref, right_ref, scratch, lab_scratch,
):
    parts = (x0, x1, x2, x3)
    back = (b0, b1, b2, b3)
    values = gather_rows(parts, scratch, 0)
    g = gather_rows(parts, scratch, D)
    labels = gather_rows(parts, lab_scratch, 2 * D)
    g16 = g.astype(BF16)
    normed, xhat, rstd = norm_parts(values, gain[...])
    normed_ref[...] = normed
    proj = dot_nn(normed, wqkv[...]).astype(BF16)
    datt = dot_nt(g16, wout[...]).astype(BF16)
    attended, dproj = attention(proj, label_bias(labels), grad=datt)
    att_ref[...] = attended
    store_right(dproj, g16, right_ref)
    dnormed = dot_nt(dproj, wqkv[...])
    scatter_rows(norm_back(dnormed, gain[...], xhat, rstd, g), scratch, back, 0)


def second_pack(
    me, normed, attended, right, x0, x1, x2, x3, wout,
    p0, p1, p2, p3, r0, r1, r2, r3, left_n, left_a, scratch,
):
    order = regroup(row_order(chip_second))
    left_n[...] = dot_nn(normed[...], order).astype(BF16)
    left_a[...] = dot_nn(attended[...], order).astype(BF16)
    pack(members_second(*here(me))[0], (left_n, left_a), right, (p0, p1, p2, p3))
    values = gather_rows((x0, x1, x2, x3), scratch, 0)
    scatter_rows(values + dot_nn(attended[...], wout[...]), scratch, (r0, r1, r2, r3), 0)


def first_backward(
    me, b0, b1, b2, b3, wout, keep, right_ref, p0, p1, p2, p3, scratch, left_n, left_a
):
    g16 = gather_rows((b0, b1, b2, b3), scratch, 0).astype(BF16)
    datt = dot_nt(g16, wout[...]).astype(BF16)
    bias = label_bias(keep[:, 5 * D :].astype(F32))
    _, dproj = attention(keep[...], bias, grad=datt, attended=keep[:, 3 * D : 4 * D])
    store_right(dproj, g16, right_ref)
    order = regroup(row_order(chip_first))
    left_n[...] = dot_nn(keep[:, 4 * D : 5 * D], order).astype(BF16)
    left_a[...] = dot_nn(keep[:, 3 * D : 4 * D], order).astype(BF16)
    pack(members_first(*here(me))[0], (left_n, left_a), right_ref, (p0, p1, p2, p3))


def place(r0, r1, r2, r3, result_ref, scratch):
    put_field(gather_rows((r0, r1, r2, r3), scratch, 0), scratch, result_ref)


def first_rest(b0, b1, b2, b3, tok, gain, wqkv, right, tg_ref, scratch):
    _, xhat, rstd = norm_parts(take_field(tok, scratch), gain[...])
    g = gather_rows((b0, b1, b2, b3), scratch, 0)
    dnormed = dot_nt(right[0], wqkv[:, :D])
    dnormed += dot_nt(right[1], wqkv[:, D : 2 * D])
    dnormed += dot_nt(right[2], wqkv[:, 2 * D :])
    put_field(norm_back(dnormed, gain[...], xhat, rstd, g), scratch, tg_ref)


def weights(member, p0, p1, p2, p3, q0, q1, q2, q3, scratch):
    total = jnp.zeros((D, WIDE), F32)
    for part in (p0, p1, p2, p3):
        total += dot_tn(part[:, :D], part[:, D:])
    scratch[...] = total
    for step, ref in enumerate((q0, q1, q2, q3)):
        first = pl.multiple_of((member ^ step) * PLANE_ROWS, PLANE_ROWS)
        ref[...] = scratch[pl.ds(first, PLANE_ROWS), :].astype(BF16)


def first_weights(me, *refs):
    weights(members_first(*here(me))[1], *refs)


def second_weights(me, *refs):
    weights(members_second(*here(me))[1], *refs)


PIECE = OWN * WIDE // LANES
SHEET = [(x, z) for x in range(X) for z in range(Z)]


def add_rows(a0, a1, a2, a3, b0, b1, b2, b3, out_ref, scratch):
    blocks = ((members_first, (a0, a1, a2, a3)), (members_second, (b0, b1, b2, b3)))
    for slot, (members, parts) in enumerate(blocks):
        total = sum(part[...].astype(F32) for part in parts)
        for peer, (x, z) in enumerate(SHEET):
            m1, _, m3 = members(x, 0, z)
            row = (m3 * GROUP + m1) * OWN
            for c in range(WIDE // LANES):
                first = slot * PIECE + c * OWN
                scratch[peer, first : first + OWN, :] = total[
                    row : row + OWN, c * LANES : (c + 1) * LANES
                ]
    out_ref[...] = scratch[...].astype(BF16)


def own_rows(parts, rows_ref, tile_ref):
    norm = jnp.zeros((1, 1), F32)
    for slot, members in enumerate((members_first, members_second)):
        totals = [jnp.zeros((PIECE, LANES), F32)] * GROUP
        for source, (x, z) in enumerate(SHEET):
            m1 = members(x, 0, z)[0]
            piece = parts[source, slot * PIECE : (slot + 1) * PIECE, :]
            totals[m1] = totals[m1] + piece.astype(F32)
        for m1, total in enumerate(totals):
            rows_ref[m1, slot * PIECE : (slot + 1) * PIECE, :] = total
        norm += jnp.sum(sum(total * total for total in totals), keepdims=True)
    tile_ref[...] = jnp.broadcast_to(norm[None], tile_ref.shape)


def clipped(tiles, rows, qkv_a, out_a, qkv_b, out_b):
    total = jnp.sum(tiles[...], 0)[:1, :1]
    factor = jnp.minimum(1.0, math.sqrt(8.0) * D / jnp.sqrt(total))
    for slot, refs in enumerate(((qkv_a, out_a), (qkv_b, out_b))):
        for k in range(GROUP):
            ref, column = (refs[0], k * WIDE) if k < GROUP - 1 else (refs[1], 0)
            for c in range(WIDE // LANES):
                first = slot * PIECE + c * OWN
                ref[:, column + c * LANES : column + (c + 1) * LANES] = (
                    rows[k, first : first + OWN, :] * factor
                )


def shape_of(*dims, dtype=BF16):
    return jax.ShapeDtypeStruct(dims, dtype)


def call(kernel, outs, scratch, *args, scalar=False, far=0):
    whole = pl.BlockSpec(memory_space=pltpu.VMEM)
    specs = [whole] * (len(args) - far) + [pl.BlockSpec(memory_space=pl.ANY)] * far
    if scalar:
        specs[0] = pl.BlockSpec(memory_space=pltpu.SMEM)
    scratch = [pltpu.VMEM(s, F32) if isinstance(s, tuple) else s for s in scratch]
    return pl.pallas_call(
        kernel,
        out_shape=outs,
        in_specs=specs,
        out_specs=[whole] * len(outs),
        scratch_shapes=scratch,
        compiler_params=pltpu.CompilerParams(vmem_limit_bytes=VMEM_BYTES),
        name=kernel.__name__,
    )(*args)


def in_vmem(*arrays):
    return [pltpu.with_memory_space_constraint(array, pltpu.VMEM) for array in arrays]


def in_hbm(*arrays):
    return [pltpu.with_memory_space_constraint(array, pltpu.HBM) for array in arrays]


def moves(lat_count, lon_count):
    tables = []
    for a in range(2):
        for b in range(2):
            table = []
            for i in range(lat_count):
                for j in range(lon_count):
                    ti = (i - (1 - a)) % lat_count
                    tj = (j - (1 - b)) % lon_count
                    table.append((i * lon_count + j, ti * lon_count + tj))
            tables.append(table)
    return tables


def send(parts, tables, back=False):
    out = []
    for part, table in zip(parts, tables):
        if all(s == t for s, t in table):
            out.append(part)
            continue
        pairs = [(t, s) for s, t in table] if back else table
        out.append(lax.ppermute(part, ("lat", "lon"), pairs))
    return out


def index_of(x, y, z):
    return (x * YLO + y % YLO) * LON + y // YLO * Z + z


CHIPS = [(x, y, z) for x in range(X) for y in range(Y) for z in range(Z)]


SHEETS = [[index_of(x, y, z) for x, z in SHEET] for y in range(Y)]


def swap(parts, members, chip, level):
    out = list(parts)
    for step in (3, 1, 2):
        pairs = []
        for here_chip in CHIPS:
            numbers = list(members(*here_chip))
            numbers[level] ^= step
            pairs.append((index_of(*here_chip), index_of(*chip(*numbers))))
        out[step] = lax.ppermute(parts[step], ("lat", "lon"), pairs)
    return out


def swap_first(parts, level):
    return swap(parts, members_first, chip_first, level)


def swap_second(parts, level):
    return swap(parts, members_second, chip_second, level)


def exchange(parts, groups):
    return lax.all_to_all(parts, ("lat", "lon"), 0, 0, axis_index_groups=groups)


def after(value, earlier):
    return lax.optimization_barrier((value, earlier))[0]


def on_device(
    tokens,
    cotangent,
    region,
    unshifted_norm_gain,
    unshifted_query_key_value,
    out_first,
    shifted_norm_gain,
    shifted_query_key_value,
    out_second,
):
    tables = moves(LAT, LON)
    lat, lon = lax.axis_index("lat"), lax.axis_index("lon")
    me = (lat * LON + lon).astype(jnp.int32).reshape(1)
    gain_a = unshifted_norm_gain.reshape(1, D)
    gain_b = shifted_norm_gain.reshape(1, D)
    tok = tokens.transpose(1, 2, 0, 3)
    cot = cotangent.transpose(1, 2, 0, 3)
    lab = region.transpose(1, 0, 2)

    field = shape_of(TOK, D)
    fields = shape_of(GROUP, TOK, D)
    packs = [shape_of(TOK, D + WIDE)] * GROUP
    *x, keep = call(
        first_forward,
        [shape_of(QUART, SEND)] * 4 + [shape_of(TOK, 5 * D + LANES)],
        [
            (TOK, D),
            (TOK, LANES),
            pltpu.VMEM(tok.shape, BF16),
            (1, D),
            pltpu.VMEM(lab.shape, jnp.int32),
            pltpu.VMEM(cot.shape, BF16),
            pltpu.VMEM((D, 3 * D), BF16),
            pltpu.VMEM((D, D), BF16),
            pltpu.SemaphoreType.DMA((6,)),
        ],
        me, *in_hbm(tok, gain_a, lab, cot, unshifted_query_key_value, out_first),
        scalar=True, far=6,
    )
    x = send(x, tables)
    *back, normed_b, att_b, right_b = call(
        second_main,
        [shape_of(QUART, D)] * 4 + [field, field, fields],
        [(TOK, D), (TOK, LANES)],
        *x, gain_b, shifted_query_key_value, out_second,
    )
    back = send(back, tables, back=True)
    half = pltpu.VMEM((TOK, D), BF16)
    *pack_b, r0, r1, r2, r3 = call(
        second_pack,
        packs + [pltpu.HBM((QUART, D), BF16)] * 4,
        [half, half, (TOK, D)],
        me, normed_b, att_b, right_b, *x, out_second,
        scalar=True,
    )
    pack_b = swap_second(after(pack_b, back[:3]), 0)
    right_a, *pack_a = call(
        first_backward,
        [fields] + packs,
        [(TOK, D), half, half],
        me, *back, out_first, keep,
        scalar=True,
    )
    pack_a = swap_first(pack_a, 0)
    grid = shape_of(WLAT, WLON, WLEV, D)
    (token_gradient,) = call(
        first_rest,
        [grid],
        [(TOK, D)],
        *back, tok, gain_a, unshifted_query_key_value, right_a,
    )
    pack_b, token_gradient = lax.optimization_barrier((pack_b, token_gradient))
    token_gradient = token_gradient.transpose(2, 0, 1, 3)

    rows = [shape_of(PLANE_ROWS, WIDE)] * GROUP
    sum_b = swap_second(call(second_weights, rows, [(D, WIDE)], me, *in_vmem(*pack_b), scalar=True), 1)
    sum_a = swap_first(call(first_weights, rows, [(D, WIDE)], me, *in_vmem(*pack_a), scalar=True), 1)
    piece = (len(SHEET), 2 * PIECE, LANES)
    (sums,) = call(add_rows, [shape_of(*piece)], [piece], *sum_a, *sum_b)
    res = send(after([r0, r1, r2, r3], sums), tables, back=True)
    sums, res = lax.optimization_barrier((exchange(sums, SHEETS), res))
    (result,) = call(place, [grid], [(TOK, D)], *res)
    result = result.transpose(2, 0, 1, 3)
    mine, tiles = call(
        own_rows,
        [shape_of(GROUP, 2 * PIECE, LANES, dtype=F32), shape_of(LAT * LON, 1, LANES, dtype=F32)],
        [],
        sums,
    )
    tiles = lax.all_to_all(tiles, ("lat", "lon"), 0, 0)
    out_qkv, out_out = shape_of(OWN, 3 * D, dtype=F32), shape_of(OWN, D, dtype=F32)
    clips = call(clipped, [out_qkv, out_out] * 2, [], tiles, mine)
    return (result, token_gradient, *clips)


def solution(mesh):
    field = P("rep", "lat", "lon", None)
    rows = P(("rep", "lat", "lon"), None)
    in_specs = (field, field, P("rep", "lat", "lon"), P(), P(), P(), P(), P(), P())
    return jax.shard_map(
        on_device,
        mesh=mesh,
        in_specs=in_specs,
        out_specs=(field, field, rows, rows, rows, rows),
        check_vma=False,
    )
```

```python
import math

import jax
import jax.numpy as jnp
from jax import lax
from jax.experimental import pallas as pl
from jax.experimental.pallas import tpu as pltpu
from jax.sharding import PartitionSpec as P

D = 512
HEADS = 8
HEAD = 64
PAIRS = HEADS // 2
WLEV = 2
WLAT = 6
WLON = 12
HLAT = WLAT // 2
HLON = WLON // 2
TOK = WLEV * WLAT * WLON
QUART = TOK // 4
LANES = 128

X, YLO, YHI, Z = 4, 2, 2, 8
Y = YHI * YLO
LAT, LON = X * YLO, YHI * Z
OWN = D // (LAT * LON)
GROUP = 4
LAST = 8
WIDE = 4 * D // GROUP
PLANE_ROWS = D // GROUP
LAST_ROWS = PLANE_ROWS // LAST
SEND = 2 * D + LANES

EPSILON = 1e-05
NEGATIVE = -1e30
F32 = jnp.float32
BF16 = jnp.bfloat16
VMEM_BYTES = 16 * 1024 * 1024


def dot_nn(a, b):
    return lax.dot_general(a, b, (((1,), (0,)), ((), ())), preferred_element_type=F32)


def dot_nt(a, b):
    return lax.dot_general(a, b, (((1,), (1,)), ((), ())), preferred_element_type=F32)


def dot_tn(a, b):
    return lax.dot_general(a, b, (((0,), (0,)), ((), ())), preferred_element_type=F32)


def norm_parts(values, gain):
    average = jnp.mean(values, -1, keepdims=True)
    centered = values - average
    rstd = lax.rsqrt(jnp.mean(centered * centered, -1, keepdims=True) + EPSILON)
    xhat = centered * rstd
    return (xhat * gain).astype(BF16), xhat, rstd


def norm_back(dnormed, gain, xhat, rstd, incoming):
    s = dnormed * gain
    return (
        rstd * (s - jnp.mean(s, -1, keepdims=True) - xhat * jnp.mean(s * xhat, -1, keepdims=True))
        + incoming
    )


def label_bias(labels):
    lane = lax.broadcasted_iota(jnp.int32, (TOK, LANES), 1).astype(F32)
    hot = jnp.where((lane == labels) & (lane > 0.5), 1.0, 0.0).astype(BF16)
    return (1.0 - dot_nt(hot, hot)) * NEGATIVE


def pair_of(fields, part, pair):
    start = part * D + pair * LANES
    return fields[:, start : start + LANES]


def softmax_rows(scores):
    shifted = jnp.exp(scores - jnp.max(scores, -1, keepdims=True))
    return shifted * (1.0 / jnp.sum(shifted, -1, keepdims=True))


def attention(proj, bias, grad=None, attended=None):
    lane = lax.broadcasted_iota(jnp.int32, (1, LANES), 1)
    is_low = lane < HEAD
    low = is_low.astype(F32)
    masks = (low.astype(BF16), (1.0 - low).astype(BF16))
    bias = jnp.concatenate([bias, bias], 0)

    def stacked(field):
        return jnp.concatenate([field * masks[0], field * masks[1]], 0)

    def merged(both):
        return jnp.where(is_low, both[:TOK], both[TOK:])

    att, dq, dk, dv = [], [], [], []
    for pair in range(PAIRS):
        q = stacked(pair_of(proj, 0, pair) * BF16(HEAD**-0.5))
        k = pair_of(proj, 1, pair)
        v = pair_of(proj, 2, pair)
        probs = softmax_rows(dot_nt(q, k) + bias)
        p16 = probs.astype(BF16)
        if attended is None:
            o = merged(dot_nn(p16, v)).astype(BF16)
            att.append(o)
        else:
            o = pair_of(attended, 0, pair)
        if grad is not None:
            g = pair_of(grad, 0, pair)
            g_both = stacked(g)
            product = g.astype(F32) * o.astype(F32)
            delta = jnp.concatenate(
                [
                    jnp.sum(product * low, -1, keepdims=True),
                    jnp.sum(product * (1.0 - low), -1, keepdims=True),
                ],
                0,
            )
            ds16 = (probs * (dot_nt(g_both, v) - delta)).astype(BF16)
            dq.append((merged(dot_nn(ds16, k)) * HEAD**-0.5).astype(BF16))
            dk.append(dot_tn(ds16, q).astype(BF16))
            dv.append(dot_tn(p16, g_both).astype(BF16))
    if attended is None:
        attended = jnp.concatenate(att, -1)
    dproj = jnp.concatenate(dq + dk + dv, -1) if grad is not None else None
    return attended, dproj


def take_field(ref, scratch):
    half = HLON * WLEV
    for row in range(WLAT):
        values = ref[row].astype(F32).reshape(2 * half, D)
        for b in range(2):
            first = (2 * (row // HLAT) + b) * QUART + row % HLAT * half
            scratch[first : first + half, :] = values[b * half : (b + 1) * half]
    return scratch[...]


def put_field(values, scratch, ref):
    scratch[...] = values
    half = HLON * WLEV
    for row in range(WLAT):
        for b in range(2):
            first = (2 * (row // HLAT) + b) * QUART + row % HLAT * half
            ref[row, b * HLON : (b + 1) * HLON] = (
                scratch[first : first + half, :].reshape(HLON, WLEV, D).astype(BF16)
            )


def take_labels(region):
    places = WLAT * WLEV
    table = region[...].reshape(places, WLON).astype(F32)
    token = lax.broadcasted_iota(jnp.int32, (TOK, places), 0)
    slot, rest = token // QUART, token % QUART
    row = slot // 2 * HLAT + rest // (HLON * WLEV)
    column = slot % 2 * HLON + rest % (HLON * WLEV) // WLEV
    place = lax.broadcasted_iota(jnp.int32, (TOK, places), 1)
    rows = dot_nn((place == row * WLEV + rest % WLEV).astype(F32), table)
    return jnp.sum(jnp.where(place == column, rows, 0.0), -1, keepdims=True)


def gather_rows(refs, scratch, column):
    wide = scratch.shape[1]
    for slot, ref in enumerate(refs):
        scratch[slot * QUART : (slot + 1) * QUART, :] = ref[:, column : column + wide].astype(F32)
    return scratch[...]


def scatter_rows(values, scratch, refs, column):
    scratch[...] = values
    wide = scratch.shape[1]
    for slot, ref in enumerate(refs):
        ref[:, column : column + wide] = scratch[slot * QUART : (slot + 1) * QUART, :].astype(BF16)


def regroup(source_of):
    to = lax.broadcasted_iota(jnp.int32, (1, D), 1)
    return (lax.broadcasted_iota(jnp.int32, (D, D), 0) == source_of(to)).astype(F32).astype(BF16)


def squares(x, z):
    return (x & 1) + (z & 1) * 2, (x >> 1) + (z >> 1) * 2


def members_first(x, y, z):
    m1, m3 = squares(x, z)
    return m1, y, m3


def members_second(x, y, z):
    m1, m3 = squares(x + X - 1 & X - 1, z + Z - 1 & Z - 1)
    return m1, y, m3


def chip_first(m1, m2, m3):
    return (m1 & 1) + (m3 & 1) * 2, m2, (m1 >> 1) + (m3 >> 1) * 2


def chip_second(m1, m2, m3):
    x, y, z = chip_first(m1, m2, m3)
    return x + 1 & X - 1, y, z + 1 & Z - 1


def row_order(chip):
    def source_of(to):
        m1, m3, m2 = to // OWN % GROUP, to // (OWN * GROUP) % LAST, to // (OWN * GROUP * LAST)
        x, y, z = chip(m1, m2, m3)
        return (((x * YLO + y % YLO) * YHI + y // YLO) * Z + z) * OWN + to % OWN

    return source_of


def here(me):
    place = me[0]
    return place >> 5, (place >> 3 & 1) * 2 + (place >> 4 & 1), place & 7


def pack(me, left_refs, right_ref, packs):
    for step, ref in enumerate(packs):
        peer = me ^ step
        is_att = peer == GROUP - 1

        @pl.when(is_att)
        def _():
            ref[:, :D] = left_refs[1][...]

        @pl.when(jnp.logical_not(is_att))
        def _():
            ref[:, :D] = left_refs[0][...]

        ref[:, D:] = right_ref[peer]


def store_right(dproj, g16, right_ref):
    for part in range(3):
        right_ref[part] = dproj[:, part * D : (part + 1) * D]
    right_ref[3] = g16


def first_forward(
    me, tok_hbm, gain_hbm, region_hbm, cot_hbm, wqkv_hbm, wout_hbm,
    x0, x1, x2, x3, keep_ref, scratch, lab_scratch, tok, gain, region, cot, wqkv, wout, sems,
):
    far = (tok_hbm, gain_hbm, region_hbm, cot_hbm, wqkv_hbm, wout_hbm)
    copies = [
        pltpu.make_async_copy(source, target, sems.at[i])
        for i, (source, target) in enumerate(zip(far, (tok, gain, region, cot, wqkv, wout)))
    ]
    for copy in copies:
        copy.start()
    refs = (x0, x1, x2, x3)
    copies[0].wait()
    values = take_field(tok, scratch)
    copies[1].wait()
    normed, _, _ = norm_parts(values, gain[...])
    copies[2].wait()
    labels = jnp.broadcast_to(take_labels(region), (TOK, LANES))
    near = lax.broadcasted_iota(jnp.int32, (TOK, LANES), 0) < 2 * QUART
    moved = labels + jnp.where(near & (me[0] < LON), 4.0, 0.0)
    scatter_rows(moved, lab_scratch, refs, 2 * D)
    copies[3].wait()
    take_field(cot, scratch)
    for slot, ref in enumerate(refs):
        ref[:, D : 2 * D] = scratch[slot * QUART : (slot + 1) * QUART, :].astype(BF16)
    copies[4].wait()
    proj = dot_nn(normed, wqkv[...]).astype(BF16)
    keep_ref[:, : 3 * D] = proj
    keep_ref[:, 4 * D : 5 * D] = normed
    keep_ref[:, 5 * D :] = labels.astype(BF16)
    attended, _ = attention(proj, label_bias(labels))
    keep_ref[:, 3 * D : 4 * D] = attended
    copies[5].wait()
    scatter_rows(values + dot_nn(attended, wout[...]), scratch, refs, 0)


def second_main(
    x0, x1, x2, x3, gain, wqkv, wout,
    b0, b1, b2, b3, normed_ref, att_ref, right_ref, scratch, lab_scratch,
):
    parts = (x0, x1, x2, x3)
    back = (b0, b1, b2, b3)
    values = gather_rows(parts, scratch, 0)
    g = gather_rows(parts, scratch, D)
    labels = gather_rows(parts, lab_scratch, 2 * D)
    g16 = g.astype(BF16)
    normed, xhat, rstd = norm_parts(values, gain[...])
    normed_ref[...] = normed
    proj = dot_nn(normed, wqkv[...]).astype(BF16)
    datt = dot_nt(g16, wout[...]).astype(BF16)
    attended, dproj = attention(proj, label_bias(labels), grad=datt)
    att_ref[...] = attended
    store_right(dproj, g16, right_ref)
    scatter_rows(values + dot_nn(attended, wout[...]), scratch, back, 0)
    dnormed = dot_nt(dproj, wqkv[...])
    scatter_rows(norm_back(dnormed, gain[...], xhat, rstd, g), scratch, back, D)


def second_pack(me, normed, attended, right, p0, p1, p2, p3, left_n, left_a):
    order = regroup(row_order(chip_second))
    left_n[...] = dot_nn(normed[...], order).astype(BF16)
    left_a[...] = dot_nn(attended[...], order).astype(BF16)
    pack(members_second(*here(me))[0], (left_n, left_a), right, (p0, p1, p2, p3))


def first_backward(
    me, b0, b1, b2, b3, wout, keep, right_ref, p0, p1, p2, p3, scratch, left_n, left_a
):
    g16 = gather_rows((b0, b1, b2, b3), scratch, D).astype(BF16)
    datt = dot_nt(g16, wout[...]).astype(BF16)
    bias = label_bias(keep[:, 5 * D :].astype(F32))
    _, dproj = attention(keep[...], bias, grad=datt, attended=keep[:, 3 * D : 4 * D])
    store_right(dproj, g16, right_ref)
    order = regroup(row_order(chip_first))
    left_n[...] = dot_nn(keep[:, 4 * D : 5 * D], order).astype(BF16)
    left_a[...] = dot_nn(keep[:, 3 * D : 4 * D], order).astype(BF16)
    pack(members_first(*here(me))[0], (left_n, left_a), right_ref, (p0, p1, p2, p3))


def first_rest(b0, b1, b2, b3, tok, gain, wqkv, right, tg_ref, result_ref, scratch):
    back = (b0, b1, b2, b3)
    put_field(gather_rows(back, scratch, 0), scratch, result_ref)
    _, xhat, rstd = norm_parts(take_field(tok, scratch), gain[...])
    g = gather_rows(back, scratch, D)
    dnormed = dot_nt(right[0], wqkv[:, :D])
    dnormed += dot_nt(right[1], wqkv[:, D : 2 * D])
    dnormed += dot_nt(right[2], wqkv[:, 2 * D :])
    put_field(norm_back(dnormed, gain[...], xhat, rstd, g), scratch, tg_ref)


def weights(member, p0, p1, p2, p3, q0, q1, q2, q3, scratch):
    total = jnp.zeros((D, WIDE), F32)
    for part in (p0, p1, p2, p3):
        total += dot_tn(part[:, :D], part[:, D:])
    scratch[...] = total
    for step, ref in enumerate((q0, q1, q2, q3)):
        first = pl.multiple_of((member ^ step) * PLANE_ROWS, PLANE_ROWS)
        ref[...] = scratch[pl.ds(first, PLANE_ROWS), :].astype(BF16)


def first_weights(me, *refs):
    weights(members_first(*here(me))[1], *refs)


def second_weights(me, *refs):
    weights(members_second(*here(me))[1], *refs)


PIECE = OWN * WIDE // LANES
SHEET = [(x, z) for x in range(X) for z in range(Z)]


def add_rows(a0, a1, a2, a3, b0, b1, b2, b3, out_ref, scratch):
    blocks = ((members_first, (a0, a1, a2, a3)), (members_second, (b0, b1, b2, b3)))
    for slot, (members, parts) in enumerate(blocks):
        total = sum(part[...].astype(F32) for part in parts)
        for peer, (x, z) in enumerate(SHEET):
            m1, _, m3 = members(x, 0, z)
            row = (m3 * GROUP + m1) * OWN
            for c in range(WIDE // LANES):
                first = slot * PIECE + c * OWN
                scratch[peer, first : first + OWN, :] = total[
                    row : row + OWN, c * LANES : (c + 1) * LANES
                ]
    out_ref[...] = scratch[...].astype(BF16)


def own_rows(parts, rows_ref, tile_ref):
    norm = jnp.zeros((1, 1), F32)
    for slot, members in enumerate((members_first, members_second)):
        totals = [jnp.zeros((PIECE, LANES), F32)] * GROUP
        for source, (x, z) in enumerate(SHEET):
            m1 = members(x, 0, z)[0]
            piece = parts[source, slot * PIECE : (slot + 1) * PIECE, :]
            totals[m1] = totals[m1] + piece.astype(F32)
        for m1, total in enumerate(totals):
            rows_ref[m1, slot * PIECE : (slot + 1) * PIECE, :] = total
        norm += jnp.sum(sum(total * total for total in totals), keepdims=True)
    tile_ref[...] = jnp.broadcast_to(norm[None], tile_ref.shape)


def clipped(tiles, rows, qkv_a, out_a, qkv_b, out_b):
    total = jnp.sum(tiles[...], 0)[:1, :1]
    factor = jnp.minimum(1.0, math.sqrt(8.0) * D / jnp.sqrt(total))
    for slot, refs in enumerate(((qkv_a, out_a), (qkv_b, out_b))):
        for k in range(GROUP):
            ref, column = (refs[0], k * WIDE) if k < GROUP - 1 else (refs[1], 0)
            for c in range(WIDE // LANES):
                first = slot * PIECE + c * OWN
                ref[:, column + c * LANES : column + (c + 1) * LANES] = (
                    rows[k, first : first + OWN, :] * factor
                )


def shape_of(*dims, dtype=BF16):
    return jax.ShapeDtypeStruct(dims, dtype)


def call(kernel, outs, scratch, *args, scalar=False, far=0):
    whole = pl.BlockSpec(memory_space=pltpu.VMEM)
    specs = [whole] * (len(args) - far) + [pl.BlockSpec(memory_space=pl.ANY)] * far
    if scalar:
        specs[0] = pl.BlockSpec(memory_space=pltpu.SMEM)
    scratch = [pltpu.VMEM(s, F32) if isinstance(s, tuple) else s for s in scratch]
    return pl.pallas_call(
        kernel,
        out_shape=outs,
        in_specs=specs,
        out_specs=[whole] * len(outs),
        scratch_shapes=scratch,
        compiler_params=pltpu.CompilerParams(vmem_limit_bytes=VMEM_BYTES),
        name=kernel.__name__,
    )(*args)


def in_vmem(*arrays):
    return [pltpu.with_memory_space_constraint(array, pltpu.VMEM) for array in arrays]


def in_hbm(*arrays):
    return [pltpu.with_memory_space_constraint(array, pltpu.HBM) for array in arrays]


def moves(lat_count, lon_count):
    tables = []
    for a in range(2):
        for b in range(2):
            table = []
            for i in range(lat_count):
                for j in range(lon_count):
                    ti = (i - (1 - a)) % lat_count
                    tj = (j - (1 - b)) % lon_count
                    table.append((i * lon_count + j, ti * lon_count + tj))
            tables.append(table)
    return tables


def send(parts, tables, back=False):
    out = []
    for part, table in zip(parts, tables):
        if all(s == t for s, t in table):
            out.append(part)
            continue
        pairs = [(t, s) for s, t in table] if back else table
        out.append(lax.ppermute(part, ("lat", "lon"), pairs))
    return out


def index_of(x, y, z):
    return (x * YLO + y % YLO) * LON + y // YLO * Z + z


CHIPS = [(x, y, z) for x in range(X) for y in range(Y) for z in range(Z)]


SHEETS = [[index_of(x, y, z) for x, z in SHEET] for y in range(Y)]


def swap(parts, members, chip, level, steps):
    out = list(parts)
    for step in steps:
        pairs = []
        for here_chip in CHIPS:
            numbers = list(members(*here_chip))
            numbers[level] ^= step
            pairs.append((index_of(*here_chip), index_of(*chip(*numbers))))
        out[step] = lax.ppermute(parts[step], ("lat", "lon"), pairs)
    return out


def swap_first(parts, level, steps):
    return swap(parts, members_first, chip_first, level, steps)


def swap_second(parts, level, steps):
    return swap(parts, members_second, chip_second, level, steps)


def exchange(parts, groups):
    return lax.all_to_all(parts, ("lat", "lon"), 0, 0, axis_index_groups=groups)


def after(value, earlier):
    return lax.optimization_barrier((value, earlier))[0]


def on_device(
    tokens,
    cotangent,
    region,
    unshifted_norm_gain,
    unshifted_query_key_value,
    out_first,
    shifted_norm_gain,
    shifted_query_key_value,
    out_second,
):
    tables = moves(LAT, LON)
    lat, lon = lax.axis_index("lat"), lax.axis_index("lon")
    me = (lat * LON + lon).astype(jnp.int32).reshape(1)
    gain_a = unshifted_norm_gain.reshape(1, D)
    gain_b = shifted_norm_gain.reshape(1, D)
    tok = tokens.transpose(1, 2, 0, 3)
    cot = cotangent.transpose(1, 2, 0, 3)
    lab = region.transpose(1, 0, 2)

    field = shape_of(TOK, D)
    fields = shape_of(GROUP, TOK, D)
    packs = [shape_of(TOK, D + WIDE)] * GROUP
    *x, keep = call(
        first_forward,
        [shape_of(QUART, SEND)] * 4 + [shape_of(TOK, 5 * D + LANES)],
        [
            (TOK, D),
            (TOK, LANES),
            pltpu.VMEM(tok.shape, BF16),
            (1, D),
            pltpu.VMEM(lab.shape, jnp.int32),
            pltpu.VMEM(cot.shape, BF16),
            pltpu.VMEM((D, 3 * D), BF16),
            pltpu.VMEM((D, D), BF16),
            pltpu.SemaphoreType.DMA((6,)),
        ],
        me, *in_hbm(tok, gain_a, lab, cot, unshifted_query_key_value, out_first),
        scalar=True, far=6,
    )
    x = send(x, tables)
    *back, normed_b, att_b, right_b = call(
        second_main,
        [shape_of(QUART, 2 * D)] * 4 + [field, field, fields],
        [(TOK, D), (TOK, LANES)],
        *x, gain_b, shifted_query_key_value, out_second,
    )
    back = send(back, tables, back=True)
    half = pltpu.VMEM((TOK, D), BF16)
    pack_b = call(
        second_pack, packs, [half, half], me, normed_b, att_b, right_b, scalar=True
    )
    pack_b = swap_second(after(pack_b, back[:3]), 0, (3, 1, 2))
    right_a, *pack_a = call(
        first_backward,
        [fields] + packs,
        [(TOK, D), half, half],
        me, *back, out_first, keep,
        scalar=True,
    )
    pack_a = swap_first(pack_a, 0, (3, 1, 2))
    grid = shape_of(WLAT, WLON, WLEV, D)
    token_gradient, result = call(
        first_rest,
        [grid, grid],
        [(TOK, D)],
        *back, tok, gain_a, unshifted_query_key_value, right_a,
    )
    token_gradient = token_gradient.transpose(2, 0, 1, 3)
    result = result.transpose(2, 0, 1, 3)

    rows = [shape_of(PLANE_ROWS, WIDE)] * GROUP
    sum_b = call(second_weights, rows, [(D, WIDE)], me, *in_vmem(*pack_b), scalar=True)
    sum_b = swap_second(sum_b, 1, (2, 1, 3))
    sum_a = call(first_weights, rows, [(D, WIDE)], me, *in_vmem(*pack_a), scalar=True)
    sum_a = swap_first(sum_a, 1, (1, 2, 3))
    piece = (len(SHEET), 2 * PIECE, LANES)
    (sums,) = call(add_rows, [shape_of(*piece)], [piece], *sum_a, *sum_b)
    sums = exchange(sums, SHEETS)
    mine, tiles = call(
        own_rows,
        [shape_of(GROUP, 2 * PIECE, LANES, dtype=F32), shape_of(LAT * LON, 1, LANES, dtype=F32)],
        [],
        sums,
    )
    tiles = lax.all_to_all(tiles, ("lat", "lon"), 0, 0)
    out_qkv, out_out = shape_of(OWN, 3 * D, dtype=F32), shape_of(OWN, D, dtype=F32)
    clips = call(clipped, [out_qkv, out_out] * 2, [], tiles, mine)
    return (result, token_gradient, *clips)


def solution(mesh):
    field = P("rep", "lat", "lon", None)
    rows = P(("rep", "lat", "lon"), None)
    in_specs = (field, field, P("rep", "lat", "lon"), P(), P(), P(), P(), P(), P())
    return jax.shard_map(
        on_device,
        mesh=mesh,
        in_specs=in_specs,
        out_specs=(field, field, rows, rows, rows, rows),
        check_vma=False,
    )
```

```python
import math

import jax
import jax.numpy as jnp
from jax import lax
from jax.experimental import pallas as pl
from jax.experimental.pallas import tpu as pltpu
from jax.sharding import PartitionSpec as P

D = 512
HEADS = 8
HEAD = 64
PAIRS = HEADS // 2
WLEV = 2
WLAT = 6
WLON = 12
HLAT = WLAT // 2
HLON = WLON // 2
TOK = WLEV * WLAT * WLON
QUART = TOK // 4
LANES = 128

X, YLO, YHI, Z = 4, 2, 2, 8
Y = YHI * YLO
LAT, LON = X * YLO, YHI * Z
OWN = D // (LAT * LON)
GROUP = 4
LAST = 8
WIDE = 4 * D // GROUP
PLANE_ROWS = D // GROUP
LAST_ROWS = PLANE_ROWS // LAST
SEND = 2 * D + LANES

EPSILON = 1e-05
NEGATIVE = -1e30
F32 = jnp.float32
BF16 = jnp.bfloat16
VMEM_BYTES = 16 * 1024 * 1024


def dot_nn(a, b):
    return lax.dot_general(a, b, (((1,), (0,)), ((), ())), preferred_element_type=F32)


def dot_nt(a, b):
    return lax.dot_general(a, b, (((1,), (1,)), ((), ())), preferred_element_type=F32)


def dot_tn(a, b):
    return lax.dot_general(a, b, (((0,), (0,)), ((), ())), preferred_element_type=F32)


def norm_parts(values, gain):
    average = jnp.mean(values, -1, keepdims=True)
    centered = values - average
    rstd = lax.rsqrt(jnp.mean(centered * centered, -1, keepdims=True) + EPSILON)
    xhat = centered * rstd
    return (xhat * gain).astype(BF16), xhat, rstd


def norm_back(dnormed, gain, xhat, rstd, incoming):
    s = dnormed * gain
    return (
        rstd * (s - jnp.mean(s, -1, keepdims=True) - xhat * jnp.mean(s * xhat, -1, keepdims=True))
        + incoming
    )


def label_bias(labels):
    lane = lax.broadcasted_iota(jnp.int32, (TOK, LANES), 1).astype(F32)
    hot = jnp.where((lane == labels) & (lane > 0.5), 1.0, 0.0).astype(BF16)
    return (1.0 - dot_nt(hot, hot)) * NEGATIVE


def pair_of(fields, part, pair):
    start = part * D + pair * LANES
    return fields[:, start : start + LANES]


def softmax_rows(scores):
    shifted = jnp.exp(scores - jnp.max(scores, -1, keepdims=True))
    return shifted * (1.0 / jnp.sum(shifted, -1, keepdims=True))


def attention(proj, bias, grad=None, attended=None):
    lane = lax.broadcasted_iota(jnp.int32, (1, LANES), 1)
    is_low = lane < HEAD
    low = is_low.astype(F32)
    masks = (low.astype(BF16), (1.0 - low).astype(BF16))
    bias = jnp.concatenate([bias, bias], 0)

    def stacked(field):
        return jnp.concatenate([field * masks[0], field * masks[1]], 0)

    def merged(both):
        return jnp.where(is_low, both[:TOK], both[TOK:])

    att, dq, dk, dv = [], [], [], []
    for pair in range(PAIRS):
        q = stacked(pair_of(proj, 0, pair) * BF16(HEAD**-0.5))
        k = pair_of(proj, 1, pair)
        v = pair_of(proj, 2, pair)
        probs = softmax_rows(dot_nt(q, k) + bias)
        p16 = probs.astype(BF16)
        if attended is None:
            o = merged(dot_nn(p16, v)).astype(BF16)
            att.append(o)
        else:
            o = pair_of(attended, 0, pair)
        if grad is not None:
            g = pair_of(grad, 0, pair)
            g_both = stacked(g)
            product = g.astype(F32) * o.astype(F32)
            delta = jnp.concatenate(
                [
                    jnp.sum(product * low, -1, keepdims=True),
                    jnp.sum(product * (1.0 - low), -1, keepdims=True),
                ],
                0,
            )
            ds16 = (probs * (dot_nt(g_both, v) - delta)).astype(BF16)
            dq.append((merged(dot_nn(ds16, k)) * HEAD**-0.5).astype(BF16))
            dk.append(dot_tn(ds16, q).astype(BF16))
            dv.append(dot_tn(p16, g_both).astype(BF16))
    if attended is None:
        attended = jnp.concatenate(att, -1)
    dproj = jnp.concatenate(dq + dk + dv, -1) if grad is not None else None
    return attended, dproj


def take_field(ref, scratch):
    half = HLON * WLEV
    for row in range(WLAT):
        values = ref[row].astype(F32).reshape(2 * half, D)
        for b in range(2):
            first = (2 * (row // HLAT) + b) * QUART + row % HLAT * half
            scratch[first : first + half, :] = values[b * half : (b + 1) * half]
    return scratch[...]


def put_field(values, scratch, ref):
    scratch[...] = values
    half = HLON * WLEV
    for row in range(WLAT):
        for b in range(2):
            first = (2 * (row // HLAT) + b) * QUART + row % HLAT * half
            ref[row, b * HLON : (b + 1) * HLON] = (
                scratch[first : first + half, :].reshape(HLON, WLEV, D).astype(BF16)
            )


def take_labels(region):
    places = WLAT * WLEV
    table = region[...].reshape(places, WLON).astype(F32)
    token = lax.broadcasted_iota(jnp.int32, (TOK, places), 0)
    slot, rest = token // QUART, token % QUART
    row = slot // 2 * HLAT + rest // (HLON * WLEV)
    column = slot % 2 * HLON + rest % (HLON * WLEV) // WLEV
    place = lax.broadcasted_iota(jnp.int32, (TOK, places), 1)
    rows = dot_nn((place == row * WLEV + rest % WLEV).astype(F32), table)
    return jnp.sum(jnp.where(place == column, rows, 0.0), -1, keepdims=True)


def gather_rows(refs, scratch, column):
    wide = scratch.shape[1]
    for slot, ref in enumerate(refs):
        scratch[slot * QUART : (slot + 1) * QUART, :] = ref[:, column : column + wide].astype(F32)
    return scratch[...]


def scatter_rows(values, scratch, refs, column):
    scratch[...] = values
    wide = scratch.shape[1]
    for slot, ref in enumerate(refs):
        ref[:, column : column + wide] = scratch[slot * QUART : (slot + 1) * QUART, :].astype(BF16)


def regroup(source_of):
    to = lax.broadcasted_iota(jnp.int32, (1, D), 1)
    return (lax.broadcasted_iota(jnp.int32, (D, D), 0) == source_of(to)).astype(F32).astype(BF16)


def squares(x, z):
    return (x & 1) + (z & 1) * 2, (x >> 1) + (z >> 1) * 2


def members_first(x, y, z):
    m1, m3 = squares(x, z)
    return m1, y, m3


def members_second(x, y, z):
    m1, m3 = squares(x + X - 1 & X - 1, z + Z - 1 & Z - 1)
    return m1, y, m3


def chip_first(m1, m2, m3):
    return (m1 & 1) + (m3 & 1) * 2, m2, (m1 >> 1) + (m3 >> 1) * 2


def chip_second(m1, m2, m3):
    x, y, z = chip_first(m1, m2, m3)
    return x + 1 & X - 1, y, z + 1 & Z - 1


def row_order(chip):
    def source_of(to):
        m1, m3, m2 = to // OWN % GROUP, to // (OWN * GROUP) % LAST, to // (OWN * GROUP * LAST)
        x, y, z = chip(m1, m2, m3)
        return (((x * YLO + y % YLO) * YHI + y // YLO) * Z + z) * OWN + to % OWN

    return source_of


def here(me):
    place = me[0]
    return place >> 5, (place >> 3 & 1) * 2 + (place >> 4 & 1), place & 7


def pack(me, left_refs, right_ref, packs):
    for step, ref in enumerate(packs):
        peer = me ^ step
        is_att = peer == GROUP - 1

        @pl.when(is_att)
        def _():
            ref[:, :D] = left_refs[1][...]

        @pl.when(jnp.logical_not(is_att))
        def _():
            ref[:, :D] = left_refs[0][...]

        ref[:, D:] = right_ref[peer]


def store_right(dproj, g16, right_ref):
    for part in range(3):
        right_ref[part] = dproj[:, part * D : (part + 1) * D]
    right_ref[3] = g16


def first_forward(
    me, tok_hbm, gain_hbm, region_hbm, cot_hbm, wqkv_hbm, wout_hbm,
    x0, x1, x2, x3, keep_ref, scratch, lab_scratch, tok, gain, region, cot, wqkv, wout, sems,
):
    far = (tok_hbm, gain_hbm, region_hbm, cot_hbm, wqkv_hbm, wout_hbm)
    copies = [
        pltpu.make_async_copy(source, target, sems.at[i])
        for i, (source, target) in enumerate(zip(far, (tok, gain, region, cot, wqkv, wout)))
    ]
    for copy in copies:
        copy.start()
    refs = (x0, x1, x2, x3)
    copies[0].wait()
    values = take_field(tok, scratch)
    copies[1].wait()
    normed, _, _ = norm_parts(values, gain[...])
    copies[2].wait()
    labels = jnp.broadcast_to(take_labels(region), (TOK, LANES))
    near = lax.broadcasted_iota(jnp.int32, (TOK, LANES), 0) < 2 * QUART
    moved = labels + jnp.where(near & (me[0] < LON), 4.0, 0.0)
    scatter_rows(moved, lab_scratch, refs, 2 * D)
    copies[3].wait()
    take_field(cot, scratch)
    for slot, ref in enumerate(refs):
        ref[:, D : 2 * D] = scratch[slot * QUART : (slot + 1) * QUART, :].astype(BF16)
    copies[4].wait()
    proj = dot_nn(normed, wqkv[...]).astype(BF16)
    keep_ref[:, : 3 * D] = proj
    keep_ref[:, 4 * D : 5 * D] = normed
    keep_ref[:, 5 * D :] = labels.astype(BF16)
    attended, _ = attention(proj, label_bias(labels))
    keep_ref[:, 3 * D : 4 * D] = attended
    copies[5].wait()
    scatter_rows(values + dot_nn(attended, wout[...]), scratch, refs, 0)


def second_main(
    x0, x1, x2, x3, gain, wqkv, wout,
    b0, b1, b2, b3, normed_ref, att_ref, right_ref, scratch, lab_scratch,
):
    parts = (x0, x1, x2, x3)
    back = (b0, b1, b2, b3)
    values = gather_rows(parts, scratch, 0)
    g = gather_rows(parts, scratch, D)
    labels = gather_rows(parts, lab_scratch, 2 * D)
    g16 = g.astype(BF16)
    normed, xhat, rstd = norm_parts(values, gain[...])
    normed_ref[...] = normed
    proj = dot_nn(normed, wqkv[...]).astype(BF16)
    datt = dot_nt(g16, wout[...]).astype(BF16)
    attended, dproj = attention(proj, label_bias(labels), grad=datt)
    att_ref[...] = attended
    store_right(dproj, g16, right_ref)
    scatter_rows(values + dot_nn(attended, wout[...]), scratch, back, 0)
    dnormed = dot_nt(dproj, wqkv[...])
    scatter_rows(norm_back(dnormed, gain[...], xhat, rstd, g), scratch, back, D)


def second_pack(me, normed, attended, right, p0, p1, p2, p3, left_n, left_a):
    order = regroup(row_order(chip_second))
    left_n[...] = dot_nn(normed[...], order).astype(BF16)
    left_a[...] = dot_nn(attended[...], order).astype(BF16)
    pack(members_second(*here(me))[0], (left_n, left_a), right, (p0, p1, p2, p3))


def first_backward(
    me, b0, b1, b2, b3, wout, keep, right_ref, p0, p1, p2, p3, scratch, left_n, left_a
):
    g16 = gather_rows((b0, b1, b2, b3), scratch, D).astype(BF16)
    datt = dot_nt(g16, wout[...]).astype(BF16)
    bias = label_bias(keep[:, 5 * D :].astype(F32))
    _, dproj = attention(keep[...], bias, grad=datt, attended=keep[:, 3 * D : 4 * D])
    store_right(dproj, g16, right_ref)
    order = regroup(row_order(chip_first))
    left_n[...] = dot_nn(keep[:, 4 * D : 5 * D], order).astype(BF16)
    left_a[...] = dot_nn(keep[:, 3 * D : 4 * D], order).astype(BF16)
    pack(members_first(*here(me))[0], (left_n, left_a), right_ref, (p0, p1, p2, p3))


def first_rest(b0, b1, b2, b3, tok, gain, wqkv, right, tg_ref, result_ref, scratch):
    back = (b0, b1, b2, b3)
    put_field(gather_rows(back, scratch, 0), scratch, result_ref)
    _, xhat, rstd = norm_parts(take_field(tok, scratch), gain[...])
    g = gather_rows(back, scratch, D)
    dnormed = dot_nt(right[0], wqkv[:, :D])
    dnormed += dot_nt(right[1], wqkv[:, D : 2 * D])
    dnormed += dot_nt(right[2], wqkv[:, 2 * D :])
    put_field(norm_back(dnormed, gain[...], xhat, rstd, g), scratch, tg_ref)


def weights(member, p0, p1, p2, p3, q0, q1, q2, q3, scratch):
    total = jnp.zeros((D, WIDE), F32)
    for part in (p0, p1, p2, p3):
        total += dot_tn(part[:, :D], part[:, D:])
    scratch[...] = total
    for step, ref in enumerate((q0, q1, q2, q3)):
        first = pl.multiple_of((member ^ step) * PLANE_ROWS, PLANE_ROWS)
        ref[...] = scratch[pl.ds(first, PLANE_ROWS), :].astype(BF16)


def first_weights(me, *refs):
    weights(members_first(*here(me))[1], *refs)


def second_weights(me, *refs):
    weights(members_second(*here(me))[1], *refs)


PIECE = OWN * WIDE // LANES
SHEET = [(x, z) for x in range(X) for z in range(Z)]


def add_rows(a0, a1, a2, a3, b0, b1, b2, b3, out_ref, scratch):
    blocks = ((members_first, (a0, a1, a2, a3)), (members_second, (b0, b1, b2, b3)))
    for slot, (members, parts) in enumerate(blocks):
        total = sum(part[...].astype(F32) for part in parts)
        for peer, (x, z) in enumerate(SHEET):
            m1, _, m3 = members(x, 0, z)
            row = (m3 * GROUP + m1) * OWN
            for c in range(WIDE // LANES):
                first = slot * PIECE + c * OWN
                scratch[peer, first : first + OWN, :] = total[
                    row : row + OWN, c * LANES : (c + 1) * LANES
                ]
    out_ref[...] = scratch[...].astype(BF16)


def own_rows(parts, rows_ref, tile_ref):
    norm = jnp.zeros((1, 1), F32)
    for slot, members in enumerate((members_first, members_second)):
        totals = [jnp.zeros((PIECE, LANES), F32)] * GROUP
        for source, (x, z) in enumerate(SHEET):
            m1 = members(x, 0, z)[0]
            piece = parts[source, slot * PIECE : (slot + 1) * PIECE, :]
            totals[m1] = totals[m1] + piece.astype(F32)
        for m1, total in enumerate(totals):
            rows_ref[m1, slot * PIECE : (slot + 1) * PIECE, :] = total
        norm += jnp.sum(sum(total * total for total in totals), keepdims=True)
    tile_ref[...] = jnp.broadcast_to(norm[None], tile_ref.shape)


def clipped(tiles, rows, qkv_a, out_a, qkv_b, out_b):
    total = jnp.sum(tiles[...], 0)[:1, :1]
    factor = jnp.minimum(1.0, math.sqrt(8.0) * D / jnp.sqrt(total))
    for slot, refs in enumerate(((qkv_a, out_a), (qkv_b, out_b))):
        for k in range(GROUP):
            ref, column = (refs[0], k * WIDE) if k < GROUP - 1 else (refs[1], 0)
            for c in range(WIDE // LANES):
                first = slot * PIECE + c * OWN
                ref[:, column + c * LANES : column + (c + 1) * LANES] = (
                    rows[k, first : first + OWN, :] * factor
                )


def shape_of(*dims, dtype=BF16):
    return jax.ShapeDtypeStruct(dims, dtype)


def call(kernel, outs, scratch, *args, scalar=False, far=0):
    whole = pl.BlockSpec(memory_space=pltpu.VMEM)
    specs = [whole] * (len(args) - far) + [pl.BlockSpec(memory_space=pl.ANY)] * far
    if scalar:
        specs[0] = pl.BlockSpec(memory_space=pltpu.SMEM)
    scratch = [pltpu.VMEM(s, F32) if isinstance(s, tuple) else s for s in scratch]
    return pl.pallas_call(
        kernel,
        out_shape=outs,
        in_specs=specs,
        out_specs=[whole] * len(outs),
        scratch_shapes=scratch,
        compiler_params=pltpu.CompilerParams(vmem_limit_bytes=VMEM_BYTES),
        name=kernel.__name__,
    )(*args)


def in_vmem(*arrays):
    return [pltpu.with_memory_space_constraint(array, pltpu.VMEM) for array in arrays]


def in_hbm(*arrays):
    return [pltpu.with_memory_space_constraint(array, pltpu.HBM) for array in arrays]


def moves(lat_count, lon_count):
    tables = []
    for a in range(2):
        for b in range(2):
            table = []
            for i in range(lat_count):
                for j in range(lon_count):
                    ti = (i - (1 - a)) % lat_count
                    tj = (j - (1 - b)) % lon_count
                    table.append((i * lon_count + j, ti * lon_count + tj))
            tables.append(table)
    return tables


def send(parts, tables, back=False):
    out = list(parts)
    for slot in (2, 0, 1):
        pairs = [(t, s) for s, t in tables[slot]] if back else tables[slot]
        out[slot] = lax.ppermute(parts[slot], ("lat", "lon"), pairs)
    return out


def index_of(x, y, z):
    return (x * YLO + y % YLO) * LON + y // YLO * Z + z


CHIPS = [(x, y, z) for x in range(X) for y in range(Y) for z in range(Z)]


SHEETS = [[index_of(x, y, z) for x, z in SHEET] for y in range(Y)]


def swap(parts, members, chip, level, steps):
    out = list(parts)
    for step in steps:
        pairs = []
        for here_chip in CHIPS:
            numbers = list(members(*here_chip))
            numbers[level] ^= step
            pairs.append((index_of(*here_chip), index_of(*chip(*numbers))))
        out[step] = lax.ppermute(parts[step], ("lat", "lon"), pairs)
    return out


def swap_first(parts, level, steps):
    return swap(parts, members_first, chip_first, level, steps)


def swap_second(parts, level, steps):
    return swap(parts, members_second, chip_second, level, steps)


def exchange(parts, groups):
    return lax.all_to_all(parts, ("lat", "lon"), 0, 0, axis_index_groups=groups)


def after(value, earlier):
    return lax.optimization_barrier((value, earlier))[0]


def on_device(
    tokens,
    cotangent,
    region,
    unshifted_norm_gain,
    unshifted_query_key_value,
    out_first,
    shifted_norm_gain,
    shifted_query_key_value,
    out_second,
):
    tables = moves(LAT, LON)
    lat, lon = lax.axis_index("lat"), lax.axis_index("lon")
    me = (lat * LON + lon).astype(jnp.int32).reshape(1)
    gain_a = unshifted_norm_gain.reshape(1, D)
    gain_b = shifted_norm_gain.reshape(1, D)
    tok = tokens.transpose(1, 2, 0, 3)
    cot = cotangent.transpose(1, 2, 0, 3)
    lab = region.transpose(1, 0, 2)

    field = shape_of(TOK, D)
    fields = shape_of(GROUP, TOK, D)
    packs = [shape_of(TOK, D + WIDE)] * GROUP
    *x, keep = call(
        first_forward,
        [shape_of(QUART, SEND)] * 4 + [shape_of(TOK, 5 * D + LANES)],
        [
            (TOK, D),
            (TOK, LANES),
            pltpu.VMEM(tok.shape, BF16),
            (1, D),
            pltpu.VMEM(lab.shape, jnp.int32),
            pltpu.VMEM(cot.shape, BF16),
            pltpu.VMEM((D, 3 * D), BF16),
            pltpu.VMEM((D, D), BF16),
            pltpu.SemaphoreType.DMA((6,)),
        ],
        me, *in_hbm(tok, gain_a, lab, cot, unshifted_query_key_value, out_first),
        scalar=True, far=6,
    )
    x = send(x, tables)
    *back, normed_b, att_b, right_b = call(
        second_main,
        [shape_of(QUART, 2 * D)] * 4 + [field, field, fields],
        [(TOK, D), (TOK, LANES)],
        *x, gain_b, shifted_query_key_value, out_second,
    )
    back = send(back, tables, back=True)
    half = pltpu.VMEM((TOK, D), BF16)
    pack_b = call(
        second_pack, packs, [half, half], me, normed_b, att_b, right_b, scalar=True
    )
    pack_b = swap_second(after(pack_b, back[:3]), 0, (3, 1, 2))
    right_a, *pack_a = call(
        first_backward,
        [fields] + packs,
        [(TOK, D), half, half],
        me, *back, out_first, keep,
        scalar=True,
    )
    pack_a = swap_first(pack_a, 0, (3, 1, 2))
    grid = shape_of(WLAT, WLON, WLEV, D)
    token_gradient, result = call(
        first_rest,
        [grid, grid],
        [(TOK, D)],
        *back, tok, gain_a, unshifted_query_key_value, right_a,
    )
    token_gradient = token_gradient.transpose(2, 0, 1, 3)
    result = result.transpose(2, 0, 1, 3)

    rows = [shape_of(PLANE_ROWS, WIDE)] * GROUP
    sum_b = call(second_weights, rows, [(D, WIDE)], me, *in_vmem(*pack_b), scalar=True)
    sum_b = swap_second(sum_b, 1, (2, 1, 3))
    sum_a = call(first_weights, rows, [(D, WIDE)], me, *in_vmem(*pack_a), scalar=True)
    sum_a = swap_first(sum_a, 1, (1, 2, 3))
    piece = (len(SHEET), 2 * PIECE, LANES)
    (sums,) = call(add_rows, [shape_of(*piece)], [piece], *sum_a, *sum_b)
    sums = exchange(sums, SHEETS)
    mine, tiles = call(
        own_rows,
        [shape_of(GROUP, 2 * PIECE, LANES, dtype=F32), shape_of(LAT * LON, 1, LANES, dtype=F32)],
        [],
        sums,
    )
    tiles = lax.all_to_all(tiles, ("lat", "lon"), 0, 0)
    out_qkv, out_out = shape_of(OWN, 3 * D, dtype=F32), shape_of(OWN, D, dtype=F32)
    clips = call(clipped, [out_qkv, out_out] * 2, [], tiles, mine)
    return (result, token_gradient, *clips)


def solution(mesh):
    field = P("rep", "lat", "lon", None)
    rows = P(("rep", "lat", "lon"), None)
    in_specs = (field, field, P("rep", "lat", "lon"), P(), P(), P(), P(), P(), P())
    return jax.shard_map(
        on_device,
        mesh=mesh,
        in_specs=in_specs,
        out_specs=(field, field, rows, rows, rows, rows),
        check_vma=False,
    )
```

```python
import math

import jax
import jax.numpy as jnp
from jax import lax
from jax.experimental import pallas as pl
from jax.experimental.pallas import tpu as pltpu
from jax.sharding import PartitionSpec as P

D = 512
HEADS = 8
HEAD = 64
PAIRS = HEADS // 2
WLEV = 2
WLAT = 6
WLON = 12
HLAT = WLAT // 2
HLON = WLON // 2
TOK = WLEV * WLAT * WLON
QUART = TOK // 4
LANES = 128

X, YLO, YHI, Z = 4, 2, 2, 8
Y = YHI * YLO
LAT, LON = X * YLO, YHI * Z
OWN = D // (LAT * LON)
GROUP = 4
LAST = 8
WIDE = 4 * D // GROUP
PLANE_ROWS = D // GROUP
LAST_ROWS = PLANE_ROWS // LAST
SEND = 2 * D + LANES

EPSILON = 1e-05
NEGATIVE = -1e30
F32 = jnp.float32
BF16 = jnp.bfloat16
VMEM_BYTES = 16 * 1024 * 1024


def dot_nn(a, b):
    return lax.dot_general(a, b, (((1,), (0,)), ((), ())), preferred_element_type=F32)


def dot_nt(a, b):
    return lax.dot_general(a, b, (((1,), (1,)), ((), ())), preferred_element_type=F32)


def dot_tn(a, b):
    return lax.dot_general(a, b, (((0,), (0,)), ((), ())), preferred_element_type=F32)


def norm_parts(values, gain):
    average = jnp.mean(values, -1, keepdims=True)
    centered = values - average
    rstd = lax.rsqrt(jnp.mean(centered * centered, -1, keepdims=True) + EPSILON)
    xhat = centered * rstd
    return (xhat * gain).astype(BF16), xhat, rstd


def norm_back(dnormed, gain, xhat, rstd, incoming):
    s = dnormed * gain
    return (
        rstd * (s - jnp.mean(s, -1, keepdims=True) - xhat * jnp.mean(s * xhat, -1, keepdims=True))
        + incoming
    )


def label_bias(labels):
    lane = lax.broadcasted_iota(jnp.int32, (TOK, LANES), 1).astype(F32)
    hot = jnp.where((lane == labels) & (lane > 0.5), 1.0, 0.0).astype(BF16)
    return (1.0 - dot_nt(hot, hot)) * NEGATIVE


def pair_of(fields, part, pair):
    start = part * D + pair * LANES
    return fields[:, start : start + LANES]


def softmax_rows(scores):
    shifted = jnp.exp(scores - jnp.max(scores, -1, keepdims=True))
    return shifted * (1.0 / jnp.sum(shifted, -1, keepdims=True))


def attention(proj, bias, grad=None, attended=None):
    lane = lax.broadcasted_iota(jnp.int32, (1, LANES), 1)
    is_low = lane < HEAD
    low = is_low.astype(F32)
    masks = (low.astype(BF16), (1.0 - low).astype(BF16))
    bias = jnp.concatenate([bias, bias], 0)

    def stacked(field):
        return jnp.concatenate([field * masks[0], field * masks[1]], 0)

    def merged(both):
        return jnp.where(is_low, both[:TOK], both[TOK:])

    att, dq, dk, dv = [], [], [], []
    for pair in range(PAIRS):
        q = stacked(pair_of(proj, 0, pair) * BF16(HEAD**-0.5))
        k = pair_of(proj, 1, pair)
        v = pair_of(proj, 2, pair)
        probs = softmax_rows(dot_nt(q, k) + bias)
        p16 = probs.astype(BF16)
        if attended is None:
            o = merged(dot_nn(p16, v)).astype(BF16)
            att.append(o)
        else:
            o = pair_of(attended, 0, pair)
        if grad is not None:
            g = pair_of(grad, 0, pair)
            g_both = stacked(g)
            product = g.astype(F32) * o.astype(F32)
            delta = jnp.concatenate(
                [
                    jnp.sum(product * low, -1, keepdims=True),
                    jnp.sum(product * (1.0 - low), -1, keepdims=True),
                ],
                0,
            )
            ds16 = (probs * (dot_nt(g_both, v) - delta)).astype(BF16)
            dq.append((merged(dot_nn(ds16, k)) * HEAD**-0.5).astype(BF16))
            dk.append(dot_tn(ds16, q).astype(BF16))
            dv.append(dot_tn(p16, g_both).astype(BF16))
    if attended is None:
        attended = jnp.concatenate(att, -1)
    dproj = jnp.concatenate(dq + dk + dv, -1) if grad is not None else None
    return attended, dproj


def take_field(ref, scratch):
    half = HLON * WLEV
    for row in range(WLAT):
        values = ref[row].astype(F32).reshape(2 * half, D)
        for b in range(2):
            first = (2 * (row // HLAT) + b) * QUART + row % HLAT * half
            scratch[first : first + half, :] = values[b * half : (b + 1) * half]
    return scratch[...]


def put_field(values, scratch, ref):
    scratch[...] = values
    half = HLON * WLEV
    for row in range(WLAT):
        for b in range(2):
            first = (2 * (row // HLAT) + b) * QUART + row % HLAT * half
            ref[row, b * HLON : (b + 1) * HLON] = (
                scratch[first : first + half, :].reshape(HLON, WLEV, D).astype(BF16)
            )


def take_labels(region):
    places = WLAT * WLEV
    table = region[...].reshape(places, WLON).astype(F32)
    token = lax.broadcasted_iota(jnp.int32, (TOK, places), 0)
    slot, rest = token // QUART, token % QUART
    row = slot // 2 * HLAT + rest // (HLON * WLEV)
    column = slot % 2 * HLON + rest % (HLON * WLEV) // WLEV
    place = lax.broadcasted_iota(jnp.int32, (TOK, places), 1)
    rows = dot_nn((place == row * WLEV + rest % WLEV).astype(F32), table)
    return jnp.sum(jnp.where(place == column, rows, 0.0), -1, keepdims=True)


def gather_rows(refs, scratch, column):
    wide = scratch.shape[1]
    for slot, ref in enumerate(refs):
        scratch[slot * QUART : (slot + 1) * QUART, :] = ref[:, column : column + wide].astype(F32)
    return scratch[...]


def scatter_rows(values, scratch, refs, column):
    scratch[...] = values
    wide = scratch.shape[1]
    for slot, ref in enumerate(refs):
        ref[:, column : column + wide] = scratch[slot * QUART : (slot + 1) * QUART, :].astype(BF16)


def regroup(source_of):
    to = lax.broadcasted_iota(jnp.int32, (1, D), 1)
    return (lax.broadcasted_iota(jnp.int32, (D, D), 0) == source_of(to)).astype(F32).astype(BF16)


def squares(x, z):
    return (x & 1) + (z & 1) * 2, (x >> 1) + (z >> 1) * 2


def members_first(x, y, z):
    m1, m3 = squares(x, z)
    return m1, y, m3


def members_second(x, y, z):
    m1, m3 = squares(x + X - 1 & X - 1, z + Z - 1 & Z - 1)
    return m1, y, m3


def chip_first(m1, m2, m3):
    return (m1 & 1) + (m3 & 1) * 2, m2, (m1 >> 1) + (m3 >> 1) * 2


def chip_second(m1, m2, m3):
    x, y, z = chip_first(m1, m2, m3)
    return x + 1 & X - 1, y, z + 1 & Z - 1


def row_order(chip):
    def source_of(to):
        m1, m3, m2 = to // OWN % GROUP, to // (OWN * GROUP) % LAST, to // (OWN * GROUP * LAST)
        x, y, z = chip(m1, m2, m3)
        return (((x * YLO + y % YLO) * YHI + y // YLO) * Z + z) * OWN + to % OWN

    return source_of


def here(me):
    place = me[0]
    return place >> 5, (place >> 3 & 1) * 2 + (place >> 4 & 1), place & 7


def pack(me, left_refs, right_ref, packs):
    for step, ref in enumerate(packs):
        peer = me ^ step
        is_att = peer == GROUP - 1

        @pl.when(is_att)
        def _():
            ref[:, :D] = left_refs[1][...]

        @pl.when(jnp.logical_not(is_att))
        def _():
            ref[:, :D] = left_refs[0][...]

        ref[:, D:] = right_ref[peer]


def store_right(dproj, g16, right_ref):
    for part in range(3):
        right_ref[part] = dproj[:, part * D : (part + 1) * D]
    right_ref[3] = g16


def first_forward(
    me, tok_hbm, gain_hbm, region_hbm, cot_hbm, wqkv_hbm, wout_hbm,
    x0, x1, x2, x3, keep_ref, scratch, lab_scratch, tok, gain, region, cot, wqkv, wout, sems,
):
    far = (tok_hbm, gain_hbm, region_hbm, cot_hbm, wqkv_hbm, wout_hbm)
    copies = [
        pltpu.make_async_copy(source, target, sems.at[i])
        for i, (source, target) in enumerate(zip(far, (tok, gain, region, cot, wqkv, wout)))
    ]
    for copy in copies:
        copy.start()
    refs = (x0, x1, x2, x3)
    copies[0].wait()
    values = take_field(tok, scratch)
    copies[1].wait()
    normed, _, _ = norm_parts(values, gain[...])
    copies[2].wait()
    labels = jnp.broadcast_to(take_labels(region), (TOK, LANES))
    near = lax.broadcasted_iota(jnp.int32, (TOK, LANES), 0) < 2 * QUART
    moved = labels + jnp.where(near & (me[0] < LON), 4.0, 0.0)
    scatter_rows(moved, lab_scratch, refs, 2 * D)
    copies[3].wait()
    take_field(cot, scratch)
    for slot, ref in enumerate(refs):
        ref[:, D : 2 * D] = scratch[slot * QUART : (slot + 1) * QUART, :].astype(BF16)
    copies[4].wait()
    proj = dot_nn(normed, wqkv[...]).astype(BF16)
    keep_ref[:, : 3 * D] = proj
    keep_ref[:, 4 * D : 5 * D] = normed
    keep_ref[:, 5 * D :] = labels.astype(BF16)
    attended, _ = attention(proj, label_bias(labels))
    keep_ref[:, 3 * D : 4 * D] = attended
    copies[5].wait()
    scatter_rows(values + dot_nn(attended, wout[...]), scratch, refs, 0)


def second_main(
    x2, x0, x1, x3, gain, wqkv, wout,
    b0, b1, b2, b3, normed_ref, att_ref, right_ref, scratch, lab_scratch,
):
    parts = (x0, x1, x2, x3)
    back = (b0, b1, b2, b3)
    values = gather_rows(parts, scratch, 0)
    g = gather_rows(parts, scratch, D)
    labels = gather_rows(parts, lab_scratch, 2 * D)
    g16 = g.astype(BF16)
    normed, xhat, rstd = norm_parts(values, gain[...])
    normed_ref[...] = normed
    proj = dot_nn(normed, wqkv[...]).astype(BF16)
    datt = dot_nt(g16, wout[...]).astype(BF16)
    attended, dproj = attention(proj, label_bias(labels), grad=datt)
    att_ref[...] = attended
    store_right(dproj, g16, right_ref)
    scatter_rows(values + dot_nn(attended, wout[...]), scratch, back, 0)
    dnormed = dot_nt(dproj, wqkv[...])
    scatter_rows(norm_back(dnormed, gain[...], xhat, rstd, g), scratch, back, D)


def second_pack(me, normed, attended, right, p0, p1, p2, p3, left_n, left_a):
    order = regroup(row_order(chip_second))
    left_n[...] = dot_nn(normed[...], order).astype(BF16)
    left_a[...] = dot_nn(attended[...], order).astype(BF16)
    pack(members_second(*here(me))[0], (left_n, left_a), right, (p0, p1, p2, p3))


def first_backward(
    me, b2, b0, b1, b3, wout, keep, right_ref, p0, p1, p2, p3, scratch, left_n, left_a
):
    g16 = gather_rows((b0, b1, b2, b3), scratch, D).astype(BF16)
    datt = dot_nt(g16, wout[...]).astype(BF16)
    bias = label_bias(keep[:, 5 * D :].astype(F32))
    _, dproj = attention(keep[...], bias, grad=datt, attended=keep[:, 3 * D : 4 * D])
    store_right(dproj, g16, right_ref)
    order = regroup(row_order(chip_first))
    left_n[...] = dot_nn(keep[:, 4 * D : 5 * D], order).astype(BF16)
    left_a[...] = dot_nn(keep[:, 3 * D : 4 * D], order).astype(BF16)
    pack(members_first(*here(me))[0], (left_n, left_a), right_ref, (p0, p1, p2, p3))


def first_rest(b2, b0, b1, b3, tok, gain, wqkv, right, tg_ref, result_ref, scratch):
    back = (b0, b1, b2, b3)
    put_field(gather_rows(back, scratch, 0), scratch, result_ref)
    _, xhat, rstd = norm_parts(take_field(tok, scratch), gain[...])
    g = gather_rows(back, scratch, D)
    dnormed = dot_nt(right[0], wqkv[:, :D])
    dnormed += dot_nt(right[1], wqkv[:, D : 2 * D])
    dnormed += dot_nt(right[2], wqkv[:, 2 * D :])
    put_field(norm_back(dnormed, gain[...], xhat, rstd, g), scratch, tg_ref)


def weights(member, p0, p1, p2, p3, q0, q1, q2, q3, scratch):
    total = jnp.zeros((D, WIDE), F32)
    for part in (p0, p1, p2, p3):
        total += dot_tn(part[:, :D], part[:, D:])
    scratch[...] = total
    for step, ref in enumerate((q0, q1, q2, q3)):
        first = pl.multiple_of((member ^ step) * PLANE_ROWS, PLANE_ROWS)
        ref[...] = scratch[pl.ds(first, PLANE_ROWS), :].astype(BF16)


def first_weights(me, *refs):
    weights(members_first(*here(me))[1], *refs)


def second_weights(me, *refs):
    weights(members_second(*here(me))[1], *refs)


PIECE = OWN * WIDE // LANES
SHEET = [(x, z) for x in range(X) for z in range(Z)]


def add_rows(a0, a1, a2, a3, b0, b1, b2, b3, out_ref, scratch):
    blocks = ((members_first, (a0, a1, a2, a3)), (members_second, (b0, b1, b2, b3)))
    for slot, (members, parts) in enumerate(blocks):
        total = sum(part[...].astype(F32) for part in parts)
        for peer, (x, z) in enumerate(SHEET):
            m1, _, m3 = members(x, 0, z)
            row = (m3 * GROUP + m1) * OWN
            for c in range(WIDE // LANES):
                first = slot * PIECE + c * OWN
                scratch[peer, first : first + OWN, :] = total[
                    row : row + OWN, c * LANES : (c + 1) * LANES
                ]
    out_ref[...] = scratch[...].astype(BF16)


def own_rows(parts, rows_ref, tile_ref):
    norm = jnp.zeros((1, 1), F32)
    for slot, members in enumerate((members_first, members_second)):
        totals = [jnp.zeros((PIECE, LANES), F32)] * GROUP
        for source, (x, z) in enumerate(SHEET):
            m1 = members(x, 0, z)[0]
            piece = parts[source, slot * PIECE : (slot + 1) * PIECE, :]
            totals[m1] = totals[m1] + piece.astype(F32)
        for m1, total in enumerate(totals):
            rows_ref[m1, slot * PIECE : (slot + 1) * PIECE, :] = total
        norm += jnp.sum(sum(total * total for total in totals), keepdims=True)
    tile_ref[...] = jnp.broadcast_to(norm[None], tile_ref.shape)


def clipped(tiles, rows, qkv_a, out_a, qkv_b, out_b):
    total = jnp.sum(tiles[...], 0)[:1, :1]
    factor = jnp.minimum(1.0, math.sqrt(8.0) * D / jnp.sqrt(total))
    for slot, refs in enumerate(((qkv_a, out_a), (qkv_b, out_b))):
        for k in range(GROUP):
            ref, column = (refs[0], k * WIDE) if k < GROUP - 1 else (refs[1], 0)
            for c in range(WIDE // LANES):
                first = slot * PIECE + c * OWN
                ref[:, column + c * LANES : column + (c + 1) * LANES] = (
                    rows[k, first : first + OWN, :] * factor
                )


def shape_of(*dims, dtype=BF16):
    return jax.ShapeDtypeStruct(dims, dtype)


def call(kernel, outs, scratch, *args, scalar=False, far=0):
    whole = pl.BlockSpec(memory_space=pltpu.VMEM)
    specs = [whole] * (len(args) - far) + [pl.BlockSpec(memory_space=pl.ANY)] * far
    if scalar:
        specs[0] = pl.BlockSpec(memory_space=pltpu.SMEM)
    scratch = [pltpu.VMEM(s, F32) if isinstance(s, tuple) else s for s in scratch]
    return pl.pallas_call(
        kernel,
        out_shape=outs,
        in_specs=specs,
        out_specs=[whole] * len(outs),
        scratch_shapes=scratch,
        compiler_params=pltpu.CompilerParams(vmem_limit_bytes=VMEM_BYTES),
        name=kernel.__name__,
    )(*args)


def in_vmem(*arrays):
    return [pltpu.with_memory_space_constraint(array, pltpu.VMEM) for array in arrays]


def in_hbm(*arrays):
    return [pltpu.with_memory_space_constraint(array, pltpu.HBM) for array in arrays]


def moves(lat_count, lon_count):
    tables = []
    for a in range(2):
        for b in range(2):
            table = []
            for i in range(lat_count):
                for j in range(lon_count):
                    ti = (i - (1 - a)) % lat_count
                    tj = (j - (1 - b)) % lon_count
                    table.append((i * lon_count + j, ti * lon_count + tj))
            tables.append(table)
    return tables


def send(parts, tables, back=False):
    out = list(parts)
    for slot in range(3):
        pairs = [(t, s) for s, t in tables[slot]] if back else tables[slot]
        out[slot] = lax.ppermute(parts[slot], ("lat", "lon"), pairs)
    return out


def longest_first(parts):
    return [parts[slot] for slot in (2, 0, 1, 3)]


def two_hops_first(parts):
    return [parts[step] for step in (0, 3, 1, 2)]


def index_of(x, y, z):
    return (x * YLO + y % YLO) * LON + y // YLO * Z + z


CHIPS = [(x, y, z) for x in range(X) for y in range(Y) for z in range(Z)]


SHEETS = [[index_of(x, y, z) for x, z in SHEET] for y in range(Y)]


def swap(parts, members, chip, level, steps):
    out = list(parts)
    for step in steps:
        pairs = []
        for here_chip in CHIPS:
            numbers = list(members(*here_chip))
            numbers[level] ^= step
            pairs.append((index_of(*here_chip), index_of(*chip(*numbers))))
        out[step] = lax.ppermute(parts[step], ("lat", "lon"), pairs)
    return out


def swap_first(parts, level, steps):
    return swap(parts, members_first, chip_first, level, steps)


def swap_second(parts, level, steps):
    return swap(parts, members_second, chip_second, level, steps)


def exchange(parts, groups):
    return lax.all_to_all(parts, ("lat", "lon"), 0, 0, axis_index_groups=groups)


def after(value, earlier):
    return lax.optimization_barrier((value, earlier))[0]


def on_device(
    tokens,
    cotangent,
    region,
    unshifted_norm_gain,
    unshifted_query_key_value,
    out_first,
    shifted_norm_gain,
    shifted_query_key_value,
    out_second,
):
    tables = moves(LAT, LON)
    lat, lon = lax.axis_index("lat"), lax.axis_index("lon")
    me = (lat * LON + lon).astype(jnp.int32).reshape(1)
    gain_a = unshifted_norm_gain.reshape(1, D)
    gain_b = shifted_norm_gain.reshape(1, D)
    tok = tokens.transpose(1, 2, 0, 3)
    cot = cotangent.transpose(1, 2, 0, 3)
    lab = region.transpose(1, 0, 2)

    field = shape_of(TOK, D)
    fields = shape_of(GROUP, TOK, D)
    packs = [shape_of(TOK, D + WIDE)] * GROUP
    *x, keep = call(
        first_forward,
        [shape_of(QUART, SEND)] * 4 + [shape_of(TOK, 5 * D + LANES)],
        [
            (TOK, D),
            (TOK, LANES),
            pltpu.VMEM(tok.shape, BF16),
            (1, D),
            pltpu.VMEM(lab.shape, jnp.int32),
            pltpu.VMEM(cot.shape, BF16),
            pltpu.VMEM((D, 3 * D), BF16),
            pltpu.VMEM((D, D), BF16),
            pltpu.SemaphoreType.DMA((6,)),
        ],
        me, *in_hbm(tok, gain_a, lab, cot, unshifted_query_key_value, out_first),
        scalar=True, far=6,
    )
    x = send(x, tables)
    *back, normed_b, att_b, right_b = call(
        second_main,
        [shape_of(QUART, 2 * D)] * 4 + [field, field, fields],
        [(TOK, D), (TOK, LANES)],
        *longest_first(x), gain_b, shifted_query_key_value, out_second,
    )
    back = send(back, tables, back=True)
    half = pltpu.VMEM((TOK, D), BF16)
    pack_b = call(
        second_pack, packs, [half, half], me, normed_b, att_b, right_b, scalar=True
    )
    pack_b = swap_second(after(pack_b, back[:3]), 0, (3, 1, 2))
    right_a, *pack_a = call(
        first_backward,
        [fields] + packs,
        [(TOK, D), half, half],
        me, *longest_first(back), out_first, keep,
        scalar=True,
    )
    pack_a = swap_first(pack_a, 0, (3, 1, 2))
    grid = shape_of(WLAT, WLON, WLEV, D)
    token_gradient, result = call(
        first_rest,
        [grid, grid],
        [(TOK, D)],
        *longest_first(back), tok, gain_a, unshifted_query_key_value, right_a,
    )
    token_gradient = token_gradient.transpose(2, 0, 1, 3)
    result = result.transpose(2, 0, 1, 3)

    rows = [shape_of(PLANE_ROWS, WIDE)] * GROUP
    sum_b = call(second_weights, rows, [(D, WIDE)], me, *in_vmem(*two_hops_first(pack_b)), scalar=True)
    sum_b = swap_second(sum_b, 1, (2, 1, 3))
    sum_a = call(first_weights, rows, [(D, WIDE)], me, *in_vmem(*two_hops_first(pack_a)), scalar=True)
    sum_a = swap_first(sum_a, 1, (1, 2, 3))
    piece = (len(SHEET), 2 * PIECE, LANES)
    (sums,) = call(add_rows, [shape_of(*piece)], [piece], *sum_a, *sum_b)
    sums = exchange(sums, SHEETS)
    mine, tiles = call(
        own_rows,
        [shape_of(GROUP, 2 * PIECE, LANES, dtype=F32), shape_of(LAT * LON, 1, LANES, dtype=F32)],
        [],
        sums,
    )
    tiles = lax.all_to_all(tiles, ("lat", "lon"), 0, 0)
    out_qkv, out_out = shape_of(OWN, 3 * D, dtype=F32), shape_of(OWN, D, dtype=F32)
    clips = call(clipped, [out_qkv, out_out] * 2, [], tiles, mine)
    return (result, token_gradient, *clips)


def solution(mesh):
    field = P("rep", "lat", "lon", None)
    rows = P(("rep", "lat", "lon"), None)
    in_specs = (field, field, P("rep", "lat", "lon"), P(), P(), P(), P(), P(), P())
    return jax.shard_map(
        on_device,
        mesh=mesh,
        in_specs=in_specs,
        out_specs=(field, field, rows, rows, rows, rows),
        check_vma=False,
    )
```

```python
import math

import jax
import jax.numpy as jnp
from jax import lax
from jax.experimental import pallas as pl
from jax.experimental.pallas import tpu as pltpu
from jax.sharding import PartitionSpec as P

D = 512
HEADS = 8
HEAD = 64
PAIRS = HEADS // 2
WLEV = 2
WLAT = 6
WLON = 12
HLAT = WLAT // 2
HLON = WLON // 2
TOK = WLEV * WLAT * WLON
QUART = TOK // 4
LANES = 128

X, YLO, YHI, Z = 4, 2, 2, 8
Y = YHI * YLO
LAT, LON = X * YLO, YHI * Z
OWN = D // (LAT * LON)
GROUP = 4
LAST = 8
WIDE = 4 * D // GROUP
PLANE_ROWS = D // GROUP
LAST_ROWS = PLANE_ROWS // LAST
SEND = 2 * D + LANES

EPSILON = 1e-05
NEGATIVE = -1e30
F32 = jnp.float32
BF16 = jnp.bfloat16
VMEM_BYTES = 16 * 1024 * 1024


def dot_nn(a, b):
    return lax.dot_general(a, b, (((1,), (0,)), ((), ())), preferred_element_type=F32)


def dot_nt(a, b):
    return lax.dot_general(a, b, (((1,), (1,)), ((), ())), preferred_element_type=F32)


def dot_tn(a, b):
    return lax.dot_general(a, b, (((0,), (0,)), ((), ())), preferred_element_type=F32)


def norm_parts(values, gain):
    average = jnp.mean(values, -1, keepdims=True)
    centered = values - average
    rstd = lax.rsqrt(jnp.mean(centered * centered, -1, keepdims=True) + EPSILON)
    xhat = centered * rstd
    return (xhat * gain).astype(BF16), xhat, rstd


def norm_back(dnormed, gain, xhat, rstd, incoming):
    s = dnormed * gain
    return (
        rstd * (s - jnp.mean(s, -1, keepdims=True) - xhat * jnp.mean(s * xhat, -1, keepdims=True))
        + incoming
    )


def label_bias(labels):
    lane = lax.broadcasted_iota(jnp.int32, (TOK, LANES), 1).astype(F32)
    hot = jnp.where((lane == labels) & (lane > 0.5), 1.0, 0.0).astype(BF16)
    return (1.0 - dot_nt(hot, hot)) * NEGATIVE


def pair_of(fields, part, pair):
    start = part * D + pair * LANES
    return fields[:, start : start + LANES]


def softmax_rows(scores):
    shifted = jnp.exp(scores - jnp.max(scores, -1, keepdims=True))
    return shifted * (1.0 / jnp.sum(shifted, -1, keepdims=True))


def attention(proj, bias, grad=None, attended=None):
    lane = lax.broadcasted_iota(jnp.int32, (1, LANES), 1)
    is_low = lane < HEAD
    low = is_low.astype(F32)
    masks = (low.astype(BF16), (1.0 - low).astype(BF16))
    bias = jnp.concatenate([bias, bias], 0)

    def stacked(field):
        return jnp.concatenate([field * masks[0], field * masks[1]], 0)

    def merged(both):
        return jnp.where(is_low, both[:TOK], both[TOK:])

    att, dq, dk, dv = [], [], [], []
    for pair in range(PAIRS):
        q = stacked(pair_of(proj, 0, pair) * BF16(HEAD**-0.5))
        k = pair_of(proj, 1, pair)
        v = pair_of(proj, 2, pair)
        probs = softmax_rows(dot_nt(q, k) + bias)
        p16 = probs.astype(BF16)
        if attended is None:
            o = merged(dot_nn(p16, v)).astype(BF16)
            att.append(o)
        else:
            o = pair_of(attended, 0, pair)
        if grad is not None:
            g = pair_of(grad, 0, pair)
            g_both = stacked(g)
            product = g.astype(F32) * o.astype(F32)
            delta = jnp.concatenate(
                [
                    jnp.sum(product * low, -1, keepdims=True),
                    jnp.sum(product * (1.0 - low), -1, keepdims=True),
                ],
                0,
            )
            ds16 = (probs * (dot_nt(g_both, v) - delta)).astype(BF16)
            dq.append((merged(dot_nn(ds16, k)) * HEAD**-0.5).astype(BF16))
            dk.append(dot_tn(ds16, q).astype(BF16))
            dv.append(dot_tn(p16, g_both).astype(BF16))
    if attended is None:
        attended = jnp.concatenate(att, -1)
    dproj = jnp.concatenate(dq + dk + dv, -1) if grad is not None else None
    return attended, dproj


def take_field(ref, scratch):
    half = HLON * WLEV
    for row in range(WLAT):
        values = ref[row].astype(F32).reshape(2 * half, D)
        for b in range(2):
            first = (2 * (row // HLAT) + b) * QUART + row % HLAT * half
            scratch[first : first + half, :] = values[b * half : (b + 1) * half]
    return scratch[...]


def put_field(values, scratch, ref):
    scratch[...] = values
    half = HLON * WLEV
    for row in range(WLAT):
        for b in range(2):
            first = (2 * (row // HLAT) + b) * QUART + row % HLAT * half
            ref[row, b * HLON : (b + 1) * HLON] = (
                scratch[first : first + half, :].reshape(HLON, WLEV, D).astype(BF16)
            )


def take_labels(region):
    places = WLAT * WLEV
    table = region[...].reshape(places, WLON).astype(F32)
    token = lax.broadcasted_iota(jnp.int32, (TOK, places), 0)
    slot, rest = token // QUART, token % QUART
    row = slot // 2 * HLAT + rest // (HLON * WLEV)
    column = slot % 2 * HLON + rest % (HLON * WLEV) // WLEV
    place = lax.broadcasted_iota(jnp.int32, (TOK, places), 1)
    rows = dot_nn((place == row * WLEV + rest % WLEV).astype(F32), table)
    return jnp.sum(jnp.where(place == column, rows, 0.0), -1, keepdims=True)


def gather_rows(refs, scratch, column):
    wide = scratch.shape[1]
    for slot, ref in enumerate(refs):
        scratch[slot * QUART : (slot + 1) * QUART, :] = ref[:, column : column + wide].astype(F32)
    return scratch[...]


def scatter_rows(values, scratch, refs, column):
    scratch[...] = values
    wide = scratch.shape[1]
    for slot, ref in enumerate(refs):
        ref[:, column : column + wide] = scratch[slot * QUART : (slot + 1) * QUART, :].astype(BF16)


def regroup(source_of):
    to = lax.broadcasted_iota(jnp.int32, (1, D), 1)
    return (lax.broadcasted_iota(jnp.int32, (D, D), 0) == source_of(to)).astype(F32).astype(BF16)


def squares(x, z):
    return (x & 1) + (z & 1) * 2, (x >> 1) + (z >> 1) * 2


def members_first(x, y, z):
    m1, m3 = squares(x, z)
    return m1, y, m3


def members_second(x, y, z):
    m1, m3 = squares(x + X - 1 & X - 1, z + Z - 1 & Z - 1)
    return m1, y, m3


def chip_first(m1, m2, m3):
    return (m1 & 1) + (m3 & 1) * 2, m2, (m1 >> 1) + (m3 >> 1) * 2


def chip_second(m1, m2, m3):
    x, y, z = chip_first(m1, m2, m3)
    return x + 1 & X - 1, y, z + 1 & Z - 1


def row_order(chip):
    def source_of(to):
        m1, m3, m2 = to // OWN % GROUP, to // (OWN * GROUP) % LAST, to // (OWN * GROUP * LAST)
        x, y, z = chip(m1, m2, m3)
        return (((x * YLO + y % YLO) * YHI + y // YLO) * Z + z) * OWN + to % OWN

    return source_of


def here(me):
    place = me[0]
    return place >> 5, (place >> 3 & 1) * 2 + (place >> 4 & 1), place & 7


def pack(me, left_refs, right_ref, packs):
    for step, ref in enumerate(packs):
        peer = me ^ step
        is_att = peer == GROUP - 1

        @pl.when(is_att)
        def _():
            ref[:, :D] = left_refs[1][...]

        @pl.when(jnp.logical_not(is_att))
        def _():
            ref[:, :D] = left_refs[0][...]

        ref[:, D:] = right_ref[peer]


def store_right(dproj, g16, right_ref):
    for part in range(3):
        right_ref[part] = dproj[:, part * D : (part + 1) * D]
    right_ref[3] = g16


def first_forward(
    me, tok_hbm, gain_hbm, region_hbm, cot_hbm, wqkv_hbm, wout_hbm,
    x0, x1, x2, x3, keep_ref, scratch, lab_scratch, tok, gain, region, cot, wqkv, wout, sems,
):
    far = (tok_hbm, gain_hbm, region_hbm, cot_hbm, wqkv_hbm, wout_hbm)
    copies = [
        pltpu.make_async_copy(source, target, sems.at[i])
        for i, (source, target) in enumerate(zip(far, (tok, gain, region, cot, wqkv, wout)))
    ]
    for copy in copies:
        copy.start()
    refs = (x0, x1, x2, x3)
    copies[0].wait()
    values = take_field(tok, scratch)
    copies[1].wait()
    normed, _, _ = norm_parts(values, gain[...])
    copies[2].wait()
    labels = jnp.broadcast_to(take_labels(region), (TOK, LANES))
    near = lax.broadcasted_iota(jnp.int32, (TOK, LANES), 0) < 2 * QUART
    moved = labels + jnp.where(near & (me[0] < LON), 4.0, 0.0)
    scatter_rows(moved, lab_scratch, refs, 2 * D)
    copies[3].wait()
    take_field(cot, scratch)
    for slot, ref in enumerate(refs):
        ref[:, D : 2 * D] = scratch[slot * QUART : (slot + 1) * QUART, :].astype(BF16)
    copies[4].wait()
    proj = dot_nn(normed, wqkv[...]).astype(BF16)
    keep_ref[:, : 3 * D] = proj
    keep_ref[:, 4 * D : 5 * D] = normed
    keep_ref[:, 5 * D :] = labels.astype(BF16)
    attended, _ = attention(proj, label_bias(labels))
    keep_ref[:, 3 * D : 4 * D] = attended
    copies[5].wait()
    scatter_rows(values + dot_nn(attended, wout[...]), scratch, refs, 0)


def second_main(
    x2, x0, x1, x3, gain, wqkv, wout,
    b0, b1, b2, b3, normed_ref, att_ref, right_ref, scratch, lab_scratch,
):
    parts = (x0, x1, x2, x3)
    back = (b0, b1, b2, b3)
    values = gather_rows(parts, scratch, 0)
    g = gather_rows(parts, scratch, D)
    labels = gather_rows(parts, lab_scratch, 2 * D)
    g16 = g.astype(BF16)
    normed, xhat, rstd = norm_parts(values, gain[...])
    normed_ref[...] = normed
    proj = dot_nn(normed, wqkv[...]).astype(BF16)
    datt = dot_nt(g16, wout[...]).astype(BF16)
    attended, dproj = attention(proj, label_bias(labels), grad=datt)
    att_ref[...] = attended
    store_right(dproj, g16, right_ref)
    scatter_rows(values + dot_nn(attended, wout[...]), scratch, back, 0)
    dnormed = dot_nt(dproj, wqkv[...])
    scatter_rows(norm_back(dnormed, gain[...], xhat, rstd, g), scratch, back, D)


def second_pack(me, normed, attended, right, p0, p1, p2, p3, left_n, left_a):
    order = regroup(row_order(chip_second))
    left_n[...] = dot_nn(normed[...], order).astype(BF16)
    left_a[...] = dot_nn(attended[...], order).astype(BF16)
    pack(members_second(*here(me))[0], (left_n, left_a), right, (p0, p1, p2, p3))


def first_backward(
    me, b0, b1, b2, b3, wout, keep, right_ref, p0, p1, p2, p3, scratch, left_n, left_a
):
    g16 = gather_rows((b0, b1, b2, b3), scratch, D).astype(BF16)
    datt = dot_nt(g16, wout[...]).astype(BF16)
    bias = label_bias(keep[:, 5 * D :].astype(F32))
    _, dproj = attention(keep[...], bias, grad=datt, attended=keep[:, 3 * D : 4 * D])
    store_right(dproj, g16, right_ref)
    order = regroup(row_order(chip_first))
    left_n[...] = dot_nn(keep[:, 4 * D : 5 * D], order).astype(BF16)
    left_a[...] = dot_nn(keep[:, 3 * D : 4 * D], order).astype(BF16)
    pack(members_first(*here(me))[0], (left_n, left_a), right_ref, (p0, p1, p2, p3))


def first_rest(b0, b1, b2, b3, tok, gain, wqkv, right, tg_ref, result_ref, scratch):
    back = (b0, b1, b2, b3)
    put_field(gather_rows(back, scratch, 0), scratch, result_ref)
    _, xhat, rstd = norm_parts(take_field(tok, scratch), gain[...])
    g = gather_rows(back, scratch, D)
    dnormed = dot_nt(right[0], wqkv[:, :D])
    dnormed += dot_nt(right[1], wqkv[:, D : 2 * D])
    dnormed += dot_nt(right[2], wqkv[:, 2 * D :])
    put_field(norm_back(dnormed, gain[...], xhat, rstd, g), scratch, tg_ref)


def weights(member, p0, p1, p2, p3, q0, q1, q2, q3, scratch):
    total = jnp.zeros((D, WIDE), F32)
    for part in (p0, p1, p2, p3):
        total += dot_tn(part[:, :D], part[:, D:])
    scratch[...] = total
    for step, ref in enumerate((q0, q1, q2, q3)):
        first = pl.multiple_of((member ^ step) * PLANE_ROWS, PLANE_ROWS)
        ref[...] = scratch[pl.ds(first, PLANE_ROWS), :].astype(BF16)


def first_weights(me, *refs):
    weights(members_first(*here(me))[1], *refs)


def second_weights(me, *refs):
    weights(members_second(*here(me))[1], *refs)


PIECE = OWN * WIDE // LANES
SHEET = [(x, z) for x in range(X) for z in range(Z)]


def add_rows(a0, a1, a2, a3, b0, b1, b2, b3, out_ref, scratch):
    blocks = ((members_first, (a0, a1, a2, a3)), (members_second, (b0, b1, b2, b3)))
    for slot, (members, parts) in enumerate(blocks):
        total = sum(part[...].astype(F32) for part in parts)
        for peer, (x, z) in enumerate(SHEET):
            m1, _, m3 = members(x, 0, z)
            row = (m3 * GROUP + m1) * OWN
            for c in range(WIDE // LANES):
                first = slot * PIECE + c * OWN
                scratch[peer, first : first + OWN, :] = total[
                    row : row + OWN, c * LANES : (c + 1) * LANES
                ]
    out_ref[...] = scratch[...].astype(BF16)


def own_rows(parts, rows_ref, tile_ref):
    norm = jnp.zeros((1, 1), F32)
    for slot, members in enumerate((members_first, members_second)):
        totals = [jnp.zeros((PIECE, LANES), F32)] * GROUP
        for source, (x, z) in enumerate(SHEET):
            m1 = members(x, 0, z)[0]
            piece = parts[source, slot * PIECE : (slot + 1) * PIECE, :]
            totals[m1] = totals[m1] + piece.astype(F32)
        for m1, total in enumerate(totals):
            rows_ref[m1, slot * PIECE : (slot + 1) * PIECE, :] = total
        norm += jnp.sum(sum(total * total for total in totals), keepdims=True)
    tile_ref[...] = jnp.broadcast_to(norm[None], tile_ref.shape)


def clipped(tiles, rows, qkv_a, out_a, qkv_b, out_b):
    total = jnp.sum(tiles[...], 0)[:1, :1]
    factor = jnp.minimum(1.0, math.sqrt(8.0) * D / jnp.sqrt(total))
    for slot, refs in enumerate(((qkv_a, out_a), (qkv_b, out_b))):
        for k in range(GROUP):
            ref, column = (refs[0], k * WIDE) if k < GROUP - 1 else (refs[1], 0)
            for c in range(WIDE // LANES):
                first = slot * PIECE + c * OWN
                ref[:, column + c * LANES : column + (c + 1) * LANES] = (
                    rows[k, first : first + OWN, :] * factor
                )


def shape_of(*dims, dtype=BF16):
    return jax.ShapeDtypeStruct(dims, dtype)


def call(kernel, outs, scratch, *args, scalar=False, far=0):
    whole = pl.BlockSpec(memory_space=pltpu.VMEM)
    specs = [whole] * (len(args) - far) + [pl.BlockSpec(memory_space=pl.ANY)] * far
    if scalar:
        specs[0] = pl.BlockSpec(memory_space=pltpu.SMEM)
    scratch = [pltpu.VMEM(s, F32) if isinstance(s, tuple) else s for s in scratch]
    return pl.pallas_call(
        kernel,
        out_shape=outs,
        in_specs=specs,
        out_specs=[whole] * len(outs),
        scratch_shapes=scratch,
        compiler_params=pltpu.CompilerParams(vmem_limit_bytes=VMEM_BYTES),
        name=kernel.__name__,
    )(*args)


def in_vmem(*arrays):
    return [pltpu.with_memory_space_constraint(array, pltpu.VMEM) for array in arrays]


def in_hbm(*arrays):
    return [pltpu.with_memory_space_constraint(array, pltpu.HBM) for array in arrays]


def moves(lat_count, lon_count):
    tables = []
    for a in range(2):
        for b in range(2):
            table = []
            for i in range(lat_count):
                for j in range(lon_count):
                    ti = (i - (1 - a)) % lat_count
                    tj = (j - (1 - b)) % lon_count
                    table.append((i * lon_count + j, ti * lon_count + tj))
            tables.append(table)
    return tables


def send(parts, tables, back=False):
    out = list(parts)
    for slot in (2, 0, 1):
        pairs = [(t, s) for s, t in tables[slot]] if back else tables[slot]
        out[slot] = lax.ppermute(parts[slot], ("lat", "lon"), pairs)
    return out


def index_of(x, y, z):
    return (x * YLO + y % YLO) * LON + y // YLO * Z + z


CHIPS = [(x, y, z) for x in range(X) for y in range(Y) for z in range(Z)]


SHEETS = [[index_of(x, y, z) for x, z in SHEET] for y in range(Y)]


def swap(parts, members, chip, level, steps):
    out = list(parts)
    for step in steps:
        pairs = []
        for here_chip in CHIPS:
            numbers = list(members(*here_chip))
            numbers[level] ^= step
            pairs.append((index_of(*here_chip), index_of(*chip(*numbers))))
        out[step] = lax.ppermute(parts[step], ("lat", "lon"), pairs)
    return out


def swap_first(parts, level, steps):
    return swap(parts, members_first, chip_first, level, steps)


def swap_second(parts, level, steps):
    return swap(parts, members_second, chip_second, level, steps)


def exchange(parts, groups):
    return lax.all_to_all(parts, ("lat", "lon"), 0, 0, axis_index_groups=groups)


def after(value, earlier):
    return lax.optimization_barrier((value, earlier))[0]


def on_device(
    tokens,
    cotangent,
    region,
    unshifted_norm_gain,
    unshifted_query_key_value,
    out_first,
    shifted_norm_gain,
    shifted_query_key_value,
    out_second,
):
    tables = moves(LAT, LON)
    lat, lon = lax.axis_index("lat"), lax.axis_index("lon")
    me = (lat * LON + lon).astype(jnp.int32).reshape(1)
    gain_a = unshifted_norm_gain.reshape(1, D)
    gain_b = shifted_norm_gain.reshape(1, D)
    tok = tokens.transpose(1, 2, 0, 3)
    cot = cotangent.transpose(1, 2, 0, 3)
    lab = region.transpose(1, 0, 2)

    field = shape_of(TOK, D)
    fields = shape_of(GROUP, TOK, D)
    packs = [shape_of(TOK, D + WIDE)] * GROUP
    *x, keep = call(
        first_forward,
        [shape_of(QUART, SEND)] * 4 + [shape_of(TOK, 5 * D + LANES)],
        [
            (TOK, D),
            (TOK, LANES),
            pltpu.VMEM(tok.shape, BF16),
            (1, D),
            pltpu.VMEM(lab.shape, jnp.int32),
            pltpu.VMEM(cot.shape, BF16),
            pltpu.VMEM((D, 3 * D), BF16),
            pltpu.VMEM((D, D), BF16),
            pltpu.SemaphoreType.DMA((6,)),
        ],
        me, *in_hbm(tok, gain_a, lab, cot, unshifted_query_key_value, out_first),
        scalar=True, far=6,
    )
    x = send(x, tables)
    *back, normed_b, att_b, right_b = call(
        second_main,
        [shape_of(QUART, 2 * D)] * 4 + [field, field, fields],
        [(TOK, D), (TOK, LANES)],
        x[2], x[0], x[1], x[3], gain_b, shifted_query_key_value, out_second,
    )
    back = send(back, tables, back=True)
    half = pltpu.VMEM((TOK, D), BF16)
    pack_b = call(
        second_pack, packs, [half, half], me, normed_b, att_b, right_b, scalar=True
    )
    pack_b = swap_second(after(pack_b, back[:3]), 0, (3, 1, 2))
    right_a, *pack_a = call(
        first_backward,
        [fields] + packs,
        [(TOK, D), half, half],
        me, *back, out_first, keep,
        scalar=True,
    )
    pack_a = swap_first(pack_a, 0, (3, 1, 2))
    grid = shape_of(WLAT, WLON, WLEV, D)
    token_gradient, result = call(
        first_rest,
        [grid, grid],
        [(TOK, D)],
        *back, tok, gain_a, unshifted_query_key_value, right_a,
    )
    token_gradient = token_gradient.transpose(2, 0, 1, 3)
    result = result.transpose(2, 0, 1, 3)

    rows = [shape_of(PLANE_ROWS, WIDE)] * GROUP
    sum_b = call(second_weights, rows, [(D, WIDE)], me, *in_vmem(*pack_b), scalar=True)
    sum_b = swap_second(sum_b, 1, (2, 1, 3))
    sum_a = call(first_weights, rows, [(D, WIDE)], me, *in_vmem(*pack_a), scalar=True)
    sum_a = swap_first(sum_a, 1, (1, 2, 3))
    piece = (len(SHEET), 2 * PIECE, LANES)
    (sums,) = call(add_rows, [shape_of(*piece)], [piece], *sum_a, *sum_b)
    sums = exchange(sums, SHEETS)
    mine, tiles = call(
        own_rows,
        [shape_of(GROUP, 2 * PIECE, LANES, dtype=F32), shape_of(LAT * LON, 1, LANES, dtype=F32)],
        [],
        sums,
    )
    tiles = lax.all_to_all(tiles, ("lat", "lon"), 0, 0)
    out_qkv, out_out = shape_of(OWN, 3 * D, dtype=F32), shape_of(OWN, D, dtype=F32)
    clips = call(clipped, [out_qkv, out_out] * 2, [], tiles, mine)
    return (result, token_gradient, *clips)


def solution(mesh):
    field = P("rep", "lat", "lon", None)
    rows = P(("rep", "lat", "lon"), None)
    in_specs = (field, field, P("rep", "lat", "lon"), P(), P(), P(), P(), P(), P())
    return jax.shard_map(
        on_device,
        mesh=mesh,
        in_specs=in_specs,
        out_specs=(field, field, rows, rows, rows, rows),
        check_vma=False,
    )
```

```python
import math

import jax
import jax.numpy as jnp
from jax import lax
from jax.experimental import pallas as pl
from jax.experimental.pallas import tpu as pltpu
from jax.sharding import PartitionSpec as P

D = 512
HEADS = 8
HEAD = 64
PAIRS = HEADS // 2
WLEV = 2
WLAT = 6
WLON = 12
HLAT = WLAT // 2
HLON = WLON // 2
TOK = WLEV * WLAT * WLON
QUART = TOK // 4
LANES = 128

X, YLO, YHI, Z = 4, 2, 2, 8
Y = YHI * YLO
LAT, LON = X * YLO, YHI * Z
OWN = D // (LAT * LON)
GROUP = 4
LAST = 8
WIDE = 4 * D // GROUP
PLANE_ROWS = D // GROUP
LAST_ROWS = PLANE_ROWS // LAST
SEND = 2 * D + LANES

EPSILON = 1e-05
NEGATIVE = -1e30
F32 = jnp.float32
BF16 = jnp.bfloat16
VMEM_BYTES = 16 * 1024 * 1024


def dot_nn(a, b):
    return lax.dot_general(a, b, (((1,), (0,)), ((), ())), preferred_element_type=F32)


def dot_nt(a, b):
    return lax.dot_general(a, b, (((1,), (1,)), ((), ())), preferred_element_type=F32)


def dot_tn(a, b):
    return lax.dot_general(a, b, (((0,), (0,)), ((), ())), preferred_element_type=F32)


def norm_parts(values, gain):
    average = jnp.mean(values, -1, keepdims=True)
    centered = values - average
    rstd = lax.rsqrt(jnp.mean(centered * centered, -1, keepdims=True) + EPSILON)
    xhat = centered * rstd
    return (xhat * gain).astype(BF16), xhat, rstd


def norm_back(dnormed, gain, xhat, rstd, incoming):
    s = dnormed * gain
    return (
        rstd * (s - jnp.mean(s, -1, keepdims=True) - xhat * jnp.mean(s * xhat, -1, keepdims=True))
        + incoming
    )


def label_bias(labels):
    lane = lax.broadcasted_iota(jnp.int32, (TOK, LANES), 1).astype(F32)
    hot = jnp.where((lane == labels) & (lane > 0.5), 1.0, 0.0).astype(BF16)
    return (1.0 - dot_nt(hot, hot)) * NEGATIVE


def pair_of(fields, part, pair):
    start = part * D + pair * LANES
    return fields[:, start : start + LANES]


def softmax_rows(scores):
    shifted = jnp.exp(scores - jnp.max(scores, -1, keepdims=True))
    return shifted * (1.0 / jnp.sum(shifted, -1, keepdims=True))


def attention(proj, bias, grad=None, attended=None):
    lane = lax.broadcasted_iota(jnp.int32, (1, LANES), 1)
    is_low = lane < HEAD
    low = is_low.astype(F32)
    masks = (low.astype(BF16), (1.0 - low).astype(BF16))
    bias = jnp.concatenate([bias, bias], 0)

    def stacked(field):
        return jnp.concatenate([field * masks[0], field * masks[1]], 0)

    def merged(both):
        return jnp.where(is_low, both[:TOK], both[TOK:])

    att, dq, dk, dv = [], [], [], []
    for pair in range(PAIRS):
        q = stacked(pair_of(proj, 0, pair) * BF16(HEAD**-0.5))
        k = pair_of(proj, 1, pair)
        v = pair_of(proj, 2, pair)
        probs = softmax_rows(dot_nt(q, k) + bias)
        p16 = probs.astype(BF16)
        if attended is None:
            o = merged(dot_nn(p16, v)).astype(BF16)
            att.append(o)
        else:
            o = pair_of(attended, 0, pair)
        if grad is not None:
            g = pair_of(grad, 0, pair)
            g_both = stacked(g)
            product = g.astype(F32) * o.astype(F32)
            delta = jnp.concatenate(
                [
                    jnp.sum(product * low, -1, keepdims=True),
                    jnp.sum(product * (1.0 - low), -1, keepdims=True),
                ],
                0,
            )
            ds16 = (probs * (dot_nt(g_both, v) - delta)).astype(BF16)
            dq.append((merged(dot_nn(ds16, k)) * HEAD**-0.5).astype(BF16))
            dk.append(dot_tn(ds16, q).astype(BF16))
            dv.append(dot_tn(p16, g_both).astype(BF16))
    if attended is None:
        attended = jnp.concatenate(att, -1)
    dproj = jnp.concatenate(dq + dk + dv, -1) if grad is not None else None
    return attended, dproj


def take_field(ref, scratch):
    half = HLON * WLEV
    for row in range(WLAT):
        values = ref[row].astype(F32).reshape(2 * half, D)
        for b in range(2):
            first = (2 * (row // HLAT) + b) * QUART + row % HLAT * half
            scratch[first : first + half, :] = values[b * half : (b + 1) * half]
    return scratch[...]


def put_field(values, scratch, ref):
    scratch[...] = values
    half = HLON * WLEV
    for row in range(WLAT):
        for b in range(2):
            first = (2 * (row // HLAT) + b) * QUART + row % HLAT * half
            ref[row, b * HLON : (b + 1) * HLON] = (
                scratch[first : first + half, :].reshape(HLON, WLEV, D).astype(BF16)
            )


def take_labels(region):
    places = WLAT * WLEV
    table = region[...].reshape(places, WLON).astype(F32)
    token = lax.broadcasted_iota(jnp.int32, (TOK, places), 0)
    slot, rest = token // QUART, token % QUART
    row = slot // 2 * HLAT + rest // (HLON * WLEV)
    column = slot % 2 * HLON + rest % (HLON * WLEV) // WLEV
    place = lax.broadcasted_iota(jnp.int32, (TOK, places), 1)
    rows = dot_nn((place == row * WLEV + rest % WLEV).astype(F32), table)
    return jnp.sum(jnp.where(place == column, rows, 0.0), -1, keepdims=True)


def gather_rows(refs, scratch, column):
    wide = scratch.shape[1]
    for slot, ref in enumerate(refs):
        scratch[slot * QUART : (slot + 1) * QUART, :] = ref[:, column : column + wide].astype(F32)
    return scratch[...]


def scatter_rows(values, scratch, refs, column):
    scratch[...] = values
    wide = scratch.shape[1]
    for slot, ref in enumerate(refs):
        ref[:, column : column + wide] = scratch[slot * QUART : (slot + 1) * QUART, :].astype(BF16)


def regroup(source_of):
    to = lax.broadcasted_iota(jnp.int32, (1, D), 1)
    return (lax.broadcasted_iota(jnp.int32, (D, D), 0) == source_of(to)).astype(F32).astype(BF16)


def squares(x, z):
    return (x & 1) + (z & 1) * 2, (x >> 1) + (z >> 1) * 2


def members_first(x, y, z):
    m1, m3 = squares(x, z)
    return m1, y, m3


def members_second(x, y, z):
    m1, m3 = squares(x + X - 1 & X - 1, z + Z - 1 & Z - 1)
    return m1, y, m3


def chip_first(m1, m2, m3):
    return (m1 & 1) + (m3 & 1) * 2, m2, (m1 >> 1) + (m3 >> 1) * 2


def chip_second(m1, m2, m3):
    x, y, z = chip_first(m1, m2, m3)
    return x + 1 & X - 1, y, z + 1 & Z - 1


def row_order(chip):
    def source_of(to):
        m1, m3, m2 = to // OWN % GROUP, to // (OWN * GROUP) % LAST, to // (OWN * GROUP * LAST)
        x, y, z = chip(m1, m2, m3)
        return (((x * YLO + y % YLO) * YHI + y // YLO) * Z + z) * OWN + to % OWN

    return source_of


def here(me):
    place = me[0]
    return place >> 5, (place >> 3 & 1) * 2 + (place >> 4 & 1), place & 7


def pack(me, left_refs, right_ref, packs):
    for step, ref in enumerate(packs):
        peer = me ^ step
        is_att = peer == GROUP - 1

        @pl.when(is_att)
        def _():
            ref[:, :D] = left_refs[1][...]

        @pl.when(jnp.logical_not(is_att))
        def _():
            ref[:, :D] = left_refs[0][...]

        ref[:, D:] = right_ref[peer]


def store_right(dproj, g16, right_ref):
    for part in range(3):
        right_ref[part] = dproj[:, part * D : (part + 1) * D]
    right_ref[3] = g16


def first_forward(
    me, tok_hbm, gain_hbm, region_hbm, cot_hbm, wqkv_hbm, wout_hbm,
    x0, x1, x2, x3, keep_ref, scratch, lab_scratch, tok, gain, region, cot, wqkv, wout, sems,
):
    far = (tok_hbm, gain_hbm, region_hbm, cot_hbm, wqkv_hbm, wout_hbm)
    copies = [
        pltpu.make_async_copy(source, target, sems.at[i])
        for i, (source, target) in enumerate(zip(far, (tok, gain, region, cot, wqkv, wout)))
    ]
    for copy in copies:
        copy.start()
    refs = (x0, x1, x2, x3)
    copies[0].wait()
    values = take_field(tok, scratch)
    copies[1].wait()
    normed, _, _ = norm_parts(values, gain[...])
    copies[2].wait()
    labels = jnp.broadcast_to(take_labels(region), (TOK, LANES))
    near = lax.broadcasted_iota(jnp.int32, (TOK, LANES), 0) < 2 * QUART
    moved = labels + jnp.where(near & (me[0] < LON), 4.0, 0.0)
    scatter_rows(moved, lab_scratch, refs, 2 * D)
    copies[3].wait()
    take_field(cot, scratch)
    for slot, ref in enumerate(refs):
        ref[:, D : 2 * D] = scratch[slot * QUART : (slot + 1) * QUART, :].astype(BF16)
    copies[4].wait()
    proj = dot_nn(normed, wqkv[...]).astype(BF16)
    keep_ref[:, : 3 * D] = proj
    keep_ref[:, 4 * D : 5 * D] = normed
    keep_ref[:, 5 * D :] = labels.astype(BF16)
    attended, _ = attention(proj, label_bias(labels))
    keep_ref[:, 3 * D : 4 * D] = attended
    copies[5].wait()
    scatter_rows(values + dot_nn(attended, wout[...]), scratch, refs, 0)


def second_main(
    x0, x1, x2, x3, gain, wqkv, wout,
    b0, b1, b2, b3, normed_ref, att_ref, right_ref, scratch, lab_scratch,
):
    parts = (x0, x1, x2, x3)
    back = (b0, b1, b2, b3)
    values = gather_rows(parts, scratch, 0)
    g = gather_rows(parts, scratch, D)
    labels = gather_rows(parts, lab_scratch, 2 * D)
    g16 = g.astype(BF16)
    normed, xhat, rstd = norm_parts(values, gain[...])
    normed_ref[...] = normed
    proj = dot_nn(normed, wqkv[...]).astype(BF16)
    datt = dot_nt(g16, wout[...]).astype(BF16)
    attended, dproj = attention(proj, label_bias(labels), grad=datt)
    att_ref[...] = attended
    store_right(dproj, g16, right_ref)
    scatter_rows(values + dot_nn(attended, wout[...]), scratch, back, 0)
    dnormed = dot_nt(dproj, wqkv[...])
    scatter_rows(norm_back(dnormed, gain[...], xhat, rstd, g), scratch, back, D)


def second_pack(me, normed, attended, right, keep, p0, p1, p2, p3, left_ref, left_n, left_a):
    order = regroup(row_order(chip_second))
    left_n[...] = dot_nn(normed[...], order).astype(BF16)
    left_a[...] = dot_nn(attended[...], order).astype(BF16)
    pack(members_second(*here(me))[0], (left_n, left_a), right, (p0, p1, p2, p3))
    order = regroup(row_order(chip_first))
    left_ref[0] = dot_nn(keep[:, 4 * D : 5 * D], order).astype(BF16)
    left_ref[1] = dot_nn(keep[:, 3 * D : 4 * D], order).astype(BF16)


def first_backward(
    me, b0, b1, b2, b3, wout, keep, left, right_ref, p0, p1, p2, p3, scratch
):
    g16 = gather_rows((b0, b1, b2, b3), scratch, D).astype(BF16)
    datt = dot_nt(g16, wout[...]).astype(BF16)
    bias = label_bias(keep[:, 5 * D :].astype(F32))
    _, dproj = attention(keep[...], bias, grad=datt, attended=keep[:, 3 * D : 4 * D])
    store_right(dproj, g16, right_ref)
    pack(members_first(*here(me))[0], (left.at[0], left.at[1]), right_ref, (p0, p1, p2, p3))


def first_rest(b0, b1, b2, b3, tok, gain, wqkv, right, tg_ref, result_ref, scratch):
    back = (b0, b1, b2, b3)
    put_field(gather_rows(back, scratch, 0), scratch, result_ref)
    _, xhat, rstd = norm_parts(take_field(tok, scratch), gain[...])
    g = gather_rows(back, scratch, D)
    dnormed = dot_nt(right[0], wqkv[:, :D])
    dnormed += dot_nt(right[1], wqkv[:, D : 2 * D])
    dnormed += dot_nt(right[2], wqkv[:, 2 * D :])
    put_field(norm_back(dnormed, gain[...], xhat, rstd, g), scratch, tg_ref)


def weights(member, p0, p1, p2, p3, q0, q1, q2, q3, scratch):
    total = jnp.zeros((D, WIDE), F32)
    for part in (p0, p1, p2, p3):
        total += dot_tn(part[:, :D], part[:, D:])
    scratch[...] = total
    for step, ref in enumerate((q0, q1, q2, q3)):
        first = pl.multiple_of((member ^ step) * PLANE_ROWS, PLANE_ROWS)
        ref[...] = scratch[pl.ds(first, PLANE_ROWS), :].astype(BF16)


def first_weights(me, *refs):
    weights(members_first(*here(me))[1], *refs)


def second_weights(me, *refs):
    weights(members_second(*here(me))[1], *refs)


PIECE = OWN * WIDE // LANES
SHEET = [(x, z) for x in range(X) for z in range(Z)]


def add_rows(a0, a1, a2, a3, b0, b1, b2, b3, out_ref, scratch):
    blocks = ((members_first, (a0, a1, a2, a3)), (members_second, (b0, b1, b2, b3)))
    for slot, (members, parts) in enumerate(blocks):
        total = sum(part[...].astype(F32) for part in parts)
        for peer, (x, z) in enumerate(SHEET):
            m1, _, m3 = members(x, 0, z)
            row = (m3 * GROUP + m1) * OWN
            for c in range(WIDE // LANES):
                first = slot * PIECE + c * OWN
                scratch[peer, first : first + OWN, :] = total[
                    row : row + OWN, c * LANES : (c + 1) * LANES
                ]
    out_ref[...] = scratch[...].astype(BF16)


def own_rows(parts, rows_ref, tile_ref):
    norm = jnp.zeros((1, 1), F32)
    for slot, members in enumerate((members_first, members_second)):
        totals = [jnp.zeros((PIECE, LANES), F32)] * GROUP
        for source, (x, z) in enumerate(SHEET):
            m1 = members(x, 0, z)[0]
            piece = parts[source, slot * PIECE : (slot + 1) * PIECE, :]
            totals[m1] = totals[m1] + piece.astype(F32)
        for m1, total in enumerate(totals):
            rows_ref[m1, slot * PIECE : (slot + 1) * PIECE, :] = total
        norm += jnp.sum(sum(total * total for total in totals), keepdims=True)
    tile_ref[...] = jnp.broadcast_to(norm[None], tile_ref.shape)


def clipped(tiles, rows, qkv_a, out_a, qkv_b, out_b):
    total = jnp.sum(tiles[...], 0)[:1, :1]
    factor = jnp.minimum(1.0, math.sqrt(8.0) * D / jnp.sqrt(total))
    for slot, refs in enumerate(((qkv_a, out_a), (qkv_b, out_b))):
        for k in range(GROUP):
            ref, column = (refs[0], k * WIDE) if k < GROUP - 1 else (refs[1], 0)
            for c in range(WIDE // LANES):
                first = slot * PIECE + c * OWN
                ref[:, column + c * LANES : column + (c + 1) * LANES] = (
                    rows[k, first : first + OWN, :] * factor
                )


def shape_of(*dims, dtype=BF16):
    return jax.ShapeDtypeStruct(dims, dtype)


def call(kernel, outs, scratch, *args, scalar=False, far=0):
    whole = pl.BlockSpec(memory_space=pltpu.VMEM)
    specs = [whole] * (len(args) - far) + [pl.BlockSpec(memory_space=pl.ANY)] * far
    if scalar:
        specs[0] = pl.BlockSpec(memory_space=pltpu.SMEM)
    scratch = [pltpu.VMEM(s, F32) if isinstance(s, tuple) else s for s in scratch]
    return pl.pallas_call(
        kernel,
        out_shape=outs,
        in_specs=specs,
        out_specs=[whole] * len(outs),
        scratch_shapes=scratch,
        compiler_params=pltpu.CompilerParams(vmem_limit_bytes=VMEM_BYTES),
        name=kernel.__name__,
    )(*args)


def in_vmem(*arrays):
    return [pltpu.with_memory_space_constraint(array, pltpu.VMEM) for array in arrays]


def in_hbm(*arrays):
    return [pltpu.with_memory_space_constraint(array, pltpu.HBM) for array in arrays]


def moves(lat_count, lon_count):
    tables = []
    for a in range(2):
        for b in range(2):
            table = []
            for i in range(lat_count):
                for j in range(lon_count):
                    ti = (i - (1 - a)) % lat_count
                    tj = (j - (1 - b)) % lon_count
                    table.append((i * lon_count + j, ti * lon_count + tj))
            tables.append(table)
    return tables


def send(parts, tables, back=False):
    out = list(parts)
    for slot in (2, 0, 1):
        pairs = [(t, s) for s, t in tables[slot]] if back else tables[slot]
        out[slot] = lax.ppermute(parts[slot], ("lat", "lon"), pairs)
    return out


def index_of(x, y, z):
    return (x * YLO + y % YLO) * LON + y // YLO * Z + z


CHIPS = [(x, y, z) for x in range(X) for y in range(Y) for z in range(Z)]


SHEETS = [[index_of(x, y, z) for x, z in SHEET] for y in range(Y)]


def swap(parts, members, chip, level, steps):
    out = list(parts)
    for step in steps:
        pairs = []
        for here_chip in CHIPS:
            numbers = list(members(*here_chip))
            numbers[level] ^= step
            pairs.append((index_of(*here_chip), index_of(*chip(*numbers))))
        out[step] = lax.ppermute(parts[step], ("lat", "lon"), pairs)
    return out


def swap_first(parts, level, steps):
    return swap(parts, members_first, chip_first, level, steps)


def swap_second(parts, level, steps):
    return swap(parts, members_second, chip_second, level, steps)


def exchange(parts, groups):
    return lax.all_to_all(parts, ("lat", "lon"), 0, 0, axis_index_groups=groups)


def after(value, earlier):
    return lax.optimization_barrier((value, earlier))[0]


def on_device(
    tokens,
    cotangent,
    region,
    unshifted_norm_gain,
    unshifted_query_key_value,
    out_first,
    shifted_norm_gain,
    shifted_query_key_value,
    out_second,
):
    tables = moves(LAT, LON)
    lat, lon = lax.axis_index("lat"), lax.axis_index("lon")
    me = (lat * LON + lon).astype(jnp.int32).reshape(1)
    gain_a = unshifted_norm_gain.reshape(1, D)
    gain_b = shifted_norm_gain.reshape(1, D)
    tok = tokens.transpose(1, 2, 0, 3)
    cot = cotangent.transpose(1, 2, 0, 3)
    lab = region.transpose(1, 0, 2)

    field = shape_of(TOK, D)
    fields = shape_of(GROUP, TOK, D)
    packs = [shape_of(TOK, D + WIDE)] * GROUP
    *x, keep = call(
        first_forward,
        [shape_of(QUART, SEND)] * 4 + [shape_of(TOK, 5 * D + LANES)],
        [
            (TOK, D),
            (TOK, LANES),
            pltpu.VMEM(tok.shape, BF16),
            (1, D),
            pltpu.VMEM(lab.shape, jnp.int32),
            pltpu.VMEM(cot.shape, BF16),
            pltpu.VMEM((D, 3 * D), BF16),
            pltpu.VMEM((D, D), BF16),
            pltpu.SemaphoreType.DMA((6,)),
        ],
        me, *in_hbm(tok, gain_a, lab, cot, unshifted_query_key_value, out_first),
        scalar=True, far=6,
    )
    x = send(x, tables)
    *back, normed_b, att_b, right_b = call(
        second_main,
        [shape_of(QUART, 2 * D)] * 4 + [field, field, fields],
        [(TOK, D), (TOK, LANES)],
        *x, gain_b, shifted_query_key_value, out_second,
    )
    back = send(back, tables, back=True)
    half = pltpu.VMEM((TOK, D), BF16)
    *pack_b, left_a = call(
        second_pack,
        packs + [shape_of(2, TOK, D)],
        [half, half],
        me, normed_b, att_b, right_b, keep,
        scalar=True,
    )
    pack_b = swap_second(after(pack_b, back[:3]), 0, (3, 1, 2))
    right_a, *pack_a = call(
        first_backward,
        [fields] + packs,
        [(TOK, D)],
        me, *back, out_first, keep, left_a,
        scalar=True,
    )
    pack_a = swap_first(pack_a, 0, (3, 1, 2))
    grid = shape_of(WLAT, WLON, WLEV, D)
    token_gradient, result = call(
        first_rest,
        [grid, grid],
        [(TOK, D)],
        *back, tok, gain_a, unshifted_query_key_value, right_a,
    )
    token_gradient = token_gradient.transpose(2, 0, 1, 3)
    result = result.transpose(2, 0, 1, 3)

    rows = [shape_of(PLANE_ROWS, WIDE)] * GROUP
    sum_b = call(second_weights, rows, [(D, WIDE)], me, *in_vmem(*pack_b), scalar=True)
    sum_b = swap_second(sum_b, 1, (2, 1, 3))
    sum_a = call(first_weights, rows, [(D, WIDE)], me, *in_vmem(*pack_a), scalar=True)
    sum_a = swap_first(sum_a, 1, (1, 2, 3))
    piece = (len(SHEET), 2 * PIECE, LANES)
    (sums,) = call(add_rows, [shape_of(*piece)], [piece], *sum_a, *sum_b)
    sums = exchange(sums, SHEETS)
    mine, tiles = call(
        own_rows,
        [shape_of(GROUP, 2 * PIECE, LANES, dtype=F32), shape_of(LAT * LON, 1, LANES, dtype=F32)],
        [],
        sums,
    )
    tiles = lax.all_to_all(tiles, ("lat", "lon"), 0, 0)
    out_qkv, out_out = shape_of(OWN, 3 * D, dtype=F32), shape_of(OWN, D, dtype=F32)
    clips = call(clipped, [out_qkv, out_out] * 2, [], tiles, mine)
    return (result, token_gradient, *clips)


def solution(mesh):
    field = P("rep", "lat", "lon", None)
    rows = P(("rep", "lat", "lon"), None)
    in_specs = (field, field, P("rep", "lat", "lon"), P(), P(), P(), P(), P(), P())
    return jax.shard_map(
        on_device,
        mesh=mesh,
        in_specs=in_specs,
        out_specs=(field, field, rows, rows, rows, rows),
        check_vma=False,
    )
```
